512 devices in a mesh: visit: 16 (over y, core), patch: 32 (over x, z).
Axes of the slice: x: 4, y: 8, z: 8, core: 2. Of those that a mesh axis runs over, the one named last changes fastest.
Arguments:
- blocks: bfloat16 [16, 512, 128, 128], P('visit', 'patch'), may hold values from -6 to 6
- inv_variance: bfloat16 [16, 512, 128, 128], P('visit', 'patch'), may hold values from 0.0099487305 to 1
- destinations: int32 [16, 512, 2], P('visit', 'patch'), may hold values from 0 to 31, all different within a row; in each aligned block of 16 rows (0 to 15, 16 to 31, ..., all dimensions but the last counted through in order) at most 2 rows name the same one
- offsets: int32 [16, 512, 2, 2], P('visit', 'patch'), may hold values from 0 to 384
- coefficients: float32 [16, 512, 15], P('visit', 'patch'), may hold values from -3 to 3
- basis_rows: bfloat16 [5, 41], replicated, may hold values from -2 to 2
- basis_cols: bfloat16 [5, 41], replicated, may hold values from -2 to 2
Outputs:
- coadd: float32 [32, 512, 512], P('patch', 'visit')
The draws below stay inside these ranges and needn't reach their ends.
Inputs may be any that keep to these rules, and one draw needn't show every extreme that they name: `destinations`: the two patches of a block differ. Among the 16 blocks of one device no patch is named more than 2 times, a bound that some block reaches.
All inputs are finite; a program needn't handle non-finite values.
Results may differ from the reference program's by a relative error of at most 0.014.
Values may be sent and summed in bfloat16 or wider, within the bound.
No kernel may reach another device: no remote copies, remote signals or barrier semaphores. Data moves between devices by JAX's collectives and lax.ppermute only.
A program may use at most 64 MiB of HBM per device.

```python
import math
import jax
import jax.numpy as jnp
import numpy as np
from jax import lax

S = 128
P_SIZE = 512
NB = 16
TAPS = 41
BASIS = 5
CAP = 2
VISITS = 16
SRC_BLOCKS = 512
N_PATCH = 32


def plant(drawn, rng, low, largest):
    spot = [jax.random.randint(jax.random.fold_in(rng, axis), (), 0, length) for axis, length in enumerate(drawn.shape)]
    longest = drawn.shape.index(max(drawn.shape))
    next_to = spot[:longest] + [(spot[longest] + 1) % drawn.shape[longest]] + spot[longest + 1:]
    return drawn.at[tuple(spot)].set(low).at[tuple(next_to)].set(largest)


def level_of(own_key, shape, split, least, largest):
    loudness, own = 1.0, jax.random.fold_in(own_key, 6)
    for dim, shards_of in split:
        steps = jnp.exp(jax.random.uniform(jax.random.fold_in(own, dim), (shards_of,), jnp.float32, least / len(split), largest / len(split)))
        loudness = loudness * jnp.repeat(steps, shape[dim] // shards_of).reshape([-1 if axis == dim else 1 for axis in range(len(shape))])
    return loudness


def routed_block(own_key, own, number, rows, count, top, bound, slope):
    order = jax.random.permutation(own_key, count)
    crowded, usual = shares(count, rows * top, bound, slope, True), shares(count, rows * top, bound, slope, False)
    places = jnp.arange(count)

    def named(lengths, rotation):
        used = int((lengths > 0).sum())
        fixed = max(1, used // 4)
        shifted = fixed + (places - fixed + rotation * (used - fixed)) % max(1, count - fixed)
        return jnp.zeros((count,), jnp.int32).at[order[jnp.where(places < fixed, places, shifted)]].set(jnp.asarray(lengths, jnp.int32))

    lengths = jnp.where(number % 4 == 0, named(crowded, number // 4), named(usual, number - number // 4 - 1))
    mixed = jax.random.permutation(jax.random.fold_in(own, 3), count)
    source_of, taker = mixed[0:count // 2 * 2:2], mixed[1:count // 2 * 2:2]
    margin = jnp.minimum(lengths[source_of] - 1, bound - lengths[taker]) // 2
    margin = jnp.where((source_of == order[0]) | (taker == order[0]) | (lengths[taker] == 0), 0, jnp.maximum(margin, 0))
    shifted = jax.random.randint(jax.random.fold_in(own, 4), (count // 2,), 0, 1 << 20) % (margin + 1)
    lengths = lengths.at[source_of].add(-shifted).at[taker].add(shifted)
    items = jnp.searchsorted(jnp.cumsum(lengths), jnp.arange(rows * top), side="right").astype(jnp.int32)
    listing = items.reshape(top, rows).T
    listing = listing[jax.random.permutation(jax.random.fold_in(own, 1), rows)]
    rotation = jax.random.randint(jax.random.fold_in(own, 2), (rows, 1), 0, top)
    return jnp.take_along_axis(listing, (jnp.arange(top)[None, :] + rotation) % top, axis=1)


def shares(amount, total, bound, slope, full):
    loads = [(1 << 20) // math.isqrt(rank ** slope) + 1 for rank in range(1, amount + 1)]
    largest = bound if full else min(bound, max(-(-total // amount), total * loads[0] // sum(loads)))
    least = 1 if total - largest >= amount - 1 else 0
    holding, surplus = [largest] + [least] * (amount - 1), total - largest - least * (amount - 1)
    while surplus > 0:
        movable = [i for i in range(1, amount) if holding[i] < largest] or [i for i in range(1, amount) if holding[i] < bound]
        pool, left = sum([loads[i] for i in movable]), surplus
        for i in movable:
            more = min(bound - holding[i], max(1, left * loads[i] // pool), surplus)
            holding[i] = holding[i] + more
            surplus = surplus - more
    return np.array(holding)


def centred(key, dims, scale, bound, cuts=(), kind=jnp.bfloat16):
    entries = jax.random.normal(key, dims, jnp.float32) * scale
    if len(cuts) > 0:
        entries = level_of(key, dims, cuts, -0.22, 0.18) * entries
    return jnp.clip(entries, min=-bound, max=bound).astype(kind)


def setup_inputs(seed: int = 0) -> dict:
    arg_keys = jax.random.split(jax.random.key(seed), 8)
    blocks = centred(arg_keys[0], (VISITS, SRC_BLOCKS, S, S), 1.0, 6.0, ((0, 16), (1, 32)))
    inv_variance = jnp.clip(jnp.exp(math.log(1.0) - 4.61031033 * jax.random.uniform(arg_keys[1], (VISITS, SRC_BLOCKS, S, S), jnp.float32) ** level_of(arg_keys[1], (VISITS, SRC_BLOCKS, S, S), ((0, 16), (1, 32)), -0.2, 0.2)), 0.0099487305, 1.0).astype(jnp.bfloat16)
    destinations_keys = jax.random.split(jax.random.fold_in(arg_keys[2], 1), VISITS * SRC_BLOCKS // NB)
    destinations_turns = jax.random.permutation(jax.random.fold_in(arg_keys[2], 3), VISITS * SRC_BLOCKS // NB)
    destinations = jax.vmap(lambda own, number: routed_block(jax.random.fold_in(arg_keys[2], 2), own, number, NB, N_PATCH, 2, CAP, 2))(destinations_keys, destinations_turns).reshape((VISITS, SRC_BLOCKS, 2))
    offsets = plant(jax.random.randint(arg_keys[3], (VISITS, SRC_BLOCKS, 2, 2), 0, P_SIZE - S + 1), jax.random.fold_in(arg_keys[3], 1), 0, P_SIZE - S).astype(jnp.int32)
    coefficients = centred(arg_keys[4], (VISITS, SRC_BLOCKS, 3 * BASIS), 0.5, 3.0, ((0, 16), (1, 32)), jnp.float32)
    basis_rows = centred(arg_keys[5], (BASIS, TAPS), 0.15, 2.0)
    basis_cols = centred(arg_keys[6], (BASIS, TAPS), 0.15, 2.0)
    return dict(blocks=blocks, inv_variance=inv_variance, destinations=destinations, offsets=offsets, coefficients=coefficients, basis_rows=basis_rows, basis_cols=basis_cols)


def band_tables(kernel_taps, block_side):
    half_width = (kernel_taps.shape[1] - 1) // 2
    pixels = jnp.arange(block_side, dtype=jnp.int32)
    lag_index = pixels[:, None] - pixels[None, :] + half_width
    which = jnp.arange(kernel_taps.shape[1], dtype=jnp.int32)
    onehot = (lag_index[None, :, :] == which[:, None, None]).astype(jnp.float32)
    return jnp.einsum('kt,tab->kab', kernel_taps.astype(jnp.float32), onehot, precision=lax.Precision.HIGHEST)


def match_blocks(group_blocks, group_coef, row_table, col_table):
    block_count, block_side = group_blocks.shape[0], group_blocks.shape[1]
    basis_count = row_table.shape[0]
    across = jnp.einsum('mab,kbc->mkac', group_blocks.astype(jnp.float32), row_table, precision=lax.Precision.HIGHEST)
    basis_images = jnp.einsum('kab,mkbc->mkac', col_table, across, precision=lax.Precision.HIGHEST)
    coords = (jnp.arange(block_side, dtype=jnp.float32) - (block_side - 1) / 2.0) / block_side
    weights_three = group_coef.reshape(block_count, basis_count, 3)
    spatial = (weights_three[:, :, 0, None, None] + weights_three[:, :, 1, None, None] * coords[:, None]
               + weights_three[:, :, 2, None, None] * coords[None, :])
    return jnp.sum(spatial * basis_images, axis=1).astype(jnp.bfloat16)


def reference(blocks, inv_variance, destinations, offsets, coefficients, basis_rows, basis_cols):
    block_side = blocks.shape[-1]
    row_table = band_tables(basis_rows, block_side)
    col_table = jnp.transpose(band_tables(basis_cols, block_side), (0, 2, 1))
    pixels = jnp.arange(block_side, dtype=jnp.int32)

    def one_visit(totals, visit_data):
        own_blocks, own_ivar, own_dest, own_off, own_coef = visit_data
        grouped = (own_blocks.reshape(-1, NB, block_side, block_side), own_coef.reshape(-1, NB, own_coef.shape[-1]))
        matched = lax.map(lambda pair: match_blocks(pair[0], pair[1], row_table, col_table), grouped)
        matched = matched.reshape(-1, block_side, block_side)
        weight = own_ivar.astype(jnp.float32)
        num_term = matched.astype(jnp.float32) * weight
        numerator, denominator = totals
        for which_dest in range(2):
            row_index = own_off[:, which_dest, 0][:, None, None] + pixels[None, :, None]
            col_index = own_off[:, which_dest, 1][:, None, None] + pixels[None, None, :]
            flat_index = (own_dest[:, which_dest][:, None, None] * P_SIZE + row_index) * P_SIZE + col_index
            numerator = numerator.at[flat_index].add(num_term)
            denominator = denominator.at[flat_index].add(weight)
        return (numerator, denominator), None

    start_sums = (jnp.zeros((N_PATCH * P_SIZE * P_SIZE,), jnp.float32), jnp.zeros((N_PATCH * P_SIZE * P_SIZE,), jnp.float32))
    (numerator, denominator), unused = lax.scan(one_visit, start_sums, (blocks, inv_variance, destinations, offsets, coefficients))
    numerator = numerator.reshape(N_PATCH, P_SIZE, P_SIZE)
    denominator = denominator.reshape(N_PATCH, P_SIZE, P_SIZE)
    return numerator / jnp.maximum(denominator, 1.0)
```

```python
import functools

import jax
import jax.numpy as jnp
from jax import lax
from jax.experimental import pallas as pl
from jax.experimental.pallas import tpu as pltpu
from jax.sharding import Mesh
from jax.sharding import PartitionSpec as P

S = 128
P_SIZE = 512
TAPS = 41
HALF = (TAPS - 1) // 2
BASIS = 5
BAND = 32
LANES = 128
META = 16
LEAD = 4
STAGE = 7 * BAND


def match_kernel(coef_ref, taps_ref, blocks_ref, out_ref, rows_tab, cols_tab, stack):
    row_id = lax.broadcasted_iota(jnp.int32, (S, S), 0)
    col_id = lax.broadcasted_iota(jnp.int32, (S, S), 1)
    inside = jnp.abs(row_id - col_id) <= HALF
    for k in range(BASIS):
        for which, table in ((0, rows_tab), (1, cols_tab)):
            taps = jnp.broadcast_to(taps_ref[which * 8 + k : which * 8 + k + 1, :], (8, S))
            band = jnp.concatenate(
                [pltpu.roll(taps, (S - HALF - LEAD + row) % S, 1, stride=1, stride_axis=0) for row in range(0, S, 8)]
            )
            table[:, k * S : (k + 1) * S] = jnp.where(inside, band, 0.0).astype(jnp.bfloat16)
    y = (lax.broadcasted_iota(jnp.int32, (S, 1), 0).astype(jnp.float32) - (S - 1) / 2.0) / S
    x = (lax.broadcasted_iota(jnp.int32, (1, S), 1).astype(jnp.float32) - (S - 1) / 2.0) / S

    def one(i, carry):
        across = jnp.dot(blocks_ref[i], rows_tab[...], preferred_element_type=jnp.float32)
        for k in range(BASIS):
            part = across[:, k * S : (k + 1) * S]
            plain = coef_ref[i, 3 * k] + coef_ref[i, 3 * k + 2] * x
            for at, value in ((0, part * plain), (S, part * coef_ref[i, 3 * k + 1])):
                upper = value.astype(jnp.bfloat16)
                lower = (value - upper.astype(jnp.float32)).astype(jnp.bfloat16)
                stack[k * S : (k + 1) * S, at : at + S] = upper
                stack[k * S : (k + 1) * S, 2 * S + at : 3 * S + at] = lower
        sums = jnp.dot(cols_tab[...], stack[...], preferred_element_type=jnp.float32)
        sums = sums[:, 0 : 2 * S] + sums[:, 2 * S : 4 * S]
        out_ref[i] = (sums[:, 0:S] + y * sums[:, S : 2 * S]).astype(jnp.bfloat16)
        return carry

    lax.fori_loop(0, blocks_ref.shape[0], one, 0)


def match(blocks, coefficients, basis_rows, basis_cols):
    rows = jnp.pad(basis_rows[:, ::-1].astype(jnp.float32), ((0, 8 - BASIS), (LEAD, S - TAPS - LEAD)))
    cols = jnp.pad(basis_cols.astype(jnp.float32), ((0, 8 - BASIS), (LEAD, S - TAPS - LEAD)))
    vmem = pl.BlockSpec(memory_space=pltpu.VMEM)
    return pl.pallas_call(
        match_kernel,
        out_shape=jax.ShapeDtypeStruct(blocks.shape, jnp.bfloat16),
        in_specs=[pl.BlockSpec(memory_space=pltpu.SMEM), vmem, vmem],
        out_specs=vmem,
        scratch_shapes=[
            pltpu.VMEM((S, BASIS * S), jnp.bfloat16),
            pltpu.VMEM((S, BASIS * S), jnp.bfloat16),
            pltpu.VMEM((BASIS * S, 4 * S), jnp.bfloat16),
        ],
        compiler_params=pltpu.CompilerParams(vmem_limit_bytes=32 * 2**20),
        cost_estimate=pl.CostEstimate(flops=2**30, bytes_accessed=2**20, transcendentals=0),
        name="match",
    )(coefficients, jnp.concatenate([rows, cols]), blocks)


def place_kernel(with_matched, meta_ref, where_ref, weight_ref, *refs):
    if with_matched:
        matched_ref, out_ref, canvas, stage = refs
    else:
        out_ref, canvas, stage = refs
    mine, core = where_ref[0], where_ref[1]
    sources = weight_ref.shape[0]
    count = weight_ref.shape[1] // S
    canvas[...] = jnp.zeros_like(canvas)
    stage[...] = jnp.zeros_like(stage)
    lane = lax.broadcasted_iota(jnp.int32, (S, LANES), 1)

    def one(index, carry):
        source, block = index // count, lax.rem(index, count)
        for n in range(2):
            base = index * 10 + 5 * n
            patch = meta_ref[base]

            @pl.when(patch // 8 == mine)
            def add():
                row = meta_ref[base + 1] * LANES + meta_ref[base + 2]
                tile, shift = meta_ref[base + 3], meta_ref[base + 4]
                value = weight_ref[source, pl.ds(pl.multiple_of(block * S, S), S), :].astype(jnp.float32)
                if with_matched:
                    value = value * matched_ref[source, block].astype(jnp.float32)
                value = pltpu.roll(value, shift, 1)
                stage[0, BAND : BAND + S, :] = jnp.where(lane >= shift, value, 0.0)
                stage[1, BAND : BAND + S, :] = jnp.where(lane >= shift, 0.0, value)
                first, within = row // BAND, lax.rem(row, BAND)
                odd = lax.rem(first + core, 2)

                def band(step):
                    start = BAND + BAND * step - within
                    spot = lax.rem(patch, 8) * (P_SIZE // 2) + (first + step) // 2 * BAND
                    spot = pl.multiple_of(spot, BAND)
                    for side in range(2):
                        canvas[tile + side, pl.ds(spot, BAND), :] += stage[side, pl.ds(start, BAND), :]

                band(odd)
                band(odd + 2)

                @pl.when((odd == 0) & (within > 0))
                def last():
                    band(4)

        return carry

    lax.fori_loop(0, sources * count, one, 0)
    for tile in range(P_SIZE // LANES):
        out_ref[:, tile * LANES : (tile + 1) * LANES] = canvas[tile].astype(jnp.bfloat16)


def place(meta, where, weight, matched=None):
    patches, rows = 8, P_SIZE // 2
    vmem = pl.BlockSpec(memory_space=pltpu.VMEM)
    smem = pl.BlockSpec(memory_space=pltpu.SMEM)
    operands = (meta, where, weight) if matched is None else (meta, where, weight, matched)
    out = pl.pallas_call(
        functools.partial(place_kernel, matched is not None),
        out_shape=jax.ShapeDtypeStruct((patches * rows, P_SIZE), jnp.bfloat16),
        in_specs=[smem, smem] + [vmem] * (len(operands) - 2),
        out_specs=vmem,
        scratch_shapes=[
            pltpu.VMEM((P_SIZE // LANES + 1, patches * rows, LANES), jnp.float32),
            pltpu.VMEM((2, STAGE, LANES), jnp.float32),
        ],
        compiler_params=pltpu.CompilerParams(vmem_limit_bytes=40 * 2**20),
        cost_estimate=pl.CostEstimate(flops=2**24, bytes_accessed=2**23, transcendentals=0),
        name="place_num" if matched is not None else "place_den",
    )(*operands)
    return out.reshape(patches, rows, P_SIZE)


def body(blocks, inv_variance, destinations, offsets, coefficients, basis_rows, basis_cols):
    count = blocks.shape[1]
    place_of = jnp.concatenate(
        [destinations[0][:, :, None], jnp.stack([offsets[0] // LANES, offsets[0] % LANES], -1).reshape(count, 2, 4)], -1
    )
    lines = jnp.pad(place_of.reshape(count, 10).astype(jnp.bfloat16), ((0, META - count), (0, S - 10)))
    weight = jnp.concatenate([inv_variance[0].reshape(count * S, S), lines])
    weight = lax.all_gather(weight, ("core", "x"))
    matched = match(blocks[0], coefficients[0], basis_rows, basis_cols)
    matched = lax.all_gather(matched, ("core", "x"))

    meta = weight[:, count * S : count * S + count, :10].astype(jnp.int32).reshape(-1)
    where = jnp.stack([lax.axis_index("x"), lax.axis_index("core")]).astype(jnp.int32)
    den = place(meta, where, weight)
    den = lax.psum_scatter(den, "z", scatter_dimension=0, tiled=True)
    num = place(meta, where, weight, matched)
    num = lax.psum_scatter(num, "z", scatter_dimension=0, tiled=True)

    both = jnp.stack([num.reshape(8, BAND, P_SIZE), den.reshape(8, BAND, P_SIZE)], 1)
    both = lax.all_to_all(both, "y", 0, 0, tiled=True)
    both = jnp.sum(both.astype(jnp.float32), axis=0)
    return (both[0] / jnp.maximum(both[1], 1.0))[None]


def solution(mesh):
    visits = mesh.shape["visit"]
    grid = Mesh(mesh.devices.reshape(visits // 2, 2, 4, mesh.shape["patch"] // 4), ("y", "core", "x", "z"))
    visit, patch = ("y", "core"), ("x", "z")
    return jax.shard_map(
        body,
        mesh=grid,
        in_specs=(
            P(visit, patch, None, None),
            P(visit, patch, None, None),
            P(visit, patch, None),
            P(visit, patch, None, None),
            P(visit, patch, None),
            P(),
            P(),
        ),
        out_specs=P(patch, visit, None),
        check_vma=False,
    )
```

```python
import functools

import jax
import jax.numpy as jnp
from jax import lax
from jax.experimental import pallas as pl
from jax.experimental.pallas import tpu as pltpu
from jax.sharding import Mesh
from jax.sharding import PartitionSpec as P

S = 128
P_SIZE = 512
TAPS = 41
HALF = (TAPS - 1) // 2
BASIS = 5
BAND = 32
LANES = 128
META = 16
LEAD = 4
STAGE = 7 * BAND


def match_kernel(coef_ref, taps_ref, blocks_ref, weight_ref, out_ref, rows_tab, cols_tab, stack):
    row_id = lax.broadcasted_iota(jnp.int32, (S, S), 0)
    col_id = lax.broadcasted_iota(jnp.int32, (S, S), 1)
    inside = jnp.abs(row_id - col_id) <= HALF
    for k in range(BASIS):
        for which, table in ((0, rows_tab), (1, cols_tab)):
            taps = jnp.broadcast_to(taps_ref[which * 8 + k : which * 8 + k + 1, :], (8, S))
            band = jnp.concatenate(
                [pltpu.roll(taps, (S - HALF - LEAD + row) % S, 1, stride=1, stride_axis=0) for row in range(0, S, 8)]
            )
            table[:, k * S : (k + 1) * S] = jnp.where(inside, band, 0.0).astype(jnp.bfloat16)
    y = (lax.broadcasted_iota(jnp.int32, (S, 1), 0).astype(jnp.float32) - (S - 1) / 2.0) / S
    x = (lax.broadcasted_iota(jnp.int32, (1, S), 1).astype(jnp.float32) - (S - 1) / 2.0) / S

    def one(i, carry):
        across = jnp.dot(blocks_ref[i], rows_tab[...], preferred_element_type=jnp.float32)
        for k in range(BASIS):
            part = across[:, k * S : (k + 1) * S]
            plain = coef_ref[i, 3 * k] + coef_ref[i, 3 * k + 2] * x
            for at, value in ((0, part * plain), (S, part * coef_ref[i, 3 * k + 1])):
                upper = value.astype(jnp.bfloat16)
                lower = (value - upper.astype(jnp.float32)).astype(jnp.bfloat16)
                stack[k * S : (k + 1) * S, at : at + S] = upper
                stack[k * S : (k + 1) * S, 2 * S + at : 3 * S + at] = lower
        sums = jnp.dot(cols_tab[...], stack[...], preferred_element_type=jnp.float32)
        sums = sums[:, 0 : 2 * S] + sums[:, 2 * S : 4 * S]
        matched = sums[:, 0:S] + y * sums[:, S : 2 * S]
        term = matched * weight_ref[i].astype(jnp.float32)
        out_ref[pl.ds(pl.multiple_of(i * S, S), S), :] = term.astype(jnp.bfloat16)
        return carry

    lax.fori_loop(0, blocks_ref.shape[0], one, 0)


def match(blocks, weight, coefficients, basis_rows, basis_cols):
    rows = jnp.pad(basis_rows[:, ::-1].astype(jnp.float32), ((0, 8 - BASIS), (LEAD, S - TAPS - LEAD)))
    cols = jnp.pad(basis_cols.astype(jnp.float32), ((0, 8 - BASIS), (LEAD, S - TAPS - LEAD)))
    vmem = pl.BlockSpec(memory_space=pltpu.VMEM)
    return pl.pallas_call(
        match_kernel,
        out_shape=jax.ShapeDtypeStruct((blocks.shape[0] * S, S), jnp.bfloat16),
        in_specs=[pl.BlockSpec(memory_space=pltpu.SMEM), vmem, vmem, vmem],
        out_specs=vmem,
        scratch_shapes=[
            pltpu.VMEM((S, BASIS * S), jnp.bfloat16),
            pltpu.VMEM((S, BASIS * S), jnp.bfloat16),
            pltpu.VMEM((BASIS * S, 4 * S), jnp.bfloat16),
        ],
        compiler_params=pltpu.CompilerParams(vmem_limit_bytes=32 * 2**20),
        cost_estimate=pl.CostEstimate(flops=2**30, bytes_accessed=2**20, transcendentals=0),
        name="match",
    )(coefficients, jnp.concatenate([rows, cols]), blocks, weight)


def pack_kernel(dest_ref, off_ref, weight_ref, out_ref, taken):
    out_ref[...] = jnp.zeros_like(out_ref)
    line = lax.broadcasted_iota(jnp.int32, (META, S), 0)
    lane = lax.broadcasted_iota(jnp.int32, (META, S), 1)

    def clear(patch, carry):
        taken[patch] = 0
        return carry

    lax.fori_loop(0, out_ref.shape[0], clear, 0)

    def one(block, carry):
        value = weight_ref[block]
        for n in range(2):
            patch = dest_ref[2 * block + n]
            slot = taken[patch]
            taken[patch] = slot + 1
            row, col = off_ref[4 * block + 2 * n], off_ref[4 * block + 2 * n + 1]
            out_ref[patch, pl.ds(pl.multiple_of(slot * S, S), S), :] = value
            told = jnp.zeros((META, S), jnp.int32)
            for at, number in enumerate((1, row // LANES, lax.rem(row, LANES), col // LANES, lax.rem(col, LANES))):
                told = jnp.where(lane == at, number, told)
            before = out_ref[patch, 2 * S : 2 * S + META, :].astype(jnp.float32)
            now = jnp.where(line == slot, told.astype(jnp.float32), before)
            out_ref[patch, 2 * S : 2 * S + META, :] = now.astype(jnp.bfloat16)
        return carry

    lax.fori_loop(0, weight_ref.shape[0], one, 0)


def pack(weight, destinations, offsets, owners):
    smem = pl.BlockSpec(memory_space=pltpu.SMEM)
    vmem = pl.BlockSpec(memory_space=pltpu.VMEM)
    return pl.pallas_call(
        pack_kernel,
        out_shape=jax.ShapeDtypeStruct((owners, 2 * S + META, S), jnp.bfloat16),
        in_specs=[smem, smem, vmem],
        out_specs=vmem,
        scratch_shapes=[pltpu.SMEM((owners,), jnp.int32)],
        compiler_params=pltpu.CompilerParams(vmem_limit_bytes=24 * 2**20),
        cost_estimate=pl.CostEstimate(flops=2**20, bytes_accessed=2**21, transcendentals=0),
        name="pack",
    )(destinations.reshape(-1), offsets.reshape(-1), weight)


def whole_kernel(meta_ref, slots_ref, out_ref, canvas):
    canvas[...] = jnp.zeros_like(canvas)
    lane = lax.broadcasted_iota(jnp.int32, (S, LANES), 1)

    def one(index, carry):
        base = 5 * index

        @pl.when(meta_ref[base] > 0)
        def add():
            row = meta_ref[base + 1] * LANES + meta_ref[base + 2]
            tile, shift = meta_ref[base + 3], meta_ref[base + 4]
            source, slot = index // 2, lax.rem(index, 2)
            value = slots_ref[source, pl.ds(pl.multiple_of(slot * S, S), S), :].astype(jnp.float32)
            value = pltpu.roll(value, shift, 1)
            canvas[tile, pl.ds(row, S), :] += jnp.where(lane >= shift, value, 0.0)
            canvas[tile + 1, pl.ds(row, S), :] += jnp.where(lane >= shift, 0.0, value)

        return carry

    lax.fori_loop(0, 2 * slots_ref.shape[0], one, 0)
    for tile in range(P_SIZE // LANES):
        out_ref[:, tile * LANES : (tile + 1) * LANES] = canvas[tile].astype(jnp.bfloat16)


def place_whole(meta, slots):
    return pl.pallas_call(
        whole_kernel,
        out_shape=jax.ShapeDtypeStruct((P_SIZE, P_SIZE), jnp.bfloat16),
        in_specs=[pl.BlockSpec(memory_space=pltpu.SMEM), pl.BlockSpec(memory_space=pltpu.VMEM)],
        out_specs=pl.BlockSpec(memory_space=pltpu.VMEM),
        scratch_shapes=[pltpu.VMEM((P_SIZE // LANES + 1, P_SIZE, LANES), jnp.float32)],
        compiler_params=pltpu.CompilerParams(vmem_limit_bytes=24 * 2**20),
        cost_estimate=pl.CostEstimate(flops=2**23, bytes_accessed=2**22, transcendentals=0),
        name="place_whole",
    )(meta, slots)


def bands_kernel(meta_ref, where_ref, *refs):
    parts, (out_ref, held, canvas, stage, sems) = refs[:8], refs[8:]
    copies = [pltpu.make_async_copy(part, held.at[i], sems.at[i]) for i, part in enumerate(parts)]
    for copy in copies:
        copy.start()
    mine, core = where_ref[0], where_ref[1]
    canvas[...] = jnp.zeros_like(canvas)
    stage[...] = jnp.zeros_like(stage)
    lane = lax.broadcasted_iota(jnp.int32, (S, LANES), 1)
    for copy in copies:
        copy.wait()
    count = held.shape[1] // S

    def one(index, carry):
        source, block = index // count, lax.rem(index, count)
        lag = source // 2
        from_x = lax.rem(mine + 4 - lag, 4)
        from_core = lax.rem(core + lax.rem(source, 2), 2)
        line = (from_core * 4 + from_x) * count + block
        for n in range(2):
            base = line * 6 + 3 * n
            patch = meta_ref[base]

            @pl.when(patch // 8 == mine)
            def add():
                row, col = meta_ref[base + 1], meta_ref[base + 2]
                tile, shift = col // LANES, lax.rem(col, LANES)
                value = held[source, pl.ds(pl.multiple_of(block * S, S), S), :].astype(jnp.float32)
                value = pltpu.roll(value, shift, 1)
                stage[0, BAND : BAND + S, :] = jnp.where(lane >= shift, value, 0.0)
                stage[1, BAND : BAND + S, :] = jnp.where(lane >= shift, 0.0, value)
                first, within = row // BAND, lax.rem(row, BAND)
                odd = lax.rem(first + core, 2)

                def band(step):
                    start = BAND + BAND * step - within
                    spot = (first + step) // 2 * (8 * BAND) + lax.rem(patch, 8) * BAND
                    spot = pl.multiple_of(spot, BAND)
                    for side in range(2):
                        canvas[tile + side, pl.ds(spot, BAND), :] += stage[side, pl.ds(start, BAND), :]

                band(odd)
                band(odd + 2)

                @pl.when((odd == 0) & (within > 0))
                def last():
                    band(4)

        return carry

    lax.fori_loop(0, 8 * count, one, 0)
    for tile in range(P_SIZE // LANES):
        out_ref[:, tile * LANES : (tile + 1) * LANES] = canvas[tile].astype(jnp.bfloat16)


def place_bands(meta, where, parts):
    rows = 8 * P_SIZE // 2
    smem = pl.BlockSpec(memory_space=pltpu.SMEM)
    return pl.pallas_call(
        bands_kernel,
        out_shape=jax.ShapeDtypeStruct((rows, P_SIZE), jnp.bfloat16),
        in_specs=[smem, smem] + [pl.BlockSpec(memory_space=pl.ANY)] * len(parts),
        out_specs=pl.BlockSpec(memory_space=pltpu.VMEM),
        scratch_shapes=[
            pltpu.VMEM((len(parts),) + parts[0].shape, jnp.bfloat16),
            pltpu.VMEM((P_SIZE // LANES + 1, rows, LANES), jnp.float32),
            pltpu.VMEM((2, STAGE, LANES), jnp.float32),
            pltpu.SemaphoreType.DMA((len(parts),)),
        ],
        compiler_params=pltpu.CompilerParams(vmem_limit_bytes=40 * 2**20),
        cost_estimate=pl.CostEstimate(flops=2**24, bytes_accessed=2**23, transcendentals=0),
        name="place_bands",
    )(meta, where, *parts)


def body(blocks, inv_variance, destinations, offsets, coefficients, basis_rows, basis_cols):
    count = blocks.shape[1]
    owners = lax.axis_size("x") * lax.axis_size("z")
    weight = inv_variance[0]
    where = jnp.stack([lax.axis_index("x"), lax.axis_index("core")]).astype(jnp.int32)
    lines = jnp.concatenate([destinations[0][:, :, None], offsets[0]], -1).reshape(count, 6)
    lines = lax.all_gather(lines, ("core", "x")).reshape(-1)

    slots = pack(weight, destinations[0], offsets[0], owners)
    slots = lax.all_to_all(slots, ("x", "z"), 0, 0, tiled=True)

    terms = match(blocks[0], weight, coefficients[0], basis_rows, basis_cols)
    parts = []
    for lag in range(4):
        part = lax.ppermute(terms, "x", [(i, (i + lag) % 4) for i in range(4)]) if lag else terms
        parts += [part, lax.ppermute(part, "core", [(0, 1), (1, 0)])]
    num = place_bands(lines, where, parts).reshape(8, 8, BAND, P_SIZE)
    num = lax.psum_scatter(num, "y", scatter_dimension=0, tiled=True)
    num = lax.all_to_all(num[0], "z", 0, 0, tiled=True)

    told = slots[:, 2 * S : 2 * S + 2, :5].astype(jnp.int32).reshape(-1)
    den = place_whole(told, slots).reshape(16, BAND, P_SIZE)
    den = lax.all_to_all(den, ("y", "core"), 0, 0, tiled=True)

    num = jnp.sum(num.astype(jnp.float32), axis=0)
    den = jnp.sum(den.astype(jnp.float32), axis=0)
    return (num / jnp.maximum(den, 1.0))[None]


def solution(mesh):
    visits = mesh.shape["visit"]
    grid = Mesh(mesh.devices.reshape(visits // 2, 2, 4, mesh.shape["patch"] // 4), ("y", "core", "x", "z"))
    visit, patch = ("y", "core"), ("x", "z")
    return jax.shard_map(
        body,
        mesh=grid,
        in_specs=(
            P(visit, patch, None, None),
            P(visit, patch, None, None),
            P(visit, patch, None),
            P(visit, patch, None, None),
            P(visit, patch, None),
            P(),
            P(),
        ),
        out_specs=P(patch, visit, None),
        check_vma=False,
    )
```

```python
import functools

import jax
import jax.numpy as jnp
from jax import lax
from jax.experimental import pallas as pl
from jax.experimental.pallas import tpu as pltpu
from jax.sharding import Mesh
from jax.sharding import PartitionSpec as P

S = 128
P_SIZE = 512
TAPS = 41
HALF = (TAPS - 1) // 2
BASIS = 5
BAND = 32
LANES = 128
META = 16
LEAD = 4
GROUP = 4


def match_kernel(coef_ref, dest_ref, off_ref, taps_ref, blocks_ref, weight_ref, out_ref, rows_tab, cols_tab, stack):
    count = blocks_ref.shape[0]
    row_id = lax.broadcasted_iota(jnp.int32, (S, S), 0)
    col_id = lax.broadcasted_iota(jnp.int32, (S, S), 1)
    inside = jnp.abs(row_id - col_id) <= HALF
    for k in range(BASIS):
        for which, table in ((0, rows_tab), (1, cols_tab)):
            taps = jnp.broadcast_to(taps_ref[which * 8 + k : which * 8 + k + 1, :], (8, S))
            band = jnp.concatenate(
                [pltpu.roll(taps, (S - HALF - LEAD + row) % S, 1, stride=1, stride_axis=0) for row in range(0, S, 8)]
            )
            table[:, k * S : (k + 1) * S] = jnp.where(inside, band, 0.0).astype(jnp.bfloat16)
    y = (lax.broadcasted_iota(jnp.int32, (S, 1), 0).astype(jnp.float32) - (S - 1) / 2.0) / S
    x = (lax.broadcasted_iota(jnp.int32, (1, S), 1).astype(jnp.float32) - (S - 1) / 2.0) / S

    def some(step, carry):
        for part in range(GROUP):
            i = step * GROUP + part
            across = jnp.dot(blocks_ref[i], rows_tab[...], preferred_element_type=jnp.float32)
            for k in range(BASIS):
                image = across[:, k * S : (k + 1) * S]
                plain = coef_ref[i, 3 * k] + coef_ref[i, 3 * k + 2] * x
                stack[part, k * S : (k + 1) * S, 0:S] = (image * plain).astype(jnp.bfloat16)
                stack[part, k * S : (k + 1) * S, S : 2 * S] = (image * coef_ref[i, 3 * k + 1]).astype(jnp.bfloat16)
        for part in range(GROUP):
            i = step * GROUP + part
            sums = jnp.dot(cols_tab[...], stack[part], preferred_element_type=jnp.float32)
            term = (sums[:, 0:S] + y * sums[:, S : 2 * S]) * weight_ref[i].astype(jnp.float32)
            out_ref[pl.ds(pl.multiple_of(i * S, S), S), :] = term.astype(jnp.bfloat16)
        return carry

    lax.fori_loop(0, count // GROUP, some, 0)

    line = lax.broadcasted_iota(jnp.int32, (META, S), 0)
    lane = lax.broadcasted_iota(jnp.int32, (META, S), 1)

    def tell(i, told):
        for n in range(2):
            row, col = off_ref[4 * i + 2 * n], off_ref[4 * i + 2 * n + 1]
            numbers = (dest_ref[2 * i + n], row // LANES, lax.rem(row, LANES), col // LANES, lax.rem(col, LANES))
            for at, number in enumerate(numbers):
                told = jnp.where((line == i) & (lane == 5 * n + at), number, told)
        return told

    told = lax.fori_loop(0, count, tell, jnp.zeros((META, S), jnp.int32))
    out_ref[count * S : count * S + META, :] = told.astype(jnp.float32).astype(jnp.bfloat16)


def match(blocks, weight, destinations, offsets, coefficients, basis_rows, basis_cols):
    rows = jnp.pad(basis_rows[:, ::-1].astype(jnp.float32), ((0, 8 - BASIS), (LEAD, S - TAPS - LEAD)))
    cols = jnp.pad(basis_cols.astype(jnp.float32), ((0, 8 - BASIS), (LEAD, S - TAPS - LEAD)))
    vmem = pl.BlockSpec(memory_space=pltpu.VMEM)
    smem = pl.BlockSpec(memory_space=pltpu.SMEM)
    return pl.pallas_call(
        match_kernel,
        out_shape=jax.ShapeDtypeStruct((blocks.shape[0] * S + META, S), jnp.bfloat16),
        in_specs=[smem, smem, smem, vmem, vmem, vmem],
        out_specs=vmem,
        scratch_shapes=[
            pltpu.VMEM((S, BASIS * S), jnp.bfloat16),
            pltpu.VMEM((S, BASIS * S), jnp.bfloat16),
            pltpu.VMEM((GROUP, BASIS * S, 2 * S), jnp.bfloat16),
        ],
        compiler_params=pltpu.CompilerParams(vmem_limit_bytes=32 * 2**20),
        cost_estimate=pl.CostEstimate(flops=2**30, bytes_accessed=16 * 2**20, transcendentals=0),
        name="match",
    )(coefficients, destinations.reshape(-1), offsets.reshape(-1), jnp.concatenate([rows, cols]), blocks, weight)


def pack_kernel(dest_ref, off_ref, weight_ref, after_ref, out_ref, taken):
    out_ref[...] = jnp.zeros_like(out_ref)
    line = lax.broadcasted_iota(jnp.int32, (META, S), 0)
    lane = lax.broadcasted_iota(jnp.int32, (META, S), 1)

    def clear(patch, carry):
        taken[patch] = 0
        return carry

    lax.fori_loop(0, out_ref.shape[0], clear, 0)

    def one(block, carry):
        value = weight_ref[block]
        for n in range(2):
            patch = dest_ref[2 * block + n]
            slot = taken[patch]
            taken[patch] = slot + 1
            row, col = off_ref[4 * block + 2 * n], off_ref[4 * block + 2 * n + 1]
            out_ref[patch, pl.ds(pl.multiple_of(slot * S, S), S), :] = value
            told = jnp.zeros((META, S), jnp.int32)
            for at, number in enumerate((1, row // LANES, lax.rem(row, LANES), col // LANES, lax.rem(col, LANES))):
                told = jnp.where(lane == at, number, told)
            before = out_ref[patch, 2 * S : 2 * S + META, :].astype(jnp.float32)
            now = jnp.where(line == slot, told.astype(jnp.float32), before)
            out_ref[patch, 2 * S : 2 * S + META, :] = now.astype(jnp.bfloat16)
        return carry

    lax.fori_loop(0, weight_ref.shape[0], one, 0)


def pack(weight, destinations, offsets, owners, after):
    smem = pl.BlockSpec(memory_space=pltpu.SMEM)
    vmem = pl.BlockSpec(memory_space=pltpu.VMEM)
    return pl.pallas_call(
        pack_kernel,
        out_shape=jax.ShapeDtypeStruct((owners, 2 * S + META, S), jnp.bfloat16),
        in_specs=[smem, smem, vmem, pl.BlockSpec(memory_space=pl.ANY)],
        out_specs=vmem,
        scratch_shapes=[pltpu.SMEM((owners,), jnp.int32)],
        compiler_params=pltpu.CompilerParams(vmem_limit_bytes=24 * 2**20),
        cost_estimate=pl.CostEstimate(flops=2**20, bytes_accessed=6 * 2**20, transcendentals=0),
        name="pack",
    )(destinations.reshape(-1), offsets.reshape(-1), weight, after)


def whole_kernel(meta_ref, slots_ref, out_ref, canvas):
    canvas[...] = jnp.zeros_like(canvas)
    lane = lax.broadcasted_iota(jnp.int32, (S, LANES), 1)

    def one(index, carry):
        base = 5 * index

        @pl.when(meta_ref[base] > 0)
        def add():
            row = meta_ref[base + 1] * LANES + meta_ref[base + 2]
            tile, shift = meta_ref[base + 3], meta_ref[base + 4]
            source, slot = index // 2, lax.rem(index, 2)
            value = slots_ref[source, pl.ds(pl.multiple_of(slot * S, S), S), :].astype(jnp.float32)
            value = pltpu.roll(value, shift, 1)
            canvas[tile, pl.ds(row, S), :] += jnp.where(lane >= shift, value, 0.0)
            canvas[tile + 1, pl.ds(row, S), :] += jnp.where(lane >= shift, 0.0, value)

        return carry

    lax.fori_loop(0, 2 * slots_ref.shape[0], one, 0)
    for tile in range(P_SIZE // LANES):
        out_ref[:, tile * LANES : (tile + 1) * LANES] = canvas[tile].astype(jnp.bfloat16)


def place_whole(meta, slots):
    return pl.pallas_call(
        whole_kernel,
        out_shape=jax.ShapeDtypeStruct((P_SIZE, P_SIZE), jnp.bfloat16),
        in_specs=[pl.BlockSpec(memory_space=pltpu.SMEM), pl.BlockSpec(memory_space=pltpu.VMEM)],
        out_specs=pl.BlockSpec(memory_space=pltpu.VMEM),
        scratch_shapes=[pltpu.VMEM((P_SIZE // LANES + 1, P_SIZE, LANES), jnp.float32)],
        compiler_params=pltpu.CompilerParams(vmem_limit_bytes=24 * 2**20),
        cost_estimate=pl.CostEstimate(flops=2**23, bytes_accessed=16 * 2**20, transcendentals=0),
        name="place_whole",
    )(meta, slots)


def halves_kernel(where_ref, *refs):
    parts, (out_ref, held, canvas, told, lines, sems) = refs[:8], refs[8:]
    copies = [pltpu.make_async_copy(part, held.at[i], sems.at[i]) for i, part in enumerate(parts)]
    for copy in copies:
        copy.start()
    mine, core = where_ref[0], where_ref[1]
    count = held.shape[1] // S
    canvas[...] = jnp.zeros_like(canvas)
    for copy in copies:
        copy.wait()
    told[...] = held[:, count * S : count * S + META, :].astype(jnp.float32).astype(jnp.int32)
    tell = pltpu.make_async_copy(told, lines, sems.at[len(parts)])
    tell.start()
    tell.wait()
    lane = lax.broadcasted_iota(jnp.int32, (S, LANES), 1)

    def one(index, carry):
        source, block = index // count, lax.rem(index, count)
        for n in range(2):
            patch, tile = lines[source, block, 5 * n], lines[source, block, 5 * n + 3]
            left, right = tile - 2 * core, tile + 1 - 2 * core

            @pl.when((patch // 8 == mine) & (right >= 0) & (left < 2))
            def add():
                row = lines[source, block, 5 * n + 1] * LANES + lines[source, block, 5 * n + 2]
                shift = lines[source, block, 5 * n + 4]
                spot = pl.ds(lax.rem(patch, 8) * P_SIZE + row, S)
                value = held[source, pl.ds(pl.multiple_of(block * S, S), S), :].astype(jnp.float32)
                value = pltpu.roll(value, shift, 1)

                @pl.when(left >= 0)
                def first():
                    canvas[left, spot, :] += jnp.where(lane >= shift, value, 0.0)

                @pl.when(right < 2)
                def second():
                    canvas[right, spot, :] += jnp.where(lane >= shift, 0.0, value)

        return carry

    lax.fori_loop(0, len(parts) * count, one, 0)
    for tile in range(2):
        out_ref[:, tile * LANES : (tile + 1) * LANES] = canvas[tile].astype(jnp.bfloat16)


def place_halves(where, parts):
    rows, lines = 8 * P_SIZE, (len(parts), META, S)
    return pl.pallas_call(
        halves_kernel,
        out_shape=jax.ShapeDtypeStruct((rows, 2 * LANES), jnp.bfloat16),
        in_specs=[pl.BlockSpec(memory_space=pltpu.SMEM)] + [pl.BlockSpec(memory_space=pl.ANY)] * len(parts),
        out_specs=pl.BlockSpec(memory_space=pltpu.VMEM),
        scratch_shapes=[
            pltpu.VMEM((len(parts),) + parts[0].shape, jnp.bfloat16),
            pltpu.VMEM((2, rows, LANES), jnp.float32),
            pltpu.VMEM(lines, jnp.int32),
            pltpu.SMEM(lines, jnp.int32),
            pltpu.SemaphoreType.DMA((len(parts) + 1,)),
        ],
        compiler_params=pltpu.CompilerParams(vmem_limit_bytes=40 * 2**20),
        cost_estimate=pl.CostEstimate(flops=2**24, bytes_accessed=24 * 2**20, transcendentals=0),
        name="place_halves",
    )(where, *parts)


def body(blocks, inv_variance, destinations, offsets, coefficients, basis_rows, basis_cols):
    count = blocks.shape[1]
    owners = lax.axis_size("x") * lax.axis_size("z")
    weight = inv_variance[0]
    where = jnp.stack([lax.axis_index("x"), lax.axis_index("core")]).astype(jnp.int32)
    terms = match(blocks[0], weight, destinations[0], offsets[0], coefficients[0], basis_rows, basis_cols)
    parts = []
    for lag in range(4):
        part = lax.ppermute(terms, "x", [(i, (i + lag) % 4) for i in range(4)]) if lag else terms
        parts += [part, lax.ppermute(part, "core", [(0, 1), (1, 0)])]

    slots = pack(weight, destinations[0], offsets[0], owners, parts[1])
    slots = lax.all_to_all(slots, ("x", "z"), 0, 0, tiled=True)
    told = slots[:, 2 * S : 2 * S + 2, :5].astype(jnp.int32).reshape(-1)
    den = place_whole(told, slots).reshape(16, BAND, P_SIZE)
    den = lax.all_to_all(den, ("y", "core"), 0, 0, tiled=True)

    num = place_halves(where, parts).reshape(8, P_SIZE, 2 * LANES)
    num = lax.psum_scatter(num, "z", scatter_dimension=0, tiled=True)
    num = lax.all_to_all(num.reshape(16, BAND, 2 * LANES), ("y", "core"), 0, 0, tiled=True)

    num = jnp.sum(num.reshape(8, 2, BAND, 2 * LANES).astype(jnp.float32), axis=0)
    num = jnp.concatenate([num[0], num[1]], axis=-1)
    den = jnp.sum(den.astype(jnp.float32), axis=0)
    return (num / jnp.maximum(den, 1.0))[None]


def solution(mesh):
    visits = mesh.shape["visit"]
    grid = Mesh(mesh.devices.reshape(visits // 2, 2, 4, mesh.shape["patch"] // 4), ("y", "core", "x", "z"))
    visit, patch = ("y", "core"), ("x", "z")
    return jax.shard_map(
        body,
        mesh=grid,
        in_specs=(
            P(visit, patch, None, None),
            P(visit, patch, None, None),
            P(visit, patch, None),
            P(visit, patch, None, None),
            P(visit, patch, None),
            P(),
            P(),
        ),
        out_specs=P(patch, visit, None),
        check_vma=False,
    )
```

```python
import functools

import jax
import jax.numpy as jnp
from jax import lax
from jax.experimental import pallas as pl
from jax.experimental.pallas import tpu as pltpu
from jax.sharding import Mesh
from jax.sharding import PartitionSpec as P

S = 128
P_SIZE = 512
TAPS = 41
HALF = (TAPS - 1) // 2
BASIS = 5
BAND = 32
LANES = 128
META = 16
LEAD = 4
GROUP = 4


def places(dest_ref, off_ref, block, n):
    row, col = off_ref[block, n, 0], off_ref[block, n, 1]
    return dest_ref[block, n], row // LANES, lax.rem(row, LANES), col // LANES, lax.rem(col, LANES)


def match_kernel(
    coef_ref, dest_ref, off_ref, taps_ref, blocks_ref, weight_ref, out_ref, rows_tab, cols_tab, stack, taken
):
    row_id = lax.broadcasted_iota(jnp.int32, (S, S), 0)
    col_id = lax.broadcasted_iota(jnp.int32, (S, S), 1)
    inside = jnp.abs(row_id - col_id) <= HALF
    for k in range(BASIS):
        for which, table in ((0, rows_tab), (1, cols_tab)):
            taps = jnp.broadcast_to(taps_ref[which * 8 + k : which * 8 + k + 1, :], (8, S))
            band = jnp.concatenate(
                [pltpu.roll(taps, (S - HALF - LEAD + row) % S, 1, stride=1, stride_axis=0) for row in range(0, S, 8)]
            )
            table[:, k * S : (k + 1) * S] = jnp.where(inside, band, 0.0).astype(jnp.bfloat16)
    y = (lax.broadcasted_iota(jnp.int32, (S, 1), 0).astype(jnp.float32) - (S - 1) / 2.0) / S
    x = (lax.broadcasted_iota(jnp.int32, (1, S), 1).astype(jnp.float32) - (S - 1) / 2.0) / S
    line = lax.broadcasted_iota(jnp.int32, (META, S), 0)
    lane = lax.broadcasted_iota(jnp.int32, (META, S), 1)

    def clear(patch, carry):
        taken[patch] = 0
        out_ref[patch, 2 * S : 2 * S + META, :] = jnp.zeros((META, S), jnp.bfloat16)
        return carry

    lax.fori_loop(0, out_ref.shape[0], clear, 0)

    def some(step, carry):
        for part in range(GROUP):
            i = step * GROUP + part
            across = jnp.dot(blocks_ref[i], rows_tab[...], preferred_element_type=jnp.float32)
            for k in range(BASIS):
                image = across[:, k * S : (k + 1) * S]
                plain = coef_ref[i, 3 * k] + coef_ref[i, 3 * k + 2] * x
                stack[part, k * S : (k + 1) * S, 0:S] = (image * plain).astype(jnp.bfloat16)
                stack[part, k * S : (k + 1) * S, S : 2 * S] = (image * coef_ref[i, 3 * k + 1]).astype(jnp.bfloat16)
        for part in range(GROUP):
            i = step * GROUP + part
            sums = jnp.dot(cols_tab[...], stack[part], preferred_element_type=jnp.float32)
            term = (sums[:, 0:S] + y * sums[:, S : 2 * S]) * weight_ref[i].astype(jnp.float32)
            term = term.astype(jnp.bfloat16)
            for n in range(2):
                patch, *numbers = places(dest_ref, off_ref, i, n)
                slot = taken[patch]
                taken[patch] = slot + 1
                out_ref[patch, pl.ds(pl.multiple_of(slot * S, S), S), :] = term
                told = out_ref[patch, 2 * S : 2 * S + META, :].astype(jnp.float32).astype(jnp.int32)
                for at, number in enumerate([1] + numbers):
                    told = jnp.where((line == slot) & (lane == at), number, told)
                out_ref[patch, 2 * S : 2 * S + META, :] = told.astype(jnp.float32).astype(jnp.bfloat16)
        return carry

    lax.fori_loop(0, blocks_ref.shape[0] // GROUP, some, 0)


def match(blocks, weight, destinations, offsets, coefficients, basis_rows, basis_cols, owners):
    rows = jnp.pad(basis_rows[:, ::-1].astype(jnp.float32), ((0, 8 - BASIS), (LEAD, S - TAPS - LEAD)))
    cols = jnp.pad(basis_cols.astype(jnp.float32), ((0, 8 - BASIS), (LEAD, S - TAPS - LEAD)))
    vmem = pl.BlockSpec(memory_space=pltpu.VMEM)
    smem = pl.BlockSpec(memory_space=pltpu.SMEM)
    return pl.pallas_call(
        match_kernel,
        out_shape=jax.ShapeDtypeStruct((owners, 2 * S + META, S), jnp.bfloat16),
        in_specs=[smem, smem, smem, vmem, vmem, vmem],
        out_specs=vmem,
        scratch_shapes=[
            pltpu.VMEM((S, BASIS * S), jnp.bfloat16),
            pltpu.VMEM((S, BASIS * S), jnp.bfloat16),
            pltpu.VMEM((GROUP, BASIS * S, 2 * S), jnp.bfloat16),
            pltpu.SMEM((owners,), jnp.int32),
        ],
        compiler_params=pltpu.CompilerParams(vmem_limit_bytes=32 * 2**20),
        cost_estimate=pl.CostEstimate(flops=2**30, bytes_accessed=16 * 2**20, transcendentals=0),
        name="match",
    )(coefficients, destinations, offsets, jnp.concatenate([rows, cols]), blocks, weight)


def lines_kernel(dest_ref, off_ref, weight_ref, out_ref, told, sems):
    count = dest_ref.shape[0]
    body = pltpu.make_async_copy(weight_ref, out_ref.at[pl.ds(0, count * S)], sems.at[0])
    body.start()
    line = lax.broadcasted_iota(jnp.int32, (META, S), 0)
    lane = lax.broadcasted_iota(jnp.int32, (META, S), 1)
    words = jnp.zeros((META, S), jnp.int32)
    for block in range(count):
        for n in range(2):
            for at, number in enumerate(places(dest_ref, off_ref, block, n)):
                words = jnp.where((line == n) & (lane == 8 * block + at), number, words)
    told[...] = words.astype(jnp.float32).astype(jnp.bfloat16)
    tail = pltpu.make_async_copy(told, out_ref.at[pl.ds(count * S, META)], sems.at[1])
    tail.start()
    body.wait()
    tail.wait()


def with_lines(weight, destinations, offsets):
    smem = pl.BlockSpec(memory_space=pltpu.SMEM)
    rows = weight.shape[0] * S
    return pl.pallas_call(
        lines_kernel,
        out_shape=jax.ShapeDtypeStruct((rows + META, S), jnp.bfloat16),
        in_specs=[smem, smem, pl.BlockSpec(memory_space=pl.ANY)],
        out_specs=pl.BlockSpec(memory_space=pl.ANY),
        scratch_shapes=[pltpu.VMEM((META, S), jnp.bfloat16), pltpu.SemaphoreType.DMA((2,))],
        compiler_params=pltpu.CompilerParams(vmem_limit_bytes=4 * 2**20),
        cost_estimate=pl.CostEstimate(flops=2**16, bytes_accessed=2**20, transcendentals=0),
        name="lines",
    )(destinations, offsets, weight.reshape(rows, S))


def whole_kernel(meta_ref, slots_ref, out_ref, canvas):
    canvas[...] = jnp.zeros_like(canvas)
    lane = lax.broadcasted_iota(jnp.int32, (S, LANES), 1)

    def one(index, carry):
        base = 5 * index

        @pl.when(meta_ref[base] > 0)
        def add():
            row = meta_ref[base + 1] * LANES + meta_ref[base + 2]
            tile, shift = meta_ref[base + 3], meta_ref[base + 4]
            source, slot = index // 2, lax.rem(index, 2)
            value = slots_ref[source, pl.ds(pl.multiple_of(slot * S, S), S), :].astype(jnp.float32)
            value = pltpu.roll(value, shift, 1)
            canvas[tile, pl.ds(row, S), :] += jnp.where(lane >= shift, value, 0.0)
            canvas[tile + 1, pl.ds(row, S), :] += jnp.where(lane >= shift, 0.0, value)

        return carry

    lax.fori_loop(0, 2 * slots_ref.shape[0], one, 0)
    for tile in range(P_SIZE // LANES):
        out_ref[:, tile * LANES : (tile + 1) * LANES] = canvas[tile].astype(jnp.bfloat16)


def place_whole(meta, slots):
    return pl.pallas_call(
        whole_kernel,
        out_shape=jax.ShapeDtypeStruct((P_SIZE, P_SIZE), jnp.bfloat16),
        in_specs=[pl.BlockSpec(memory_space=pltpu.SMEM), pl.BlockSpec(memory_space=pltpu.VMEM)],
        out_specs=pl.BlockSpec(memory_space=pltpu.VMEM),
        scratch_shapes=[pltpu.VMEM((P_SIZE // LANES + 1, P_SIZE, LANES), jnp.float32)],
        compiler_params=pltpu.CompilerParams(vmem_limit_bytes=24 * 2**20),
        cost_estimate=pl.CostEstimate(flops=2**23, bytes_accessed=16 * 2**20, transcendentals=0),
        name="place_whole",
    )(meta, slots)


def halves_kernel(where_ref, parts_ref, out_ref, held, canvas, told, lines, sems):
    count = parts_ref.shape[1] // S
    fetch = pltpu.make_async_copy(parts_ref, held, sems.at[0])
    fetch.start()
    mine, core = where_ref[0], where_ref[1]
    canvas[...] = jnp.zeros_like(canvas)
    fetch.wait()
    words = held[:, count * S : count * S + META, :].astype(jnp.float32).astype(jnp.int32)
    told[...] = words[:, 0:8, :]
    tell = pltpu.make_async_copy(told, lines, sems.at[1])
    tell.start()
    tell.wait()
    lane = lax.broadcasted_iota(jnp.int32, (S, LANES), 1)

    def one(index, carry):
        source, block = index // count, lax.rem(index, count)
        for n in range(2):
            patch, tile = lines[source, n, 8 * block], lines[source, n, 8 * block + 3]
            left, right = tile - 2 * core, tile + 1 - 2 * core

            @pl.when((patch // 8 == mine) & (right >= 0) & (left < 2))
            def add():
                row = lines[source, n, 8 * block + 1] * LANES + lines[source, n, 8 * block + 2]
                shift = lines[source, n, 8 * block + 4]
                spot = pl.ds(lax.rem(patch, 8) * P_SIZE + row, S)
                value = held[source, pl.ds(pl.multiple_of(block * S, S), S), :].astype(jnp.float32)
                value = pltpu.roll(value, shift, 1)

                @pl.when(left >= 0)
                def first():
                    canvas[left, spot, :] += jnp.where(lane >= shift, value, 0.0)

                @pl.when(right < 2)
                def second():
                    canvas[right, spot, :] += jnp.where(lane >= shift, 0.0, value)

        return carry

    lax.fori_loop(0, parts_ref.shape[0] * count, one, 0)
    for band in range(out_ref.shape[0]):
        for patch in range(8):
            start = patch * P_SIZE + band * 2 * BAND
            for tile in range(2):
                rows = canvas[tile, start : start + 2 * BAND, :]
                out_ref[band, patch, :, tile * LANES : (tile + 1) * LANES] = rows.astype(jnp.bfloat16)


def place_halves(where, parts):
    sources = parts.shape[0]
    return pl.pallas_call(
        halves_kernel,
        out_shape=jax.ShapeDtypeStruct((P_SIZE // (2 * BAND), 8, 2 * BAND, 2 * LANES), jnp.bfloat16),
        in_specs=[pl.BlockSpec(memory_space=pltpu.SMEM), pl.BlockSpec(memory_space=pl.ANY)],
        out_specs=pl.BlockSpec(memory_space=pltpu.VMEM),
        scratch_shapes=[
            pltpu.VMEM(parts.shape, jnp.bfloat16),
            pltpu.VMEM((2, 8 * P_SIZE, LANES), jnp.float32),
            pltpu.VMEM((sources, 8, S), jnp.int32),
            pltpu.SMEM((sources, 8, S), jnp.int32),
            pltpu.SemaphoreType.DMA((2,)),
        ],
        compiler_params=pltpu.CompilerParams(vmem_limit_bytes=40 * 2**20),
        cost_estimate=pl.CostEstimate(flops=2**24, bytes_accessed=24 * 2**20, transcendentals=0),
        name="place_halves",
    )(where, parts)


def body(blocks, inv_variance, destinations, offsets, coefficients, basis_rows, basis_cols):
    owners = lax.axis_size("x") * lax.axis_size("z")
    weight = inv_variance[0]
    where = jnp.stack([lax.axis_index("x"), lax.axis_index("core")]).astype(jnp.int32)

    near = lax.all_gather(with_lines(weight, destinations[0], offsets[0]), ("core", "x"))
    den = place_halves(where, near)
    den = lax.psum_scatter(den, "y", scatter_dimension=0, tiled=True)
    den = lax.all_to_all(den.reshape(16, BAND, 2 * LANES), ("z", "core"), 0, 0, tiled=True)

    slots = match(blocks[0], weight, destinations[0], offsets[0], coefficients[0], basis_rows, basis_cols, owners)
    slots = lax.all_to_all(slots, ("x", "z"), 0, 0, tiled=True)
    told = slots[:, 2 * S : 2 * S + 2, :5].astype(jnp.int32).reshape(-1)
    num = place_whole(told, slots).reshape(16, BAND, P_SIZE)
    num = lax.all_to_all(num, ("y", "core"), 0, 0, tiled=True)

    num = jnp.sum(num.astype(jnp.float32), axis=0)
    den = jnp.sum(den.reshape(8, 2, BAND, 2 * LANES).astype(jnp.float32), axis=0)
    den = jnp.concatenate([den[0], den[1]], axis=-1)
    return (num / jnp.maximum(den, 1.0))[None]


def solution(mesh):
    visits = mesh.shape["visit"]
    grid = Mesh(mesh.devices.reshape(visits // 2, 2, 4, mesh.shape["patch"] // 4), ("y", "core", "x", "z"))
    visit, patch = ("y", "core"), ("x", "z")
    return jax.shard_map(
        body,
        mesh=grid,
        in_specs=(
            P(visit, patch, None, None),
            P(visit, patch, None, None),
            P(visit, patch, None),
            P(visit, patch, None, None),
            P(visit, patch, None),
            P(),
            P(),
        ),
        out_specs=P(patch, visit, None),
        check_vma=False,
    )
```

```python
import functools

import jax
import jax.numpy as jnp
from jax import lax
from jax.experimental import pallas as pl
from jax.experimental.pallas import tpu as pltpu
from jax.sharding import Mesh
from jax.sharding import PartitionSpec as P

S = 128
P_SIZE = 512
TAPS = 41
HALF = (TAPS - 1) // 2
BASIS = 5
BAND = 32
LANES = 128
META = 16
LEAD = 4
GROUP = 4


def places(dest_ref, off_ref, block, n):
    row, col = off_ref[n, 0, block], off_ref[n, 1, block]
    return dest_ref[n, block], row // LANES, lax.rem(row, LANES), col // LANES, lax.rem(col, LANES)


def match_kernel(
    coef_ref, dest_ref, off_ref, rows_ref, cols_ref, blocks_ref, weight_ref,
    out_ref, near_ref, wide, rows_tab, cols_tab, stack, told, taken, sems,
):
    count = blocks_ref.shape[0]
    body = pltpu.make_async_copy(weight_ref, near_ref.at[pl.ds(0, count * S)], sems.at[0])
    body.start()
    line = lax.broadcasted_iota(jnp.int32, (META, S), 0)
    lane = lax.broadcasted_iota(jnp.int32, (META, S), 1)
    words = jnp.zeros((META, S), jnp.int32)
    for block in range(count):
        for n in range(2):
            for at, number in enumerate(places(dest_ref, off_ref, block, n)):
                words = jnp.where((line == n) & (lane == 8 * block + at), number, words)
    told[...] = words.astype(jnp.float32).astype(jnp.bfloat16)
    tail = pltpu.make_async_copy(told, near_ref.at[pl.ds(count * S, META)], sems.at[1])
    tail.start()

    row_id = lax.broadcasted_iota(jnp.int32, (S, S), 0)
    col_id = lax.broadcasted_iota(jnp.int32, (S, S), 1)
    inside = jnp.abs(row_id - col_id) <= HALF
    wide[...] = jnp.zeros_like(wide)
    wide[0:BASIS, LEAD : LEAD + TAPS] = rows_ref[...].astype(jnp.float32)
    wide[8 : 8 + BASIS, LEAD : LEAD + TAPS] = cols_ref[...].astype(jnp.float32)
    for which in range(2):
        for k in range(BASIS):
            taps = jnp.broadcast_to(wide[which * 8 + k : which * 8 + k + 1, :], (8, S))
            band = jnp.concatenate(
                [pltpu.roll(taps, (S - HALF - LEAD + row) % S, 1, stride=1, stride_axis=0) for row in range(0, S, 8)]
            )
            band = jnp.where(inside, band, 0.0).astype(jnp.bfloat16)
            if which:
                cols_tab[:, k * S : (k + 1) * S] = band
            else:
                rows_tab[k * S : (k + 1) * S, :] = band
    y = (lax.broadcasted_iota(jnp.int32, (S, 1), 0).astype(jnp.float32) - (S - 1) / 2.0) / S
    x = (lax.broadcasted_iota(jnp.int32, (1, S), 1).astype(jnp.float32) - (S - 1) / 2.0) / S

    def clear(patch, carry):
        taken[patch] = 0
        out_ref[patch, 2 * S : 2 * S + META, :] = jnp.zeros((META, S), jnp.bfloat16)
        return carry

    lax.fori_loop(0, out_ref.shape[0], clear, 0)

    def some(step, carry):
        for part in range(GROUP):
            i = step * GROUP + part
            across = lax.dot_general(
                blocks_ref[i], rows_tab[...], (((1,), (1,)), ((), ())), preferred_element_type=jnp.float32
            )
            for k in range(BASIS):
                image = across[:, k * S : (k + 1) * S]
                plain = coef_ref[3 * k, i] + coef_ref[3 * k + 2, i] * x
                stack[part, k * S : (k + 1) * S, 0:S] = (image * plain).astype(jnp.bfloat16)
                stack[part, k * S : (k + 1) * S, S : 2 * S] = (image * coef_ref[3 * k + 1, i]).astype(jnp.bfloat16)
        for part in range(GROUP):
            i = step * GROUP + part
            sums = jnp.dot(cols_tab[...], stack[part], preferred_element_type=jnp.float32)
            weight = weight_ref[pl.ds(pl.multiple_of(i * S, S), S), :].astype(jnp.float32)
            term = ((sums[:, 0:S] + y * sums[:, S : 2 * S]) * weight).astype(jnp.bfloat16)
            for n in range(2):
                patch, *numbers = places(dest_ref, off_ref, i, n)
                slot = taken[patch]
                taken[patch] = slot + 1
                out_ref[patch, pl.ds(pl.multiple_of(slot * S, S), S), :] = term
                notes = out_ref[patch, 2 * S : 2 * S + META, :].astype(jnp.float32).astype(jnp.int32)
                for at, number in enumerate([1] + numbers):
                    notes = jnp.where((line == slot) & (lane == at), number, notes)
                out_ref[patch, 2 * S : 2 * S + META, :] = notes.astype(jnp.float32).astype(jnp.bfloat16)
        return carry

    lax.fori_loop(0, count // GROUP, some, 0)
    body.wait()
    tail.wait()


def match(blocks, weight, destinations, offsets, coefficients, basis_rows, basis_cols, owners):
    vmem = pl.BlockSpec(memory_space=pltpu.VMEM)
    smem = pl.BlockSpec(memory_space=pltpu.SMEM)
    rows = weight.shape[0] * S
    return pl.pallas_call(
        match_kernel,
        out_shape=[
            jax.ShapeDtypeStruct((owners, 2 * S + META, S), jnp.bfloat16),
            jax.ShapeDtypeStruct((rows + META, S), jnp.bfloat16),
        ],
        in_specs=[smem, smem, smem, vmem, vmem, vmem, vmem],
        out_specs=[vmem, vmem],
        scratch_shapes=[
            pltpu.VMEM((16, S), jnp.float32),
            pltpu.VMEM((BASIS * S, S), jnp.bfloat16),
            pltpu.VMEM((S, BASIS * S), jnp.bfloat16),
            pltpu.VMEM((GROUP, BASIS * S, 2 * S), jnp.bfloat16),
            pltpu.VMEM((META, S), jnp.bfloat16),
            pltpu.SMEM((owners,), jnp.int32),
            pltpu.SemaphoreType.DMA((2,)),
        ],
        compiler_params=pltpu.CompilerParams(vmem_limit_bytes=32 * 2**20),
        cost_estimate=pl.CostEstimate(flops=2**30, bytes_accessed=16 * 2**20, transcendentals=0),
        name="match",
    )(
        coefficients.T,
        destinations.T,
        jnp.transpose(offsets, (1, 2, 0)),
        basis_rows,
        basis_cols,
        blocks,
        weight.reshape(rows, S),
    )


def listed(codes, total, queue, idle):
    def one(i, found):
        code = codes(i)
        queue[found] = code
        return found + jnp.where(code >= 0, 1, 0)

    found = lax.fori_loop(0, total, one, jnp.int32(0), unroll=8)
    queue[found] = idle
    queue[found + 1] = idle
    return found


def add_pieces(queue, found, blocks, canvas):
    lane = lax.broadcasted_iota(jnp.int32, (S, LANES), 1)

    def pair(step, carry):
        values = []
        for part in range(2):
            code = queue[2 * step + part]
            shift = code & 127
            value = pltpu.roll(blocks((code >> 7) & 127).astype(jnp.float32), shift, 1)
            values.append((code >> 17, (code >> 14) & 7, value, lane >= shift))
        for row, tile, value, here in values:
            canvas[tile, pl.ds(row, S), :] += jnp.where(here, value, 0.0)
            canvas[tile + 1, pl.ds(row, S), :] += jnp.where(here, 0.0, value)
        return carry

    lax.fori_loop(0, (found + 1) // 2, pair, 0)


def whole_kernel(slots_ref, out_ref, canvas, told, codes, queue, sem):
    sources = slots_ref.shape[0]
    notes = slots_ref[:, 2 * S : 2 * S + META, :].astype(jnp.float32).astype(jnp.int32)[:, 0:8, :]
    notes = notes.reshape(sources * 8, S)
    at = [notes] + [pltpu.roll(notes, S - i, 1) for i in range(1, 5)]
    place = lax.broadcasted_iota(jnp.int32, notes.shape, 0)
    place = (place >> 3) * 2 + (place & 7)
    code = ((at[1] * LANES + at[2]) << 17) + (at[3] << 14) + (place << 7) + at[4]
    code = jnp.where(at[0] > 0, code, -1)[:, 0:1].reshape(sources, 8, 1)
    lane = lax.broadcasted_iota(jnp.int32, (sources, 8, S), 2)
    source = lax.broadcasted_iota(jnp.int32, (sources, 8, S), 0)
    told[...] = jnp.sum(jnp.where(lane == source, code, 0), axis=0)
    tell = pltpu.make_async_copy(told, codes, sem)
    tell.start()
    for tile in range(P_SIZE // LANES):
        canvas[tile] = jnp.zeros((P_SIZE, LANES), jnp.float32)
    tell.wait()
    found = listed(lambda i: codes[i & 1, i >> 1], 2 * sources, queue, (P_SIZE // LANES) << 14)

    def block(i):
        return slots_ref[i >> 1, pl.ds(pl.multiple_of((i & 1) * S, S), S), :]

    add_pieces(queue, found, block, canvas)
    for tile in range(P_SIZE // LANES):
        out_ref[:, tile * LANES : (tile + 1) * LANES] = canvas[tile].astype(jnp.bfloat16)


def place_whole(slots):
    sources = slots.shape[0]
    return pl.pallas_call(
        whole_kernel,
        out_shape=jax.ShapeDtypeStruct((P_SIZE, P_SIZE), jnp.bfloat16),
        in_specs=[pl.BlockSpec(memory_space=pltpu.VMEM)],
        out_specs=pl.BlockSpec(memory_space=pltpu.VMEM),
        scratch_shapes=[
            pltpu.VMEM((P_SIZE // LANES + 2, P_SIZE, LANES), jnp.float32),
            pltpu.VMEM((8, S), jnp.int32),
            pltpu.SMEM((8, S), jnp.int32),
            pltpu.SMEM((2 * sources + 2,), jnp.int32),
            pltpu.SemaphoreType.DMA,
        ],
        compiler_params=pltpu.CompilerParams(vmem_limit_bytes=24 * 2**20),
        cost_estimate=pl.CostEstimate(flops=2**23, bytes_accessed=16 * 2**20, transcendentals=0),
        name="place_whole",
    )(slots)


def halves_kernel(where_ref, *refs):
    parts, (out_ref, held, canvas, told, codes, queue, sems) = refs[:8], refs[8:]
    count, sources = held.shape[1] // S, len(parts)
    copies = [pltpu.make_async_copy(part, held.at[i], sems.at[i]) for i, part in enumerate(parts)]
    for copy in copies:
        copy.start()
    mine, core = where_ref[0], where_ref[1]
    for tile in (1, 2):
        canvas[tile] = jnp.zeros((8 * P_SIZE, LANES), jnp.float32)
    for copy in copies:
        copy.wait()
    notes = held[:, count * S : count * S + META, :].astype(jnp.float32).astype(jnp.int32)[:, 0:8, :]
    notes = notes.reshape(sources * 8, S)
    at = [notes] + [pltpu.roll(notes, S - i, 1) for i in range(1, 5)]
    place = lax.broadcasted_iota(jnp.int32, notes.shape, 0) >> 3
    place = place * count + (lax.broadcasted_iota(jnp.int32, notes.shape, 1) >> 3)
    tile = at[3] - 2 * core + 1
    row = (at[0] & 7) * P_SIZE + at[1] * LANES + at[2]
    code = (row << 17) + (tile << 14) + (place << 7) + at[4]
    code = jnp.where(((at[0] >> 3) == mine) & (tile >= 0) & (tile <= 2), code, -1)
    first = (lax.broadcasted_iota(jnp.int32, (8, S), 1) & 7) == 0
    words = jnp.zeros((8, S), jnp.int32)
    for i in range(sources):
        words += pltpu.roll(jnp.where(first, code[8 * i : 8 * i + 8, :], 0), i, 1)
    told[...] = words
    tell = pltpu.make_async_copy(told, codes, sems.at[sources])
    tell.start()
    tell.wait()

    found = listed(lambda i: codes[i // S, lax.rem(i, S)], 2 * sources * count, queue, 3 << 14)

    def block(i):
        return held[lax.div(i, count), pl.ds(pl.multiple_of(lax.rem(i, count) * S, S), S), :]

    add_pieces(queue, found, block, canvas)
    for band in range(out_ref.shape[0]):
        for patch in range(8):
            start = patch * P_SIZE + band * 2 * BAND
            for half in range(2):
                rows = canvas[half + 1, start : start + 2 * BAND, :]
                out_ref[band, patch, :, half * LANES : (half + 1) * LANES] = rows.astype(jnp.bfloat16)


def place_halves(where, parts):
    sources = len(parts)
    pieces = 2 * sources * (parts[0].shape[0] // S)
    return pl.pallas_call(
        halves_kernel,
        out_shape=jax.ShapeDtypeStruct((P_SIZE // (2 * BAND), 8, 2 * BAND, 2 * LANES), jnp.bfloat16),
        in_specs=[pl.BlockSpec(memory_space=pltpu.SMEM)] + [pl.BlockSpec(memory_space=pl.ANY)] * sources,
        out_specs=pl.BlockSpec(memory_space=pltpu.VMEM),
        scratch_shapes=[
            pltpu.VMEM((sources,) + parts[0].shape, jnp.bfloat16),
            pltpu.VMEM((5, 8 * P_SIZE, LANES), jnp.float32),
            pltpu.VMEM((8, S), jnp.int32),
            pltpu.SMEM((8, S), jnp.int32),
            pltpu.SMEM((pieces + 2,), jnp.int32),
            pltpu.SemaphoreType.DMA((sources + 1,)),
        ],
        compiler_params=pltpu.CompilerParams(vmem_limit_bytes=40 * 2**20),
        cost_estimate=pl.CostEstimate(flops=2**24, bytes_accessed=24 * 2**20, transcendentals=0),
        name="place_halves",
    )(where, *parts)


def body(blocks, inv_variance, destinations, offsets, coefficients, basis_rows, basis_cols):
    owners = lax.axis_size("x") * lax.axis_size("z")
    where = jnp.stack([lax.axis_index("x"), lax.axis_index("core")]).astype(jnp.int32)
    slots, near = match(
        blocks[0], inv_variance[0], destinations[0], offsets[0], coefficients[0], basis_rows, basis_cols, owners
    )

    parts = []
    for lag in range(4):
        part = lax.ppermute(near, "x", [(i, (i + lag) % 4) for i in range(4)]) if lag else near
        parts += [part, lax.ppermute(part, "core", [(0, 1), (1, 0)])]
    den = place_halves(where, parts)
    den = lax.psum_scatter(den, "y", scatter_dimension=0, tiled=True)
    den = lax.all_to_all(den.reshape(16, BAND, 2 * LANES), ("z", "core"), 0, 0, tiled=True)

    slots = lax.all_to_all(slots, ("x", "z"), 0, 0, tiled=True)
    num = place_whole(slots).reshape(16, BAND, P_SIZE)
    num = lax.all_to_all(num, ("y", "core"), 0, 0, tiled=True)

    num = jnp.sum(num.astype(jnp.float32), axis=0)
    den = jnp.sum(den.reshape(8, 2, BAND, 2 * LANES).astype(jnp.float32), axis=0)
    den = jnp.concatenate([den[0], den[1]], axis=-1)
    return (num / jnp.maximum(den, 1.0))[None]


def solution(mesh):
    visits = mesh.shape["visit"]
    grid = Mesh(mesh.devices.reshape(visits // 2, 2, 4, mesh.shape["patch"] // 4), ("y", "core", "x", "z"))
    visit, patch = ("y", "core"), ("x", "z")
    return jax.shard_map(
        body,
        mesh=grid,
        in_specs=(
            P(visit, patch, None, None),
            P(visit, patch, None, None),
            P(visit, patch, None),
            P(visit, patch, None, None),
            P(visit, patch, None),
            P(),
            P(),
        ),
        out_specs=P(patch, visit, None),
        check_vma=False,
    )
```

```python
import functools

import jax
import jax.numpy as jnp
from jax import lax
from jax.experimental import pallas as pl
from jax.experimental.pallas import tpu as pltpu
from jax.sharding import Mesh
from jax.sharding import PartitionSpec as P

S = 128
P_SIZE = 512
TAPS = 41
HALF = (TAPS - 1) // 2
BASIS = 5
BAND = 32
LANES = 128
META = 16
LEAD = 4
GROUP = 4


def places(dest_ref, off_ref, block, n):
    row, col = off_ref[n, 0, block], off_ref[n, 1, block]
    return dest_ref[n, block], row // LANES, lax.rem(row, LANES), col // LANES, lax.rem(col, LANES)


def match_kernel(
    coef_ref, dest_ref, off_ref, rows_ref, cols_ref, blocks_ref, weight_ref, out_ref, wide, rows_tab, cols_tab, stack, taken
):
    count = blocks_ref.shape[0]
    line = lax.broadcasted_iota(jnp.int32, (META, S), 0)
    lane = lax.broadcasted_iota(jnp.int32, (META, S), 1)
    row_id = lax.broadcasted_iota(jnp.int32, (S, S), 0)
    col_id = lax.broadcasted_iota(jnp.int32, (S, S), 1)
    inside = jnp.abs(row_id - col_id) <= HALF
    wide[...] = jnp.zeros_like(wide)
    wide[0:BASIS, LEAD : LEAD + TAPS] = rows_ref[...].astype(jnp.float32)
    wide[8 : 8 + BASIS, LEAD : LEAD + TAPS] = cols_ref[...].astype(jnp.float32)
    for which in range(2):
        for k in range(BASIS):
            taps = jnp.broadcast_to(wide[which * 8 + k : which * 8 + k + 1, :], (8, S))
            band = jnp.concatenate(
                [pltpu.roll(taps, (S - HALF - LEAD + row) % S, 1, stride=1, stride_axis=0) for row in range(0, S, 8)]
            )
            band = jnp.where(inside, band, 0.0).astype(jnp.bfloat16)
            if which:
                cols_tab[:, k * S : (k + 1) * S] = band
            else:
                rows_tab[k * S : (k + 1) * S, :] = band
    y = (lax.broadcasted_iota(jnp.int32, (S, 1), 0).astype(jnp.float32) - (S - 1) / 2.0) / S
    x = (lax.broadcasted_iota(jnp.int32, (1, S), 1).astype(jnp.float32) - (S - 1) / 2.0) / S

    def clear(patch, carry):
        taken[patch] = 0
        out_ref[patch, 2 * S : 2 * S + META, :] = jnp.zeros((META, S), jnp.bfloat16)
        return carry

    lax.fori_loop(0, out_ref.shape[0], clear, 0)

    def some(step, carry):
        for part in range(GROUP):
            i = step * GROUP + part
            across = lax.dot_general(
                blocks_ref[i], rows_tab[...], (((1,), (1,)), ((), ())), preferred_element_type=jnp.float32
            )
            for k in range(BASIS):
                image = across[:, k * S : (k + 1) * S]
                plain = coef_ref[3 * k, i] + coef_ref[3 * k + 2, i] * x
                stack[part, k * S : (k + 1) * S, 0:S] = (image * plain).astype(jnp.bfloat16)
                stack[part, k * S : (k + 1) * S, S : 2 * S] = (image * coef_ref[3 * k + 1, i]).astype(jnp.bfloat16)
        for part in range(GROUP):
            i = step * GROUP + part
            sums = jnp.dot(cols_tab[...], stack[part], preferred_element_type=jnp.float32)
            weight = weight_ref[i].astype(jnp.float32)
            term = ((sums[:, 0:S] + y * sums[:, S : 2 * S]) * weight).astype(jnp.bfloat16)
            for n in range(2):
                patch, *numbers = places(dest_ref, off_ref, i, n)
                slot = taken[patch]
                taken[patch] = slot + 1
                out_ref[patch, pl.ds(pl.multiple_of(slot * S, S), S), :] = term
                notes = out_ref[patch, 2 * S : 2 * S + META, :].astype(jnp.float32).astype(jnp.int32)
                for at, number in enumerate([1] + numbers):
                    notes = jnp.where((line == slot) & (lane == at), number, notes)
                out_ref[patch, 2 * S : 2 * S + META, :] = notes.astype(jnp.float32).astype(jnp.bfloat16)
        return carry

    lax.fori_loop(0, count // GROUP, some, 0)


def match(blocks, weight, destinations, offsets, coefficients, basis_rows, basis_cols, owners):
    vmem = pl.BlockSpec(memory_space=pltpu.VMEM)
    smem = pl.BlockSpec(memory_space=pltpu.SMEM)
    return pl.pallas_call(
        match_kernel,
        out_shape=jax.ShapeDtypeStruct((owners, 2 * S + META, S), jnp.bfloat16),
        in_specs=[smem, smem, smem, vmem, vmem, vmem, vmem],
        out_specs=vmem,
        scratch_shapes=[
            pltpu.VMEM((16, S), jnp.float32),
            pltpu.VMEM((BASIS * S, S), jnp.bfloat16),
            pltpu.VMEM((S, BASIS * S), jnp.bfloat16),
            pltpu.VMEM((GROUP, BASIS * S, 2 * S), jnp.bfloat16),
            pltpu.SMEM((owners,), jnp.int32),
        ],
        compiler_params=pltpu.CompilerParams(vmem_limit_bytes=32 * 2**20),
        cost_estimate=pl.CostEstimate(flops=2**30, bytes_accessed=16 * 2**20, transcendentals=0),
        name="match",
    )(
        coefficients.T,
        destinations.T,
        jnp.transpose(offsets, (1, 2, 0)),
        basis_rows,
        basis_cols,
        blocks,
        weight,
    )


def lines_kernel(dest_ref, off_ref, weight_ref, near_ref):
    rows = weight_ref.shape[0]
    for copy in range(near_ref.shape[0]):
        near_ref[copy, 0:rows, :] = weight_ref[...]
    line = lax.broadcasted_iota(jnp.int32, (META, S), 0)
    lane = lax.broadcasted_iota(jnp.int32, (META, S), 1)
    words = jnp.zeros((META, S), jnp.int32)
    for block in range(rows // S):
        for n in range(2):
            for at, number in enumerate(places(dest_ref, off_ref, block, n)):
                words = jnp.where((line == n) & (lane == 8 * block + at), number, words)
    words = words.astype(jnp.float32).astype(jnp.bfloat16)
    for copy in range(near_ref.shape[0]):
        near_ref[copy, rows : rows + META, :] = words


def with_lines(weight, destinations, offsets, copies):
    smem = pl.BlockSpec(memory_space=pltpu.SMEM)
    vmem = pl.BlockSpec(memory_space=pltpu.VMEM)
    rows = weight.shape[0] * S
    return pl.pallas_call(
        lines_kernel,
        out_shape=jax.ShapeDtypeStruct((copies, rows + META, S), jnp.bfloat16),
        in_specs=[smem, smem, vmem],
        out_specs=vmem,
        compiler_params=pltpu.CompilerParams(vmem_limit_bytes=8 * 2**20),
        cost_estimate=pl.CostEstimate(flops=2**16, bytes_accessed=2**22, transcendentals=0),
        name="lines",
    )(destinations.T, jnp.transpose(offsets, (1, 2, 0)), weight.reshape(rows, S))


def together_kernel(large_ref, small_ref, large_out, small_out):
    small_out[...] = small_ref[...]


def together(large, small):
    hbm = pl.BlockSpec(memory_space=pltpu.HBM)
    vmem = pl.BlockSpec(memory_space=pltpu.VMEM)
    return pl.pallas_call(
        together_kernel,
        out_shape=[jax.ShapeDtypeStruct(array.shape, array.dtype) for array in (large, small)],
        in_specs=[hbm, vmem],
        out_specs=[hbm, vmem],
        input_output_aliases={0: 0},
        compiler_params=pltpu.CompilerParams(vmem_limit_bytes=12 * 2**20),
        cost_estimate=pl.CostEstimate(flops=2**16, bytes_accessed=2**22, transcendentals=0),
        name="together",
    )(large, small)


def listed(codes, total, queue, idle):
    def one(i, found):
        code = codes(i)
        queue[found] = code
        return found + jnp.where(code >= 0, 1, 0)

    found = lax.fori_loop(0, total, one, jnp.int32(0), unroll=8)
    queue[found] = idle
    queue[found + 1] = idle
    return found


def add_pieces(queue, found, blocks, canvas):
    lane = lax.broadcasted_iota(jnp.int32, (S, LANES), 1)

    def pair(step, carry):
        values = []
        for part in range(2):
            code = queue[2 * step + part]
            shift = code & 127
            value = pltpu.roll(blocks((code >> 7) & 127).astype(jnp.float32), shift, 1)
            values.append((code >> 17, (code >> 14) & 7, value, lane >= shift))
        for row, tile, value, here in values:
            canvas[tile, pl.ds(row, S), :] += jnp.where(here, value, 0.0)
            canvas[tile + 1, pl.ds(row, S), :] += jnp.where(here, 0.0, value)
        return carry

    lax.fori_loop(0, (found + 1) // 2, pair, 0)


def whole_kernel(slots_ref, out_ref, canvas, told, codes, queue, sem):
    sources = slots_ref.shape[0]
    notes = slots_ref[:, 2 * S : 2 * S + META, :].astype(jnp.float32).astype(jnp.int32)[:, 0:8, :]
    notes = notes.reshape(sources * 8, S)
    at = [notes] + [pltpu.roll(notes, S - i, 1) for i in range(1, 5)]
    place = lax.broadcasted_iota(jnp.int32, notes.shape, 0)
    place = (place >> 3) * 2 + (place & 7)
    code = ((at[1] * LANES + at[2]) << 17) + (at[3] << 14) + (place << 7) + at[4]
    code = jnp.where(at[0] > 0, code, -1)[:, 0:1].reshape(sources, 8, 1)
    lane = lax.broadcasted_iota(jnp.int32, (sources, 8, S), 2)
    source = lax.broadcasted_iota(jnp.int32, (sources, 8, S), 0)
    told[...] = jnp.sum(jnp.where(lane == source, code, 0), axis=0)
    tell = pltpu.make_async_copy(told, codes, sem)
    tell.start()
    for tile in range(P_SIZE // LANES):
        canvas[tile] = jnp.zeros((P_SIZE, LANES), jnp.float32)
    tell.wait()
    found = listed(lambda i: codes[i & 1, i >> 1], 2 * sources, queue, (P_SIZE // LANES) << 14)

    def block(i):
        return slots_ref[i >> 1, pl.ds(pl.multiple_of((i & 1) * S, S), S), :]

    add_pieces(queue, found, block, canvas)
    for tile in range(P_SIZE // LANES):
        out_ref[:, tile * LANES : (tile + 1) * LANES] = canvas[tile].astype(jnp.bfloat16)


def place_whole(slots):
    sources = slots.shape[0]
    return pl.pallas_call(
        whole_kernel,
        out_shape=jax.ShapeDtypeStruct((P_SIZE, P_SIZE), jnp.bfloat16),
        in_specs=[pl.BlockSpec(memory_space=pltpu.VMEM)],
        out_specs=pl.BlockSpec(memory_space=pltpu.VMEM),
        scratch_shapes=[
            pltpu.VMEM((P_SIZE // LANES + 2, P_SIZE, LANES), jnp.float32),
            pltpu.VMEM((8, S), jnp.int32),
            pltpu.SMEM((8, S), jnp.int32),
            pltpu.SMEM((2 * sources + 2,), jnp.int32),
            pltpu.SemaphoreType.DMA,
        ],
        compiler_params=pltpu.CompilerParams(vmem_limit_bytes=24 * 2**20),
        cost_estimate=pl.CostEstimate(flops=2**23, bytes_accessed=16 * 2**20, transcendentals=0),
        name="place_whole",
    )(slots)


def halves_kernel(where_ref, *refs):
    parts, (out_ref, held, canvas, told, codes, queue, sems) = refs[:2], refs[2:]
    sources, count = held.shape[0], held.shape[1] // S
    copies = [
        pltpu.make_async_copy(part, held.at[pl.ds(i * sources // 2, sources // 2)], sems.at[i])
        for i, part in enumerate(parts)
    ]
    for copy in copies:
        copy.start()
    mine, core = where_ref[0], where_ref[1]
    for tile in (1, 2):
        canvas[tile] = jnp.zeros((8 * P_SIZE, LANES), jnp.float32)
    for copy in copies:
        copy.wait()
    notes = held[:, count * S : count * S + META, :].astype(jnp.float32).astype(jnp.int32)[:, 0:8, :]
    notes = notes.reshape(sources * 8, S)
    at = [notes] + [pltpu.roll(notes, S - i, 1) for i in range(1, 5)]
    place = lax.broadcasted_iota(jnp.int32, notes.shape, 0) >> 3
    place = place * count + (lax.broadcasted_iota(jnp.int32, notes.shape, 1) >> 3)
    tile = at[3] - 2 * core + 1
    row = (at[0] & 7) * P_SIZE + at[1] * LANES + at[2]
    code = (row << 17) + (tile << 14) + (place << 7) + at[4]
    code = jnp.where(((at[0] >> 3) == mine) & (tile >= 0) & (tile <= 2), code, -1)
    first = (lax.broadcasted_iota(jnp.int32, (8, S), 1) & 7) == 0
    words = jnp.zeros((8, S), jnp.int32)
    for i in range(sources):
        words += pltpu.roll(jnp.where(first, code[8 * i : 8 * i + 8, :], 0), i, 1)
    told[...] = words
    tell = pltpu.make_async_copy(told, codes, sems.at[len(parts)])
    tell.start()
    tell.wait()

    found = listed(lambda i: codes[i // S, lax.rem(i, S)], 2 * sources * count, queue, 3 << 14)

    def block(i):
        return held[lax.div(i, count), pl.ds(pl.multiple_of(lax.rem(i, count) * S, S), S), :]

    add_pieces(queue, found, block, canvas)
    for band in range(out_ref.shape[0]):
        for patch in range(8):
            start = patch * P_SIZE + band * 2 * BAND
            for half in range(2):
                rows = canvas[half + 1, start : start + 2 * BAND, :]
                out_ref[band, patch, :, half * LANES : (half + 1) * LANES] = rows.astype(jnp.bfloat16)


def place_halves(where, parts):
    sources, rows = 2 * parts[0].shape[0], parts[0].shape[1]
    return pl.pallas_call(
        halves_kernel,
        out_shape=jax.ShapeDtypeStruct((P_SIZE // (2 * BAND), 8, 2 * BAND, 2 * LANES), jnp.bfloat16),
        in_specs=[pl.BlockSpec(memory_space=pltpu.SMEM)] + [pl.BlockSpec(memory_space=pl.ANY)] * len(parts),
        out_specs=pl.BlockSpec(memory_space=pltpu.VMEM),
        scratch_shapes=[
            pltpu.VMEM((sources, rows, S), jnp.bfloat16),
            pltpu.VMEM((5, 8 * P_SIZE, LANES), jnp.float32),
            pltpu.VMEM((8, S), jnp.int32),
            pltpu.SMEM((8, S), jnp.int32),
            pltpu.SMEM((2 * sources * (rows // S) + 2,), jnp.int32),
            pltpu.SemaphoreType.DMA((len(parts) + 1,)),
        ],
        compiler_params=pltpu.CompilerParams(vmem_limit_bytes=40 * 2**20),
        cost_estimate=pl.CostEstimate(flops=2**24, bytes_accessed=24 * 2**20, transcendentals=0),
        name="place_halves",
    )(where, *parts)


def body(blocks, inv_variance, destinations, offsets, coefficients, basis_rows, basis_cols):
    owners = lax.axis_size("x") * lax.axis_size("z")
    where = jnp.stack([lax.axis_index("x"), lax.axis_index("core")]).astype(jnp.int32)
    weight = inv_variance[0]
    near = with_lines(weight, destinations[0], offsets[0], lax.axis_size("x"))
    near = lax.all_to_all(near, "x", 0, 0, tiled=True)
    slots = match(blocks[0], weight, destinations[0], offsets[0], coefficients[0], basis_rows, basis_cols, owners)
    slots, near = together(slots, near)

    parts = [near, lax.ppermute(near, "core", [(0, 1), (1, 0)])]
    den = place_halves(where, parts)
    den = lax.psum_scatter(den, "y", scatter_dimension=0, tiled=True)
    den = lax.all_to_all(den.reshape(16, BAND, 2 * LANES), ("z", "core"), 0, 0, tiled=True)

    slots = lax.all_to_all(slots, ("x", "z"), 0, 0, tiled=True)
    num = place_whole(slots).reshape(16, BAND, P_SIZE)
    num = lax.all_to_all(num, ("y", "core"), 0, 0, tiled=True)

    num = jnp.sum(num.astype(jnp.float32), axis=0)
    den = jnp.sum(den.reshape(8, 2, BAND, 2 * LANES).astype(jnp.float32), axis=0)
    den = jnp.concatenate([den[0], den[1]], axis=-1)
    return (num / jnp.maximum(den, 1.0))[None]


def solution(mesh):
    visits = mesh.shape["visit"]
    grid = Mesh(mesh.devices.reshape(visits // 2, 2, 4, mesh.shape["patch"] // 4), ("y", "core", "x", "z"))
    visit, patch = ("y", "core"), ("x", "z")
    return jax.shard_map(
        body,
        mesh=grid,
        in_specs=(
            P(visit, patch, None, None),
            P(visit, patch, None, None),
            P(visit, patch, None),
            P(visit, patch, None, None),
            P(visit, patch, None),
            P(),
            P(),
        ),
        out_specs=P(patch, visit, None),
        check_vma=False,
    )
```

```python
import functools

import jax
import jax.numpy as jnp
from jax import lax
from jax.experimental import pallas as pl
from jax.experimental.pallas import tpu as pltpu
from jax.sharding import Mesh
from jax.sharding import PartitionSpec as P

S = 128
P_SIZE = 512
TAPS = 41
HALF = (TAPS - 1) // 2
BASIS = 5
BAND = 32
LANES = 128
META = 16
LEAD = 4
GROUP = 4


def places(dest_ref, off_ref, block, n):
    row, col = off_ref[n, 0, block], off_ref[n, 1, block]
    return dest_ref[n, block], row // LANES, lax.rem(row, LANES), col // LANES, lax.rem(col, LANES)


def match_kernel(
    coef_ref, dest_ref, off_ref, rows_ref, cols_ref, blocks_ref, weight_ref, out_ref, wide, rows_tab, cols_tab, stack, taken
):
    count = blocks_ref.shape[0]
    line = lax.broadcasted_iota(jnp.int32, (META, S), 0)
    lane = lax.broadcasted_iota(jnp.int32, (META, S), 1)
    row_id = lax.broadcasted_iota(jnp.int32, (S, S), 0)
    col_id = lax.broadcasted_iota(jnp.int32, (S, S), 1)
    inside = jnp.abs(row_id - col_id) <= HALF
    wide[...] = jnp.zeros_like(wide)
    wide[0:BASIS, LEAD : LEAD + TAPS] = rows_ref[...].astype(jnp.float32)
    wide[8 : 8 + BASIS, LEAD : LEAD + TAPS] = cols_ref[...].astype(jnp.float32)
    for which in range(2):
        for k in range(BASIS):
            taps = jnp.broadcast_to(wide[which * 8 + k : which * 8 + k + 1, :], (8, S))
            band = jnp.concatenate(
                [pltpu.roll(taps, (S - HALF - LEAD + row) % S, 1, stride=1, stride_axis=0) for row in range(0, S, 8)]
            )
            band = jnp.where(inside, band, 0.0).astype(jnp.bfloat16)
            if which:
                cols_tab[:, k * S : (k + 1) * S] = band
            else:
                rows_tab[k * S : (k + 1) * S, :] = band
    y = (lax.broadcasted_iota(jnp.int32, (S, 1), 0).astype(jnp.float32) - (S - 1) / 2.0) / S
    x = (lax.broadcasted_iota(jnp.int32, (1, S), 1).astype(jnp.float32) - (S - 1) / 2.0) / S

    def clear(patch, carry):
        taken[patch] = 0
        out_ref[patch, 2 * S : 2 * S + META, :] = jnp.zeros((META, S), jnp.bfloat16)
        return carry

    lax.fori_loop(0, out_ref.shape[0], clear, 0)

    def some(step, carry):
        for part in range(GROUP):
            i = step * GROUP + part
            across = lax.dot_general(
                blocks_ref[i], rows_tab[...], (((1,), (1,)), ((), ())), preferred_element_type=jnp.float32
            )
            for k in range(BASIS):
                image = across[:, k * S : (k + 1) * S]
                plain = coef_ref[3 * k, i] + coef_ref[3 * k + 2, i] * x
                stack[part, k * S : (k + 1) * S, 0:S] = (image * plain).astype(jnp.bfloat16)
                stack[part, k * S : (k + 1) * S, S : 2 * S] = (image * coef_ref[3 * k + 1, i]).astype(jnp.bfloat16)
        for part in range(GROUP):
            i = step * GROUP + part
            sums = jnp.dot(cols_tab[...], stack[part], preferred_element_type=jnp.float32)
            weight = weight_ref[i].astype(jnp.float32)
            term = ((sums[:, 0:S] + y * sums[:, S : 2 * S]) * weight).astype(jnp.bfloat16)
            for n in range(2):
                patch, *numbers = places(dest_ref, off_ref, i, n)
                slot = taken[patch]
                taken[patch] = slot + 1
                out_ref[patch, pl.ds(pl.multiple_of(slot * S, S), S), :] = term
                notes = out_ref[patch, 2 * S : 2 * S + META, :].astype(jnp.float32).astype(jnp.int32)
                for at, number in enumerate([1] + numbers):
                    notes = jnp.where((line == slot) & (lane == at), number, notes)
                out_ref[patch, 2 * S : 2 * S + META, :] = notes.astype(jnp.float32).astype(jnp.bfloat16)
        return carry

    lax.fori_loop(0, count // GROUP, some, 0)


def match(blocks, weight, destinations, offsets, coefficients, basis_rows, basis_cols, owners):
    vmem = pl.BlockSpec(memory_space=pltpu.VMEM)
    smem = pl.BlockSpec(memory_space=pltpu.SMEM)
    return pl.pallas_call(
        match_kernel,
        out_shape=jax.ShapeDtypeStruct((owners, 2 * S + META, S), jnp.bfloat16),
        in_specs=[smem, smem, smem, vmem, vmem, vmem, vmem],
        out_specs=vmem,
        scratch_shapes=[
            pltpu.VMEM((16, S), jnp.float32),
            pltpu.VMEM((BASIS * S, S), jnp.bfloat16),
            pltpu.VMEM((S, BASIS * S), jnp.bfloat16),
            pltpu.VMEM((GROUP, BASIS * S, 2 * S), jnp.bfloat16),
            pltpu.SMEM((owners,), jnp.int32),
        ],
        compiler_params=pltpu.CompilerParams(vmem_limit_bytes=12 * 2**20),
        cost_estimate=pl.CostEstimate(flops=2**30, bytes_accessed=16 * 2**20, transcendentals=0),
        name="match",
    )(
        coefficients.T,
        destinations.T,
        jnp.transpose(offsets, (1, 2, 0)),
        basis_rows,
        basis_cols,
        blocks,
        weight,
    )


def lines_kernel(dest_ref, off_ref, weight_ref, near_ref):
    rows = weight_ref.shape[0]
    near_ref[0:rows, :] = weight_ref[...]
    line = lax.broadcasted_iota(jnp.int32, (META, S), 0)
    lane = lax.broadcasted_iota(jnp.int32, (META, S), 1)
    words = jnp.zeros((META, S), jnp.int32)
    for block in range(rows // S):
        for n in range(2):
            for at, number in enumerate(places(dest_ref, off_ref, block, n)):
                words = jnp.where((line == n) & (lane == 8 * block + at), number, words)
    near_ref[rows : rows + META, :] = words.astype(jnp.float32).astype(jnp.bfloat16)


def with_lines(weight, destinations, offsets):
    smem = pl.BlockSpec(memory_space=pltpu.SMEM)
    vmem = pl.BlockSpec(memory_space=pltpu.VMEM)
    rows = weight.shape[0] * S
    return pl.pallas_call(
        lines_kernel,
        out_shape=jax.ShapeDtypeStruct((rows + META, S), jnp.bfloat16),
        in_specs=[smem, smem, vmem],
        out_specs=vmem,
        compiler_params=pltpu.CompilerParams(vmem_limit_bytes=8 * 2**20),
        cost_estimate=pl.CostEstimate(flops=2**16, bytes_accessed=2**22, transcendentals=0),
        name="lines",
    )(destinations.T, jnp.transpose(offsets, (1, 2, 0)), weight.reshape(rows, S))


def held_kernel(large_ref, *refs):
    pass


def held_until(large, *others):
    hbm = pl.BlockSpec(memory_space=pltpu.HBM)
    return pl.pallas_call(
        held_kernel,
        out_shape=jax.ShapeDtypeStruct(large.shape, large.dtype),
        in_specs=[hbm] + [pl.BlockSpec(memory_space=pl.ANY)] * len(others),
        out_specs=hbm,
        input_output_aliases={0: 0},
        name="held_until",
    )(large, *others)


def turn_kernel(where_ref, den_ref, *out_refs):
    for lag, out_ref in enumerate(out_refs):
        out_ref[...] = den_ref[lax.rem(where_ref[2] + lag, len(out_refs))]


def turned(where, den):
    vmem = pl.BlockSpec(memory_space=pltpu.VMEM)
    return pl.pallas_call(
        turn_kernel,
        out_shape=[jax.ShapeDtypeStruct(den.shape[1:], den.dtype)] * den.shape[0],
        in_specs=[pl.BlockSpec(memory_space=pltpu.SMEM), vmem],
        out_specs=[vmem] * den.shape[0],
        cost_estimate=pl.CostEstimate(flops=2**16, bytes_accessed=2**21, transcendentals=0),
        name="turned",
    )(where, den)


def sum_kernel(where_ref, *refs):
    blocks, (keep_ref, give_ref) = refs[:-2], refs[-2:]
    total = blocks[0][...].astype(jnp.float32)
    for block in blocks[1:]:
        total += block[...].astype(jnp.float32)
    even = where_ref[1] == 0
    keep_ref[...] = jnp.where(even, total[0:BAND], total[BAND : 2 * BAND])
    give_ref[...] = jnp.where(even, total[BAND : 2 * BAND], total[0:BAND])


def summed(where, blocks):
    vmem = pl.BlockSpec(memory_space=pltpu.VMEM)
    return pl.pallas_call(
        sum_kernel,
        out_shape=[jax.ShapeDtypeStruct((BAND, blocks[0].shape[1]), jnp.float32)] * 2,
        in_specs=[pl.BlockSpec(memory_space=pltpu.SMEM)] + [vmem] * len(blocks),
        out_specs=[vmem, vmem],
        cost_estimate=pl.CostEstimate(flops=2**18, bytes_accessed=2**21, transcendentals=0),
        name="summed",
    )(where, *blocks)


def divide_kernel(where_ref, num_ref, kept_ref, given_ref, out_ref):
    num = num_ref[0].astype(jnp.float32)
    for visit in range(1, num_ref.shape[0]):
        num += num_ref[visit].astype(jnp.float32)
    even = where_ref[1] == 0
    width = kept_ref.shape[1]
    left = jnp.where(even, kept_ref[...], given_ref[...])
    right = jnp.where(even, given_ref[...], kept_ref[...])
    out_ref[0, :, 0:width] = num[:, 0:width] / jnp.maximum(left, 1.0)
    out_ref[0, :, width : 2 * width] = num[:, width : 2 * width] / jnp.maximum(right, 1.0)


def divided(where, num, kept, given):
    vmem = pl.BlockSpec(memory_space=pltpu.VMEM)
    return pl.pallas_call(
        divide_kernel,
        out_shape=jax.ShapeDtypeStruct((1, BAND, P_SIZE), jnp.float32),
        in_specs=[pl.BlockSpec(memory_space=pltpu.SMEM), vmem, vmem, vmem],
        out_specs=vmem,
        cost_estimate=pl.CostEstimate(flops=2**18, bytes_accessed=2**20, transcendentals=0),
        name="divided",
    )(where, num, kept, given)


def listed(codes, total, queue, idle):
    def one(i, found):
        code = codes(i)
        queue[found] = code
        return found + jnp.where(code >= 0, 1, 0)

    found = lax.fori_loop(0, total, one, jnp.int32(0), unroll=8)
    queue[found] = idle
    queue[found + 1] = idle
    return found


def add_pieces(queue, found, blocks, canvas):
    lane = lax.broadcasted_iota(jnp.int32, (S, LANES), 1)

    def pair(step, carry):
        values = []
        for part in range(2):
            code = queue[2 * step + part]
            shift = code & 127
            value = pltpu.roll(blocks((code >> 7) & 127).astype(jnp.float32), shift, 1)
            values.append((code >> 17, (code >> 14) & 7, value, lane >= shift))
        for row, tile, value, here in values:
            canvas[tile, pl.ds(row, S), :] += jnp.where(here, value, 0.0)
            canvas[tile + 1, pl.ds(row, S), :] += jnp.where(here, 0.0, value)
        return carry

    lax.fori_loop(0, (found + 1) // 2, pair, 0)


def whole_kernel(slots_ref, out_ref, canvas, told, codes, queue, sem):
    sources = slots_ref.shape[0]
    notes = slots_ref[:, 2 * S : 2 * S + META, :].astype(jnp.float32).astype(jnp.int32)[:, 0:8, :]
    notes = notes.reshape(sources * 8, S)
    at = [notes] + [pltpu.roll(notes, S - i, 1) for i in range(1, 5)]
    place = lax.broadcasted_iota(jnp.int32, notes.shape, 0)
    place = (place >> 3) * 2 + (place & 7)
    code = ((at[1] * LANES + at[2]) << 17) + (at[3] << 14) + (place << 7) + at[4]
    code = jnp.where(at[0] > 0, code, -1)[:, 0:1].reshape(sources, 8, 1)
    lane = lax.broadcasted_iota(jnp.int32, (sources, 8, S), 2)
    source = lax.broadcasted_iota(jnp.int32, (sources, 8, S), 0)
    told[...] = jnp.sum(jnp.where(lane == source, code, 0), axis=0)
    tell = pltpu.make_async_copy(told, codes, sem)
    tell.start()
    for tile in range(P_SIZE // LANES):
        canvas[tile] = jnp.zeros((P_SIZE, LANES), jnp.float32)
    tell.wait()
    found = listed(lambda i: codes[i & 1, i >> 1], 2 * sources, queue, (P_SIZE // LANES) << 14)

    def block(i):
        return slots_ref[i >> 1, pl.ds(pl.multiple_of((i & 1) * S, S), S), :]

    add_pieces(queue, found, block, canvas)
    for tile in range(P_SIZE // LANES):
        out_ref[:, tile * LANES : (tile + 1) * LANES] = canvas[tile].astype(jnp.bfloat16)


def place_whole(slots):
    sources = slots.shape[0]
    return pl.pallas_call(
        whole_kernel,
        out_shape=jax.ShapeDtypeStruct((P_SIZE, P_SIZE), jnp.bfloat16),
        in_specs=[pl.BlockSpec(memory_space=pltpu.VMEM)],
        out_specs=pl.BlockSpec(memory_space=pltpu.VMEM),
        scratch_shapes=[
            pltpu.VMEM((P_SIZE // LANES + 2, P_SIZE, LANES), jnp.float32),
            pltpu.VMEM((8, S), jnp.int32),
            pltpu.SMEM((8, S), jnp.int32),
            pltpu.SMEM((2 * sources + 2,), jnp.int32),
            pltpu.SemaphoreType.DMA,
        ],
        compiler_params=pltpu.CompilerParams(vmem_limit_bytes=8 * 2**20),
        cost_estimate=pl.CostEstimate(flops=2**23, bytes_accessed=16 * 2**20, transcendentals=0),
        name="place_whole",
    )(slots)


def halves_kernel(where_ref, *refs):
    parts, (out_ref, held, canvas, told, codes, queue, sems) = refs[:8], refs[8:]
    count, sources = held.shape[1] // S, len(parts)
    copies = [pltpu.make_async_copy(part, held.at[i], sems.at[i]) for i, part in enumerate(parts)]
    for copy in copies:
        copy.start()
    mine, core = where_ref[0], where_ref[1]
    for tile in (1, 2):
        canvas[tile] = jnp.zeros((8 * P_SIZE, LANES), jnp.float32)
    for copy in copies:
        copy.wait()
    notes = held[:, count * S : count * S + META, :].astype(jnp.float32).astype(jnp.int32)[:, 0:8, :]
    notes = notes.reshape(sources * 8, S)
    at = [notes] + [pltpu.roll(notes, S - i, 1) for i in range(1, 5)]
    place = lax.broadcasted_iota(jnp.int32, notes.shape, 0) >> 3
    place = place * count + (lax.broadcasted_iota(jnp.int32, notes.shape, 1) >> 3)
    tile = at[3] - 2 * core + 1
    row = (at[0] & 7) * P_SIZE + at[1] * LANES + at[2]
    code = (row << 17) + (tile << 14) + (place << 7) + at[4]
    code = jnp.where(((at[0] >> 3) == mine) & (tile >= 0) & (tile <= 2), code, -1)
    first = (lax.broadcasted_iota(jnp.int32, (8, S), 1) & 7) == 0
    words = jnp.zeros((8, S), jnp.int32)
    for i in range(sources):
        words += pltpu.roll(jnp.where(first, code[8 * i : 8 * i + 8, :], 0), i, 1)
    told[...] = words
    tell = pltpu.make_async_copy(told, codes, sems.at[sources])
    tell.start()
    tell.wait()

    found = listed(lambda i: codes[i // S, lax.rem(i, S)], 2 * sources * count, queue, 3 << 14)

    def block(i):
        return held[lax.div(i, count), pl.ds(pl.multiple_of(lax.rem(i, count) * S, S), S), :]

    add_pieces(queue, found, block, canvas)
    for band in range(out_ref.shape[0]):
        for patch in range(8):
            start = patch * P_SIZE + band * 2 * BAND
            for half in range(2):
                rows = canvas[half + 1, start : start + 2 * BAND, :]
                out_ref[band, patch, :, half * LANES : (half + 1) * LANES] = rows.astype(jnp.bfloat16)


def place_halves(where, parts):
    sources = len(parts)
    pieces = 2 * sources * (parts[0].shape[0] // S)
    return pl.pallas_call(
        halves_kernel,
        out_shape=jax.ShapeDtypeStruct((P_SIZE // (2 * BAND), 8, 2 * BAND, 2 * LANES), jnp.bfloat16),
        in_specs=[pl.BlockSpec(memory_space=pltpu.SMEM)] + [pl.BlockSpec(memory_space=pl.ANY)] * sources,
        out_specs=pl.BlockSpec(memory_space=pltpu.VMEM),
        scratch_shapes=[
            pltpu.VMEM((sources,) + parts[0].shape, jnp.bfloat16),
            pltpu.VMEM((5, 8 * P_SIZE, LANES), jnp.float32),
            pltpu.VMEM((8, S), jnp.int32),
            pltpu.SMEM((8, S), jnp.int32),
            pltpu.SMEM((pieces + 2,), jnp.int32),
            pltpu.SemaphoreType.DMA((sources + 1,)),
        ],
        compiler_params=pltpu.CompilerParams(vmem_limit_bytes=22 * 2**20),
        cost_estimate=pl.CostEstimate(flops=2**24, bytes_accessed=24 * 2**20, transcendentals=0),
        name="place_halves",
    )(where, *parts)


def body(blocks, inv_variance, destinations, offsets, coefficients, basis_rows, basis_cols):
    owners = lax.axis_size("x") * lax.axis_size("z")
    where = jnp.stack([lax.axis_index("x"), lax.axis_index("core"), lax.axis_index("z")]).astype(jnp.int32)
    weight = inv_variance[0]
    swap = [(0, 1), (1, 0)]

    near = with_lines(weight, destinations[0], offsets[0])
    along = [lax.ppermute(near, "x", [(i, (i + lag) % 4) for i in range(4)]) for lag in (2, 1, 3)]
    parts = [near] + along
    parts = parts + [lax.ppermute(part, "core", swap) for part in parts]
    den = place_halves(where, parts)
    den = lax.psum_scatter(den, "y", scatter_dimension=0, tiled=True)[0]

    slots = match(blocks[0], weight, destinations[0], offsets[0], coefficients[0], basis_rows, basis_cols, owners)
    slots = lax.all_to_all(held_until(slots, *along, parts[4]), ("x", "z"), 0, 0, tiled=True)
    num = place_whole(slots).reshape(16, BAND, P_SIZE)
    num = lax.all_to_all(num, ("y", "core"), 0, 0, tiled=True)

    steps = list(turned(where, den))
    steps = steps[:1] + [
        lax.ppermute(step, "z", [(i, (i + lag) % 8) for i in range(8)]) for lag, step in enumerate(steps) if lag
    ]
    kept, given = summed(where, steps)
    return divided(where, num, kept, lax.ppermute(given, "core", swap))


def solution(mesh):
    visits = mesh.shape["visit"]
    grid = Mesh(mesh.devices.reshape(visits // 2, 2, 4, mesh.shape["patch"] // 4), ("y", "core", "x", "z"))
    visit, patch = ("y", "core"), ("x", "z")
    return jax.shard_map(
        body,
        mesh=grid,
        in_specs=(
            P(visit, patch, None, None),
            P(visit, patch, None, None),
            P(visit, patch, None),
            P(visit, patch, None, None),
            P(visit, patch, None),
            P(),
            P(),
        ),
        out_specs=P(patch, visit, None),
        check_vma=False,
    )
```

```python
import functools

import jax
import jax.numpy as jnp
from jax import lax
from jax.experimental import pallas as pl
from jax.experimental.pallas import tpu as pltpu
from jax.sharding import Mesh
from jax.sharding import PartitionSpec as P

S = 128
P_SIZE = 512
TAPS = 41
HALF = (TAPS - 1) // 2
BASIS = 5
BAND = 32
LANES = 128
META = 16
LEAD = 4
GROUP = 4


def places(dest_ref, off_ref, block, n):
    row, col = off_ref[n, 0, block], off_ref[n, 1, block]
    return dest_ref[n, block], row // LANES, lax.rem(row, LANES), col // LANES, lax.rem(col, LANES)


def match_kernel(
    coef_ref, dest_ref, off_ref, rows_ref, cols_ref, blocks_ref, weight_ref, out_ref, wide, rows_tab, cols_tab, stack, taken
):
    count = blocks_ref.shape[0]
    line = lax.broadcasted_iota(jnp.int32, (META, S), 0)
    lane = lax.broadcasted_iota(jnp.int32, (META, S), 1)
    row_id = lax.broadcasted_iota(jnp.int32, (S, S), 0)
    col_id = lax.broadcasted_iota(jnp.int32, (S, S), 1)
    inside = jnp.abs(row_id - col_id) <= HALF
    wide[...] = jnp.zeros_like(wide)
    wide[0:BASIS, LEAD : LEAD + TAPS] = rows_ref[...].astype(jnp.float32)
    wide[8 : 8 + BASIS, LEAD : LEAD + TAPS] = cols_ref[...].astype(jnp.float32)
    for which in range(2):
        for k in range(BASIS):
            taps = jnp.broadcast_to(wide[which * 8 + k : which * 8 + k + 1, :], (8, S))
            band = jnp.concatenate(
                [pltpu.roll(taps, (S - HALF - LEAD + row) % S, 1, stride=1, stride_axis=0) for row in range(0, S, 8)]
            )
            band = jnp.where(inside, band, 0.0).astype(jnp.bfloat16)
            if which:
                cols_tab[:, k * S : (k + 1) * S] = band
            else:
                rows_tab[k * S : (k + 1) * S, :] = band
    y = (lax.broadcasted_iota(jnp.int32, (S, 1), 0).astype(jnp.float32) - (S - 1) / 2.0) / S
    x = (lax.broadcasted_iota(jnp.int32, (1, S), 1).astype(jnp.float32) - (S - 1) / 2.0) / S

    def clear(patch, carry):
        taken[patch] = 0
        out_ref[patch, 2 * S : 2 * S + META, :] = jnp.zeros((META, S), jnp.bfloat16)
        return carry

    lax.fori_loop(0, out_ref.shape[0], clear, 0)

    def some(step, carry):
        for part in range(GROUP):
            i = step * GROUP + part
            across = lax.dot_general(
                blocks_ref[i], rows_tab[...], (((1,), (1,)), ((), ())), preferred_element_type=jnp.float32
            )
            for k in range(BASIS):
                image = across[:, k * S : (k + 1) * S]
                plain = coef_ref[3 * k, i] + coef_ref[3 * k + 2, i] * x
                stack[part, k * S : (k + 1) * S, 0:S] = (image * plain).astype(jnp.bfloat16)
                stack[part, k * S : (k + 1) * S, S : 2 * S] = (image * coef_ref[3 * k + 1, i]).astype(jnp.bfloat16)
        for part in range(GROUP):
            i = step * GROUP + part
            sums = jnp.dot(cols_tab[...], stack[part], preferred_element_type=jnp.float32)
            weight = weight_ref[i].astype(jnp.float32)
            term = ((sums[:, 0:S] + y * sums[:, S : 2 * S]) * weight).astype(jnp.bfloat16)
            for n in range(2):
                patch, *numbers = places(dest_ref, off_ref, i, n)
                slot = taken[patch]
                taken[patch] = slot + 1
                out_ref[patch, pl.ds(pl.multiple_of(slot * S, S), S), :] = term
                notes = out_ref[patch, 2 * S : 2 * S + META, :].astype(jnp.float32).astype(jnp.int32)
                for at, number in enumerate([1] + numbers):
                    notes = jnp.where((line == slot) & (lane == at), number, notes)
                out_ref[patch, 2 * S : 2 * S + META, :] = notes.astype(jnp.float32).astype(jnp.bfloat16)
        return carry

    lax.fori_loop(0, count // GROUP, some, 0)


def match(blocks, weight, destinations, offsets, coefficients, basis_rows, basis_cols, owners):
    vmem = pl.BlockSpec(memory_space=pltpu.VMEM)
    smem = pl.BlockSpec(memory_space=pltpu.SMEM)
    return pl.pallas_call(
        match_kernel,
        out_shape=jax.ShapeDtypeStruct((owners, 2 * S + META, S), jnp.bfloat16),
        in_specs=[smem, smem, smem, vmem, vmem, vmem, vmem],
        out_specs=vmem,
        scratch_shapes=[
            pltpu.VMEM((16, S), jnp.float32),
            pltpu.VMEM((BASIS * S, S), jnp.bfloat16),
            pltpu.VMEM((S, BASIS * S), jnp.bfloat16),
            pltpu.VMEM((GROUP, BASIS * S, 2 * S), jnp.bfloat16),
            pltpu.SMEM((owners,), jnp.int32),
        ],
        compiler_params=pltpu.CompilerParams(vmem_limit_bytes=60 * 2**20),
        cost_estimate=pl.CostEstimate(flops=2**30, bytes_accessed=16 * 2**20, transcendentals=0),
        name="match",
    )(
        coefficients.T,
        destinations.T,
        jnp.transpose(offsets, (1, 2, 0)),
        basis_rows,
        basis_cols,
        blocks,
        weight,
    )


def lines_kernel(dest_ref, off_ref, weight_ref, near_ref):
    rows = weight_ref.shape[0]
    near_ref[0:rows, :] = weight_ref[...]
    line = lax.broadcasted_iota(jnp.int32, (META, S), 0)
    lane = lax.broadcasted_iota(jnp.int32, (META, S), 1)
    words = jnp.zeros((META, S), jnp.int32)
    for block in range(rows // S):
        for n in range(2):
            for at, number in enumerate(places(dest_ref, off_ref, block, n)):
                words = jnp.where((line == n) & (lane == 8 * block + at), number, words)
    near_ref[rows : rows + META, :] = words.astype(jnp.float32).astype(jnp.bfloat16)


def with_lines(weight, destinations, offsets):
    smem = pl.BlockSpec(memory_space=pltpu.SMEM)
    vmem = pl.BlockSpec(memory_space=pltpu.VMEM)
    rows = weight.shape[0] * S
    return pl.pallas_call(
        lines_kernel,
        out_shape=jax.ShapeDtypeStruct((rows + META, S), jnp.bfloat16),
        in_specs=[smem, smem, vmem],
        out_specs=vmem,
        compiler_params=pltpu.CompilerParams(vmem_limit_bytes=60 * 2**20),
        cost_estimate=pl.CostEstimate(flops=2**16, bytes_accessed=2**22, transcendentals=0),
        name="lines",
    )(destinations.T, jnp.transpose(offsets, (1, 2, 0)), weight.reshape(rows, S))


def listed(codes, total, queue, idle):
    def one(i, found):
        code = codes(i)
        queue[found] = code
        return found + jnp.where(code >= 0, 1, 0)

    found = lax.fori_loop(0, total, one, jnp.int32(0), unroll=8)
    queue[found] = idle
    queue[found + 1] = idle
    return found


def add_pieces(queue, found, blocks, canvas):
    lane = lax.broadcasted_iota(jnp.int32, (S, LANES), 1)

    def pair(step, carry):
        values = []
        for part in range(2):
            code = queue[2 * step + part]
            shift = code & 127
            value = pltpu.roll(blocks((code >> 7) & 127).astype(jnp.float32), shift, 1)
            values.append((code >> 17, (code >> 14) & 7, value, lane >= shift))
        for row, tile, value, here in values:
            canvas[tile, pl.ds(row, S), :] += jnp.where(here, value, 0.0)
            canvas[tile + 1, pl.ds(row, S), :] += jnp.where(here, 0.0, value)
        return carry

    lax.fori_loop(0, (found + 1) // 2, pair, 0)


def whole_kernel(slots_ref, out_ref, canvas, told, codes, queue, sem):
    sources = slots_ref.shape[0]
    notes = slots_ref[:, 2 * S : 2 * S + META, :].astype(jnp.float32).astype(jnp.int32)[:, 0:8, :]
    notes = notes.reshape(sources * 8, S)
    at = [notes] + [pltpu.roll(notes, S - i, 1) for i in range(1, 5)]
    place = lax.broadcasted_iota(jnp.int32, notes.shape, 0)
    place = (place >> 3) * 2 + (place & 7)
    code = ((at[1] * LANES + at[2]) << 17) + (at[3] << 14) + (place << 7) + at[4]
    code = jnp.where(at[0] > 0, code, -1)[:, 0:1].reshape(sources, 8, 1)
    lane = lax.broadcasted_iota(jnp.int32, (sources, 8, S), 2)
    source = lax.broadcasted_iota(jnp.int32, (sources, 8, S), 0)
    told[...] = jnp.sum(jnp.where(lane == source, code, 0), axis=0)
    tell = pltpu.make_async_copy(told, codes, sem)
    tell.start()
    for tile in range(P_SIZE // LANES):
        canvas[tile] = jnp.zeros((P_SIZE, LANES), jnp.float32)
    tell.wait()
    found = listed(lambda i: codes[i & 1, i >> 1], 2 * sources, queue, (P_SIZE // LANES) << 14)

    def block(i):
        return slots_ref[i >> 1, pl.ds(pl.multiple_of((i & 1) * S, S), S), :]

    add_pieces(queue, found, block, canvas)
    for tile in range(P_SIZE // LANES):
        out_ref[:, tile * LANES : (tile + 1) * LANES] = canvas[tile].astype(jnp.bfloat16)


def place_whole(slots):
    sources = slots.shape[0]
    return pl.pallas_call(
        whole_kernel,
        out_shape=jax.ShapeDtypeStruct((P_SIZE, P_SIZE), jnp.bfloat16),
        in_specs=[pl.BlockSpec(memory_space=pltpu.VMEM)],
        out_specs=pl.BlockSpec(memory_space=pltpu.VMEM),
        scratch_shapes=[
            pltpu.VMEM((P_SIZE // LANES + 2, P_SIZE, LANES), jnp.float32),
            pltpu.VMEM((8, S), jnp.int32),
            pltpu.SMEM((8, S), jnp.int32),
            pltpu.SMEM((2 * sources + 2,), jnp.int32),
            pltpu.SemaphoreType.DMA,
        ],
        compiler_params=pltpu.CompilerParams(vmem_limit_bytes=8 * 2**20),
        cost_estimate=pl.CostEstimate(flops=2**23, bytes_accessed=16 * 2**20, transcendentals=0),
        name="place_whole",
    )(slots)


def halves_kernel(where_ref, parts_ref, out_ref, held, canvas, packed, told, codes, queue, sems):
    sources, count = held.shape[0], held.shape[1] // S
    patches = out_ref.shape[0]
    fetch = pltpu.make_async_copy(parts_ref, held, sems.at[patches])
    fetch.start()
    mine, core = where_ref[0], where_ref[1]
    for tile in (1, 2):
        canvas[tile] = jnp.zeros((patches * P_SIZE, LANES), jnp.float32)
    fetch.wait()
    notes = held[:, count * S : count * S + META, :].astype(jnp.float32).astype(jnp.int32)[:, 0:8, :]
    notes = notes.reshape(sources * 8, S)
    at = [notes] + [pltpu.roll(notes, S - i, 1) for i in range(1, 5)]
    place = lax.broadcasted_iota(jnp.int32, notes.shape, 0) >> 3
    place = place * count + (lax.broadcasted_iota(jnp.int32, notes.shape, 1) >> 3)
    tile = at[3] - 2 * core + 1
    row = (at[0] & 7) * P_SIZE + at[1] * LANES + at[2]
    code = (row << 17) + (tile << 14) + (place << 7) + at[4]
    code = jnp.where(((at[0] >> 3) == mine) & (tile >= 0) & (tile <= 2), code, -1)
    first = (lax.broadcasted_iota(jnp.int32, (8, S), 1) & 7) == 0
    words = jnp.zeros((8, S), jnp.int32)
    for i in range(sources):
        words += pltpu.roll(jnp.where(first, code[8 * i : 8 * i + 8, :], 0), i, 1)
    told[...] = words
    tell = pltpu.make_async_copy(told, codes, sems.at[patches + 1])
    tell.start()
    tell.wait()
    found = listed(lambda i: codes[i // S, lax.rem(i, S)], 2 * sources * count, queue, 3 << 14)

    def block(i):
        return held[lax.div(i, count), pl.ds(pl.multiple_of(lax.rem(i, count) * S, S), S), :]

    add_pieces(queue, found, block, canvas)
    copies = []
    for patch in range(patches):
        for half in range(2):
            rows = canvas[half + 1, patch * P_SIZE : (patch + 1) * P_SIZE, :]
            packed[patch, :, half * LANES : (half + 1) * LANES] = rows.astype(jnp.bfloat16)
        copies.append(pltpu.make_async_copy(packed.at[patch], out_ref.at[patch], sems.at[patch]))
        copies[-1].start()
    for copy in copies:
        copy.wait()


def place_halves(where, parts):
    sources, rows, patches = parts.shape[0], parts.shape[1], 8
    hbm = pl.BlockSpec(memory_space=pltpu.HBM)
    return pl.pallas_call(
        halves_kernel,
        out_shape=jax.ShapeDtypeStruct((patches, P_SIZE, 2 * LANES), jnp.bfloat16),
        in_specs=[pl.BlockSpec(memory_space=pltpu.SMEM), hbm],
        out_specs=hbm,
        scratch_shapes=[
            pltpu.VMEM((sources, rows, S), jnp.bfloat16),
            pltpu.VMEM((5, patches * P_SIZE, LANES), jnp.float32),
            pltpu.VMEM((patches, P_SIZE, 2 * LANES), jnp.bfloat16),
            pltpu.VMEM((8, S), jnp.int32),
            pltpu.SMEM((8, S), jnp.int32),
            pltpu.SMEM((2 * sources * (rows // S) + 2,), jnp.int32),
            pltpu.SemaphoreType.DMA((patches + 2,)),
        ],
        compiler_params=pltpu.CompilerParams(vmem_limit_bytes=60 * 2**20),
        cost_estimate=pl.CostEstimate(flops=2**24, bytes_accessed=24 * 2**20, transcendentals=0),
        name="place_halves",
    )(where, parts)


def body(blocks, inv_variance, destinations, offsets, coefficients, basis_rows, basis_cols):
    owners = lax.axis_size("x") * lax.axis_size("z")
    where = jnp.stack([lax.axis_index("x"), lax.axis_index("core")]).astype(jnp.int32)
    weight = inv_variance[0]

    near = lax.all_gather(with_lines(weight, destinations[0], offsets[0]), ("core", "x"))
    den = lax.psum_scatter(place_halves(where, near), "z", scatter_dimension=0, tiled=True)
    den = lax.all_to_all(den.reshape(16, BAND, 2 * LANES), ("y", "core"), 0, 0, tiled=True)

    slots = match(blocks[0], weight, destinations[0], offsets[0], coefficients[0], basis_rows, basis_cols, owners)
    slots = lax.all_to_all(slots, ("x", "z"), 0, 0, tiled=True)
    num = place_whole(slots).reshape(16, BAND, P_SIZE)
    num = lax.all_to_all(num, ("y", "core"), 0, 0, tiled=True)

    num = jnp.sum(num.astype(jnp.float32), axis=0)
    den = jnp.sum(den.reshape(8, 2, BAND, 2 * LANES).astype(jnp.float32), axis=0)
    den = jnp.concatenate([den[0], den[1]], axis=-1)
    return (num / jnp.maximum(den, 1.0))[None]


def solution(mesh):
    visits = mesh.shape["visit"]
    grid = Mesh(mesh.devices.reshape(visits // 2, 2, 4, mesh.shape["patch"] // 4), ("y", "core", "x", "z"))
    visit, patch = ("y", "core"), ("x", "z")
    return jax.shard_map(
        body,
        mesh=grid,
        in_specs=(
            P(visit, patch, None, None),
            P(visit, patch, None, None),
            P(visit, patch, None),
            P(visit, patch, None, None),
            P(visit, patch, None),
            P(),
            P(),
        ),
        out_specs=P(patch, visit, None),
        check_vma=False,
    )
```

```python
import functools

import jax
import jax.numpy as jnp
from jax import lax
from jax.experimental import pallas as pl
from jax.experimental.pallas import tpu as pltpu
from jax.sharding import Mesh
from jax.sharding import PartitionSpec as P

S = 128
P_SIZE = 512
TAPS = 41
HALF = (TAPS - 1) // 2
BASIS = 5
BAND = 32
LANES = 128
META = 16
LEAD = 4
GROUP = 4


def places(dest_ref, off_ref, block, n):
    row, col = off_ref[n, 0, block], off_ref[n, 1, block]
    return dest_ref[n, block], row // LANES, lax.rem(row, LANES), col // LANES, lax.rem(col, LANES)


def match_kernel(
    coef_ref, dest_ref, off_ref, rows_ref, cols_ref, blocks_ref, weight_ref, out_ref, wide, rows_tab, cols_tab, stack, taken
):
    count = blocks_ref.shape[0]
    line = lax.broadcasted_iota(jnp.int32, (META, S), 0)
    lane = lax.broadcasted_iota(jnp.int32, (META, S), 1)
    row_id = lax.broadcasted_iota(jnp.int32, (S, S), 0)
    col_id = lax.broadcasted_iota(jnp.int32, (S, S), 1)
    inside = jnp.abs(row_id - col_id) <= HALF
    wide[...] = jnp.zeros_like(wide)
    wide[0:BASIS, LEAD : LEAD + TAPS] = rows_ref[...].astype(jnp.float32)
    wide[8 : 8 + BASIS, LEAD : LEAD + TAPS] = cols_ref[...].astype(jnp.float32)
    for which in range(2):
        for k in range(BASIS):
            taps = jnp.broadcast_to(wide[which * 8 + k : which * 8 + k + 1, :], (8, S))
            band = jnp.concatenate(
                [pltpu.roll(taps, (S - HALF - LEAD + row) % S, 1, stride=1, stride_axis=0) for row in range(0, S, 8)]
            )
            band = jnp.where(inside, band, 0.0).astype(jnp.bfloat16)
            if which:
                cols_tab[:, k * S : (k + 1) * S] = band
            else:
                rows_tab[k * S : (k + 1) * S, :] = band
    y = (lax.broadcasted_iota(jnp.int32, (S, 1), 0).astype(jnp.float32) - (S - 1) / 2.0) / S
    x = (lax.broadcasted_iota(jnp.int32, (1, S), 1).astype(jnp.float32) - (S - 1) / 2.0) / S

    def clear(patch, carry):
        taken[patch] = 0
        out_ref[patch, 2 * S : 2 * S + META, :] = jnp.zeros((META, S), jnp.bfloat16)
        return carry

    lax.fori_loop(0, out_ref.shape[0], clear, 0)

    def some(step, carry):
        for part in range(GROUP):
            i = step * GROUP + part
            across = lax.dot_general(
                blocks_ref[i], rows_tab[...], (((1,), (1,)), ((), ())), preferred_element_type=jnp.float32
            )
            for k in range(BASIS):
                image = across[:, k * S : (k + 1) * S]
                plain = coef_ref[3 * k, i] + coef_ref[3 * k + 2, i] * x
                for at, value in ((0, image * plain), (S, image * coef_ref[3 * k + 1, i])):
                    upper = value.astype(jnp.bfloat16)
                    lower = (value - upper.astype(jnp.float32)).astype(jnp.bfloat16)
                    stack[part, k * S : (k + 1) * S, at : at + S] = upper
                    stack[part, k * S : (k + 1) * S, 2 * S + at : 3 * S + at] = lower
        for part in range(GROUP):
            i = step * GROUP + part
            sums = jnp.dot(cols_tab[...], stack[part], preferred_element_type=jnp.float32)
            sums = sums[:, 0 : 2 * S] + sums[:, 2 * S : 4 * S]
            weight = weight_ref[i].astype(jnp.float32)
            term = ((sums[:, 0:S] + y * sums[:, S : 2 * S]) * weight).astype(jnp.bfloat16)
            for n in range(2):
                patch, *numbers = places(dest_ref, off_ref, i, n)
                slot = taken[patch]
                taken[patch] = slot + 1
                out_ref[patch, pl.ds(pl.multiple_of(slot * S, S), S), :] = term
                notes = out_ref[patch, 2 * S : 2 * S + META, :].astype(jnp.float32).astype(jnp.int32)
                for at, number in enumerate([1] + numbers):
                    notes = jnp.where((line == slot) & (lane == at), number, notes)
                out_ref[patch, 2 * S : 2 * S + META, :] = notes.astype(jnp.float32).astype(jnp.bfloat16)
        return carry

    lax.fori_loop(0, count // GROUP, some, 0)


def match(blocks, weight, destinations, offsets, coefficients, basis_rows, basis_cols, owners):
    vmem = pl.BlockSpec(memory_space=pltpu.VMEM)
    smem = pl.BlockSpec(memory_space=pltpu.SMEM)
    return pl.pallas_call(
        match_kernel,
        out_shape=jax.ShapeDtypeStruct((owners, 2 * S + META, S), jnp.bfloat16),
        in_specs=[smem, smem, smem, vmem, vmem, vmem, vmem],
        out_specs=vmem,
        scratch_shapes=[
            pltpu.VMEM((16, S), jnp.float32),
            pltpu.VMEM((BASIS * S, S), jnp.bfloat16),
            pltpu.VMEM((S, BASIS * S), jnp.bfloat16),
            pltpu.VMEM((GROUP, BASIS * S, 4 * S), jnp.bfloat16),
            pltpu.SMEM((owners,), jnp.int32),
        ],
        compiler_params=pltpu.CompilerParams(vmem_limit_bytes=60 * 2**20),
        cost_estimate=pl.CostEstimate(flops=2**30, bytes_accessed=16 * 2**20, transcendentals=0),
        name="match",
    )(
        coefficients.T,
        destinations.T,
        jnp.transpose(offsets, (1, 2, 0)),
        basis_rows,
        basis_cols,
        blocks,
        weight,
    )


def lines_kernel(dest_ref, off_ref, out_ref):
    line = lax.broadcasted_iota(jnp.int32, (META, S), 0)
    lane = lax.broadcasted_iota(jnp.int32, (META, S), 1)
    words = jnp.zeros((META, S), jnp.int32)
    for block in range(dest_ref.shape[1]):
        for n in range(2):
            for at, number in enumerate(places(dest_ref, off_ref, block, n)):
                words = jnp.where((line == n) & (lane == 8 * block + at), number, words)
    words = words.astype(jnp.float32).astype(jnp.bfloat16)
    for taker in range(out_ref.shape[0]):
        out_ref[taker] = words


def lines_of(destinations, offsets, takers):
    smem = pl.BlockSpec(memory_space=pltpu.SMEM)
    return pl.pallas_call(
        lines_kernel,
        out_shape=jax.ShapeDtypeStruct((takers, META, S), jnp.bfloat16),
        in_specs=[smem, smem],
        out_specs=pl.BlockSpec(memory_space=pltpu.VMEM),
        compiler_params=pltpu.CompilerParams(vmem_limit_bytes=60 * 2**20),
        cost_estimate=pl.CostEstimate(flops=2**16, bytes_accessed=2**22, transcendentals=0),
        name="lines",
    )(destinations.T, jnp.transpose(offsets, (1, 2, 0)))


def held_kernel(large_ref, small_ref, out_ref):
    pass


def held_until(large, small):
    hbm = pl.BlockSpec(memory_space=pltpu.HBM)
    return pl.pallas_call(
        held_kernel,
        out_shape=jax.ShapeDtypeStruct(large.shape, large.dtype),
        in_specs=[hbm, hbm],
        out_specs=hbm,
        input_output_aliases={0: 0},
        compiler_params=pltpu.CompilerParams(vmem_limit_bytes=60 * 2**20),
        name="held_until",
    )(large, small)


def listed(codes, total, queue, idle):
    def one(i, found):
        code = codes(i)
        queue[found] = code
        return found + jnp.where(code >= 0, 1, 0)

    found = lax.fori_loop(0, total, one, jnp.int32(0), unroll=8)
    for after in range(4):
        queue[found + after] = idle
    return found


def add_pieces(queue, found, blocks, canvas):
    lane = lax.broadcasted_iota(jnp.int32, (S, LANES), 1)

    def some(step, carry):
        values = []
        for part in range(4):
            code = queue[4 * step + part]
            shift = code & 127
            value = pltpu.roll(blocks((code >> 7) & 127).astype(jnp.float32), shift, 1)
            values.append((code >> 17, (code >> 14) & 7, value, lane >= shift))
        for row, tile, value, here in values:
            canvas[tile, pl.ds(row, S), :] += jnp.where(here, value, 0.0)
            canvas[tile + 1, pl.ds(row, S), :] += jnp.where(here, 0.0, value)
        return carry

    lax.fori_loop(0, (found + 3) // 4, some, 0)


def whole_kernel(slots_ref, out_ref, canvas, told, codes, queue, sem):
    sources = slots_ref.shape[0]
    notes = slots_ref[:, 2 * S : 2 * S + META, :].astype(jnp.float32).astype(jnp.int32)[:, 0:8, :]
    notes = notes.reshape(sources * 8, S)
    at = [notes] + [pltpu.roll(notes, S - i, 1) for i in range(1, 5)]
    place = lax.broadcasted_iota(jnp.int32, notes.shape, 0)
    place = (place >> 3) * 2 + (place & 7)
    code = ((at[1] * LANES + at[2]) << 17) + (at[3] << 14) + (place << 7) + at[4]
    code = jnp.where(at[0] > 0, code, -1)[:, 0:1].reshape(sources, 8, 1)
    lane = lax.broadcasted_iota(jnp.int32, (sources, 8, S), 2)
    source = lax.broadcasted_iota(jnp.int32, (sources, 8, S), 0)
    told[...] = jnp.sum(jnp.where(lane == source, code, 0), axis=0)
    tell = pltpu.make_async_copy(told, codes, sem)
    tell.start()
    for tile in range(P_SIZE // LANES):
        canvas[tile] = jnp.zeros((P_SIZE, LANES), jnp.float32)
    tell.wait()
    found = listed(lambda i: codes[i & 1, i >> 1], 2 * sources, queue, (P_SIZE // LANES) << 14)

    def block(i):
        return slots_ref[i >> 1, pl.ds(pl.multiple_of((i & 1) * S, S), S), :]

    add_pieces(queue, found, block, canvas)
    for tile in range(P_SIZE // LANES):
        out_ref[:, tile * LANES : (tile + 1) * LANES] = canvas[tile].astype(jnp.bfloat16)


def place_whole(slots):
    sources = slots.shape[0]
    return pl.pallas_call(
        whole_kernel,
        out_shape=jax.ShapeDtypeStruct((P_SIZE, P_SIZE), jnp.bfloat16),
        in_specs=[pl.BlockSpec(memory_space=pltpu.VMEM)],
        out_specs=pl.BlockSpec(memory_space=pltpu.VMEM),
        scratch_shapes=[
            pltpu.VMEM((P_SIZE // LANES + 2, P_SIZE, LANES), jnp.float32),
            pltpu.VMEM((8, S), jnp.int32),
            pltpu.SMEM((8, S), jnp.int32),
            pltpu.SMEM((2 * sources + 4,), jnp.int32),
            pltpu.SemaphoreType.DMA,
        ],
        compiler_params=pltpu.CompilerParams(vmem_limit_bytes=8 * 2**20),
        cost_estimate=pl.CostEstimate(flops=2**23, bytes_accessed=16 * 2**20, transcendentals=0),
        name="place_whole",
    )(slots)


def halves_kernel(where_ref, parts_ref, lines_ref, out_ref, held, canvas, packed, told, codes, queue, sems):
    sources, count = held.shape[0], held.shape[1] // S
    patches = out_ref.shape[0]
    fetch = pltpu.make_async_copy(parts_ref, held, sems.at[patches])
    fetch.start()
    mine, core = where_ref[0], where_ref[1]
    for tile in (1, 2):
        canvas[tile] = jnp.zeros((patches * P_SIZE, LANES), jnp.float32)
    notes = lines_ref[...].astype(jnp.float32).astype(jnp.int32)[:, 0:8, :]
    notes = notes.reshape(sources * 8, S)
    at = [notes] + [pltpu.roll(notes, S - i, 1) for i in range(1, 5)]
    place = lax.broadcasted_iota(jnp.int32, notes.shape, 0) >> 3
    place = place * count + (lax.broadcasted_iota(jnp.int32, notes.shape, 1) >> 3)
    tile = at[3] - 2 * core + 1
    row = (at[0] & 7) * P_SIZE + at[1] * LANES + at[2]
    code = (row << 17) + (tile << 14) + (place << 7) + at[4]
    code = jnp.where(((at[0] >> 3) == mine) & (tile >= 0) & (tile <= 2), code, -1)
    first = (lax.broadcasted_iota(jnp.int32, (8, S), 1) & 7) == 0
    words = jnp.zeros((8, S), jnp.int32)
    for i in range(sources):
        words += pltpu.roll(jnp.where(first, code[8 * i : 8 * i + 8, :], 0), i, 1)
    told[...] = words
    tell = pltpu.make_async_copy(told, codes, sems.at[patches + 1])
    tell.start()
    tell.wait()
    found = listed(lambda i: codes[i // S, lax.rem(i, S)], 2 * sources * count, queue, 3 << 14)
    fetch.wait()

    def block(i):
        return held[lax.div(i, count), pl.ds(pl.multiple_of(lax.rem(i, count) * S, S), S), :]

    add_pieces(queue, found, block, canvas)
    copies = []
    for patch in range(patches):
        for half in range(2):
            rows = canvas[half + 1, patch * P_SIZE : (patch + 1) * P_SIZE, :]
            packed[patch, :, half * LANES : (half + 1) * LANES] = rows.astype(jnp.bfloat16)
        copies.append(pltpu.make_async_copy(packed.at[patch], out_ref.at[patch], sems.at[patch]))
        copies[-1].start()
    for copy in copies:
        copy.wait()


def place_halves(where, parts, lines):
    sources, rows, patches = parts.shape[0], parts.shape[1], 8
    hbm = pl.BlockSpec(memory_space=pltpu.HBM)
    return pl.pallas_call(
        halves_kernel,
        out_shape=jax.ShapeDtypeStruct((patches, P_SIZE, 2 * LANES), jnp.bfloat16),
        in_specs=[pl.BlockSpec(memory_space=pltpu.SMEM), hbm, pl.BlockSpec(memory_space=pltpu.VMEM)],
        out_specs=hbm,
        scratch_shapes=[
            pltpu.VMEM((sources, rows, S), jnp.bfloat16),
            pltpu.VMEM((5, patches * P_SIZE, LANES), jnp.float32),
            pltpu.VMEM((patches, P_SIZE, 2 * LANES), jnp.bfloat16),
            pltpu.VMEM((8, S), jnp.int32),
            pltpu.SMEM((8, S), jnp.int32),
            pltpu.SMEM((2 * sources * (rows // S) + 4,), jnp.int32),
            pltpu.SemaphoreType.DMA((patches + 2,)),
        ],
        compiler_params=pltpu.CompilerParams(vmem_limit_bytes=60 * 2**20),
        cost_estimate=pl.CostEstimate(flops=2**24, bytes_accessed=24 * 2**20, transcendentals=0),
        name="place_halves",
    )(where, parts, lines)


def body(blocks, inv_variance, destinations, offsets, coefficients, basis_rows, basis_cols):
    owners = lax.axis_size("x") * lax.axis_size("z")
    where = jnp.stack([lax.axis_index("x"), lax.axis_index("core")]).astype(jnp.int32)
    weight = inv_variance[0]

    near = lax.all_gather(weight.reshape(-1, S), ("core", "x"))
    lines = lines_of(destinations[0], offsets[0], near.shape[0])
    lines = lax.all_to_all(lines, ("core", "x"), 0, 0, tiled=True)
    den = lax.psum_scatter(place_halves(where, near, lines), "z", scatter_dimension=0, tiled=True)
    den = lax.all_to_all(den.reshape(16, BAND, 2 * LANES), ("y", "core"), 0, 0, tiled=True)

    slots = match(blocks[0], weight, destinations[0], offsets[0], coefficients[0], basis_rows, basis_cols, owners)
    slots = lax.all_to_all(held_until(slots, lines), ("x", "z"), 0, 0, tiled=True)
    num = place_whole(slots).reshape(16, BAND, P_SIZE)
    num = lax.all_to_all(num, ("y", "core"), 0, 0, tiled=True)

    num = jnp.sum(num.astype(jnp.float32), axis=0)
    den = jnp.sum(den.reshape(8, 2, BAND, 2 * LANES).astype(jnp.float32), axis=0)
    den = jnp.concatenate([den[0], den[1]], axis=-1)
    return (num / jnp.maximum(den, 1.0))[None]


def solution(mesh):
    visits = mesh.shape["visit"]
    grid = Mesh(mesh.devices.reshape(visits // 2, 2, 4, mesh.shape["patch"] // 4), ("y", "core", "x", "z"))
    visit, patch = ("y", "core"), ("x", "z")
    return jax.shard_map(
        body,
        mesh=grid,
        in_specs=(
            P(visit, patch, None, None),
            P(visit, patch, None, None),
            P(visit, patch, None),
            P(visit, patch, None, None),
            P(visit, patch, None),
            P(),
            P(),
        ),
        out_specs=P(patch, visit, None),
        check_vma=False,
    )
```

```python
import functools

import jax
import jax.numpy as jnp
from jax import lax
from jax.experimental import pallas as pl
from jax.experimental.pallas import tpu as pltpu
from jax.sharding import Mesh
from jax.sharding import PartitionSpec as P

S = 128
P_SIZE = 512
TAPS = 41
HALF = (TAPS - 1) // 2
BASIS = 5
BAND = 32
LANES = 128
META = 16
LEAD = 4
GROUP = 4
MARGIN = 48
WINDOW = 48


def places(dest_ref, off_ref, block, n):
    row, col = off_ref[n, 0, block], off_ref[n, 1, block]
    return dest_ref[n, block], row // LANES, lax.rem(row, LANES), col // LANES, lax.rem(col, LANES)


def match_kernel(
    coef_ref, dest_ref, off_ref, rows_ref, cols_ref, blocks_ref, weight_ref, out_ref, wide, rows_tab, cols_tab, stack, taken
):
    count = blocks_ref.shape[0]
    line = lax.broadcasted_iota(jnp.int32, (META, S), 0)
    lane = lax.broadcasted_iota(jnp.int32, (META, S), 1)
    row_id = lax.broadcasted_iota(jnp.int32, (S, S), 0)
    col_id = lax.broadcasted_iota(jnp.int32, (S, S), 1)
    inside = jnp.abs(row_id - col_id) <= HALF
    wide[...] = jnp.zeros_like(wide)
    wide[0:BASIS, LEAD : LEAD + TAPS] = rows_ref[...].astype(jnp.float32)
    wide[8 : 8 + BASIS, LEAD : LEAD + TAPS] = cols_ref[...].astype(jnp.float32)
    for which in range(2):
        for k in range(BASIS):
            taps = jnp.broadcast_to(wide[which * 8 + k : which * 8 + k + 1, :], (8, S))
            band = jnp.concatenate(
                [pltpu.roll(taps, (S - HALF - LEAD + row) % S, 1, stride=1, stride_axis=0) for row in range(0, S, 8)]
            )
            band = jnp.where(inside, band, 0.0).astype(jnp.bfloat16)
            if which:
                cols_tab[:, k * S : (k + 1) * S] = band
            else:
                rows_tab[k * S : (k + 1) * S, :] = band
    y = (lax.broadcasted_iota(jnp.int32, (S, 1), 0).astype(jnp.float32) - (S - 1) / 2.0) / S
    x = (lax.broadcasted_iota(jnp.int32, (1, S), 1).astype(jnp.float32) - (S - 1) / 2.0) / S

    def clear(patch, carry):
        taken[patch] = 0
        out_ref[patch, 2 * S : 2 * S + META, :] = jnp.zeros((META, S), jnp.bfloat16)
        return carry

    lax.fori_loop(0, out_ref.shape[0], clear, 0)

    def some(step, carry):
        for part in range(GROUP):
            i = step * GROUP + part
            across = lax.dot_general(
                blocks_ref[i], rows_tab[...], (((1,), (1,)), ((), ())), preferred_element_type=jnp.float32
            )
            for k in range(BASIS):
                image = across[:, k * S : (k + 1) * S]
                plain = coef_ref[3 * k, i] + coef_ref[3 * k + 2, i] * x
                for at, value in ((0, image * plain), (S, image * coef_ref[3 * k + 1, i])):
                    upper = value.astype(jnp.bfloat16)
                    lower = (value - upper.astype(jnp.float32)).astype(jnp.bfloat16)
                    stack[part, k * S : (k + 1) * S, at : at + S] = upper
                    stack[part, k * S : (k + 1) * S, 2 * S + at : 3 * S + at] = lower
        for part in range(GROUP):
            i = step * GROUP + part
            sums = jnp.dot(cols_tab[...], stack[part], preferred_element_type=jnp.float32)
            sums = sums[:, 0 : 2 * S] + sums[:, 2 * S : 4 * S]
            weight = weight_ref[i].astype(jnp.float32)
            term = ((sums[:, 0:S] + y * sums[:, S : 2 * S]) * weight).astype(jnp.bfloat16)
            for n in range(2):
                patch, *numbers = places(dest_ref, off_ref, i, n)
                slot = taken[patch]
                taken[patch] = slot + 1
                out_ref[patch, pl.ds(pl.multiple_of(slot * S, S), S), :] = term
                notes = out_ref[patch, 2 * S : 2 * S + META, :].astype(jnp.float32).astype(jnp.int32)
                for at, number in enumerate([1] + numbers):
                    notes = jnp.where((line == slot) & (lane == at), number, notes)
                out_ref[patch, 2 * S : 2 * S + META, :] = notes.astype(jnp.float32).astype(jnp.bfloat16)
        return carry

    lax.fori_loop(0, count // GROUP, some, 0)


def match(blocks, weight, destinations, offsets, coefficients, basis_rows, basis_cols, owners):
    vmem = pl.BlockSpec(memory_space=pltpu.VMEM)
    smem = pl.BlockSpec(memory_space=pltpu.SMEM)
    return pl.pallas_call(
        match_kernel,
        out_shape=jax.ShapeDtypeStruct((owners, 2 * S + META, S), jnp.bfloat16),
        in_specs=[smem, smem, smem, vmem, vmem, vmem, vmem],
        out_specs=vmem,
        scratch_shapes=[
            pltpu.VMEM((16, S), jnp.float32),
            pltpu.VMEM((BASIS * S, S), jnp.bfloat16),
            pltpu.VMEM((S, BASIS * S), jnp.bfloat16),
            pltpu.VMEM((GROUP, BASIS * S, 4 * S), jnp.bfloat16),
            pltpu.SMEM((owners,), jnp.int32),
        ],
        compiler_params=pltpu.CompilerParams(vmem_limit_bytes=60 * 2**20),
        cost_estimate=pl.CostEstimate(flops=2**30, bytes_accessed=16 * 2**20, transcendentals=0),
        name="match",
    )(
        coefficients.T,
        destinations.T,
        jnp.transpose(offsets, (1, 2, 0)),
        basis_rows,
        basis_cols,
        blocks,
        weight,
    )


def lines_kernel(dest_ref, off_ref, out_ref):
    line = lax.broadcasted_iota(jnp.int32, (META, S), 0)
    lane = lax.broadcasted_iota(jnp.int32, (META, S), 1)
    words = jnp.zeros((META, S), jnp.int32)
    for block in range(dest_ref.shape[1]):
        for n in range(2):
            for at, number in enumerate(places(dest_ref, off_ref, block, n)):
                words = jnp.where((line == n) & (lane == 8 * block + at), number, words)
    words = words.astype(jnp.float32).astype(jnp.bfloat16)
    for taker in range(out_ref.shape[0]):
        out_ref[taker] = words


def lines_of(destinations, offsets, takers):
    smem = pl.BlockSpec(memory_space=pltpu.SMEM)
    return pl.pallas_call(
        lines_kernel,
        out_shape=jax.ShapeDtypeStruct((takers, META, S), jnp.bfloat16),
        in_specs=[smem, smem],
        out_specs=pl.BlockSpec(memory_space=pltpu.VMEM),
        compiler_params=pltpu.CompilerParams(vmem_limit_bytes=60 * 2**20),
        cost_estimate=pl.CostEstimate(flops=2**16, bytes_accessed=2**22, transcendentals=0),
        name="lines",
    )(destinations.T, jnp.transpose(offsets, (1, 2, 0)))


def held_kernel(large_ref, small_ref, out_ref):
    pass


def held_until(large, small):
    hbm = pl.BlockSpec(memory_space=pltpu.HBM)
    return pl.pallas_call(
        held_kernel,
        out_shape=jax.ShapeDtypeStruct(large.shape, large.dtype),
        in_specs=[hbm, hbm],
        out_specs=hbm,
        input_output_aliases={0: 0},
        compiler_params=pltpu.CompilerParams(vmem_limit_bytes=60 * 2**20),
        name="held_until",
    )(large, small)


def listed(codes, total, queue, idle):
    def one(i, found):
        code = codes(i)
        queue[0, found] = code
        queue[1, found] = i
        return found + jnp.where(code >= 0, 1, 0)

    found = lax.fori_loop(0, total, one, jnp.int32(0), unroll=8)
    for after in range(4):
        queue[0, found + after] = idle
        queue[1, found + after] = 0
    return found


def add_pieces(queue, found, rows, piece, canvas):
    lane = lax.broadcasted_iota(jnp.int32, (rows, LANES), 1)

    def some(step, carry):
        values = []
        for part in range(4):
            code = queue[0, 4 * step + part]
            shift = code & 127
            value = piece(queue[1, 4 * step + part], ((code >> 7) & 7) * 16)
            value = pltpu.roll(value.astype(jnp.float32), shift, 1)
            values.append((code >> 13, (code >> 10) & 7, value, lane >= shift))
        for row, tile, value, here in values:
            canvas[tile, pl.ds(row, rows), :] += jnp.where(here, value, 0.0)
            canvas[tile + 1, pl.ds(row, rows), :] += jnp.where(here, 0.0, value)
        return carry

    lax.fori_loop(0, (found + 3) // 4, some, 0)


def whole_kernel(slots_ref, out_ref, canvas, told, codes, queue, sem):
    sources = slots_ref.shape[0]
    notes = slots_ref[:, 2 * S : 2 * S + META, :].astype(jnp.float32).astype(jnp.int32)[:, 0:8, :]
    notes = notes.reshape(sources * 8, S)
    at = [notes] + [pltpu.roll(notes, S - i, 1) for i in range(1, 5)]
    code = ((at[1] * LANES + at[2]) << 13) + (at[3] << 10) + at[4]
    code = jnp.where(at[0] > 0, code, -1)[:, 0:1].reshape(sources, 8, 1)
    lane = lax.broadcasted_iota(jnp.int32, (sources, 8, S), 2)
    source = lax.broadcasted_iota(jnp.int32, (sources, 8, S), 0)
    told[...] = jnp.sum(jnp.where(lane == source, code, 0), axis=0)
    tell = pltpu.make_async_copy(told, codes, sem)
    tell.start()
    for tile in range(P_SIZE // LANES):
        canvas[tile] = jnp.zeros((P_SIZE, LANES), jnp.float32)
    tell.wait()
    found = listed(lambda i: codes[i & 1, i >> 1], 2 * sources, queue, (P_SIZE // LANES) << 10)

    def piece(i, start):
        return slots_ref[i >> 1, pl.ds(pl.multiple_of((i & 1) * S, S), S), :]

    add_pieces(queue, found, S, piece, canvas)
    for tile in range(P_SIZE // LANES):
        out_ref[:, tile * LANES : (tile + 1) * LANES] = canvas[tile].astype(jnp.bfloat16)


def place_whole(slots):
    sources = slots.shape[0]
    return pl.pallas_call(
        whole_kernel,
        out_shape=jax.ShapeDtypeStruct((P_SIZE, P_SIZE), jnp.bfloat16),
        in_specs=[pl.BlockSpec(memory_space=pltpu.VMEM)],
        out_specs=pl.BlockSpec(memory_space=pltpu.VMEM),
        scratch_shapes=[
            pltpu.VMEM((P_SIZE // LANES + 2, P_SIZE, LANES), jnp.float32),
            pltpu.VMEM((8, S), jnp.int32),
            pltpu.SMEM((8, S), jnp.int32),
            pltpu.SMEM((2, 2 * sources + 4), jnp.int32),
            pltpu.SemaphoreType.DMA,
        ],
        compiler_params=pltpu.CompilerParams(vmem_limit_bytes=8 * 2**20),
        cost_estimate=pl.CostEstimate(flops=2**23, bytes_accessed=16 * 2**20, transcendentals=0),
        name="place_whole",
    )(slots)


def band_kernel(where_ref, parts_ref, lines_ref, out_ref, held, canvas, told, codes, queue, sems):
    sources, count = held.shape[0], held.shape[1] // S
    patches = out_ref.shape[0]
    fetch = pltpu.make_async_copy(parts_ref, held, sems.at[0])
    fetch.start()
    band = where_ref[0] * BAND
    for patch in range(patches):
        for tile in range(P_SIZE // LANES):
            canvas[tile, patch * S + MARGIN : patch * S + MARGIN + BAND, :] = jnp.zeros((BAND, LANES), jnp.float32)
    notes = lines_ref[...].astype(jnp.float32).astype(jnp.int32)[:, 0:8, :]
    notes = notes.reshape(sources * 8, S)
    at = [notes] + [pltpu.roll(notes, S - i, 1) for i in range(1, 5)]
    ahead = band - (at[1] * LANES + at[2])
    start = jnp.clip((ahead >> 4) << 4, 0, S - WINDOW)
    row = at[0] * S + MARGIN + start - ahead
    code = (row << 13) + (at[3] << 10) + ((start >> 4) << 7) + at[4]
    code = jnp.where((ahead > -BAND) & (ahead < S), code, -1)
    first = (lax.broadcasted_iota(jnp.int32, (8, S), 1) & 7) == 0
    for group in range(sources // 8):
        words = jnp.zeros((8, S), jnp.int32)
        for i in range(8):
            source = 8 * group + i
            words += pltpu.roll(jnp.where(first, code[8 * source : 8 * source + 8, :], 0), i, 1)
        told[group] = words
    tell = pltpu.make_async_copy(told, codes, sems.at[1])
    tell.start()
    tell.wait()
    idle = ((patches - 1) * S + MARGIN + BAND) << 13
    found = listed(lambda i: codes[i >> 8, (i >> 7) & 1, i & 127], 2 * sources * count, queue, idle)
    fetch.wait()

    def piece(i, start):
        begin = ((i & 127) >> 3) * S + start
        return held[(i >> 8) * 8 + (i & 7), pl.ds(pl.multiple_of(begin, 16), WINDOW), :]

    add_pieces(queue, found, WINDOW, piece, canvas)
    for patch in range(patches):
        for tile in range(P_SIZE // LANES):
            rows = canvas[tile, patch * S + MARGIN : patch * S + MARGIN + BAND, :]
            out_ref[patch, :, tile * LANES : (tile + 1) * LANES] = rows.astype(jnp.bfloat16)


def place_band(where, parts, lines, patches):
    sources, rows = parts.shape[0], parts.shape[1]
    vmem = pl.BlockSpec(memory_space=pltpu.VMEM)
    return pl.pallas_call(
        band_kernel,
        out_shape=jax.ShapeDtypeStruct((patches, BAND, P_SIZE), jnp.bfloat16),
        in_specs=[pl.BlockSpec(memory_space=pltpu.SMEM), pl.BlockSpec(memory_space=pltpu.HBM), vmem],
        out_specs=vmem,
        scratch_shapes=[
            pltpu.VMEM((sources, rows, S), jnp.bfloat16),
            pltpu.VMEM((P_SIZE // LANES + 1, patches * S, LANES), jnp.float32),
            pltpu.VMEM((sources // 8, 8, S), jnp.int32),
            pltpu.SMEM((sources // 8, 8, S), jnp.int32),
            pltpu.SMEM((2, 2 * sources * (rows // S) + 4), jnp.int32),
            pltpu.SemaphoreType.DMA((2,)),
        ],
        compiler_params=pltpu.CompilerParams(vmem_limit_bytes=60 * 2**20),
        cost_estimate=pl.CostEstimate(flops=2**24, bytes_accessed=24 * 2**20, transcendentals=0),
        name="place_band",
    )(where, parts, lines)


def body(blocks, inv_variance, destinations, offsets, coefficients, basis_rows, basis_cols):
    along = lax.axis_size("x")
    owners = along * lax.axis_size("z")
    where = lax.axis_index(("y", "core")).astype(jnp.int32).reshape(1)
    weight = inv_variance[0]

    near = lax.all_gather(weight.reshape(-1, S), ("y", "core"))
    lines = lines_of(destinations[0], offsets[0], near.shape[0])
    lines = lax.all_to_all(lines, ("y", "core"), 0, 0, tiled=True)
    den = place_band(where, near, lines, owners).reshape(along, owners // along, BAND, P_SIZE)
    den = lax.psum_scatter(den, "x", scatter_dimension=0, tiled=True)[0]
    den = lax.all_to_all(den, "z", 0, 0, tiled=True)

    slots = match(blocks[0], weight, destinations[0], offsets[0], coefficients[0], basis_rows, basis_cols, owners)
    slots = lax.all_to_all(held_until(slots, lines), ("x", "z"), 0, 0, tiled=True)
    num = place_whole(slots).reshape(16, BAND, P_SIZE)
    num = lax.all_to_all(num, ("y", "core"), 0, 0, tiled=True)

    num = jnp.sum(num.astype(jnp.float32), axis=0)
    den = jnp.sum(den.astype(jnp.float32), axis=0)
    return (num / jnp.maximum(den, 1.0))[None]


def solution(mesh):
    visits = mesh.shape["visit"]
    grid = Mesh(mesh.devices.reshape(visits // 2, 2, 4, mesh.shape["patch"] // 4), ("y", "core", "x", "z"))
    visit, patch = ("y", "core"), ("x", "z")
    return jax.shard_map(
        body,
        mesh=grid,
        in_specs=(
            P(visit, patch, None, None),
            P(visit, patch, None, None),
            P(visit, patch, None),
            P(visit, patch, None, None),
            P(visit, patch, None),
            P(),
            P(),
        ),
        out_specs=P(patch, visit, None),
        check_vma=False,
    )
```

```python
import functools

import jax
import jax.numpy as jnp
from jax import lax
from jax.experimental import pallas as pl
from jax.experimental.pallas import tpu as pltpu
from jax.sharding import Mesh
from jax.sharding import PartitionSpec as P

S = 128
P_SIZE = 512
TAPS = 41
HALF = (TAPS - 1) // 2
BASIS = 5
BAND = 32
LANES = 128
META = 16
LEAD = 4
GROUP = 4
MARGIN = 48
WINDOW = 48


def places(dest_ref, off_ref, block, n):
    row, col = off_ref[n, 0, block], off_ref[n, 1, block]
    return dest_ref[n, block], row // LANES, lax.rem(row, LANES), col // LANES, lax.rem(col, LANES)


def match_kernel(
    coef_ref, dest_ref, off_ref, rows_ref, cols_ref, blocks_ref, weight_ref, out_ref, wide, rows_tab, cols_tab, stack, taken
):
    count = blocks_ref.shape[0]
    line = lax.broadcasted_iota(jnp.int32, (META, S), 0)
    lane = lax.broadcasted_iota(jnp.int32, (META, S), 1)
    row_id = lax.broadcasted_iota(jnp.int32, (S, S), 0)
    col_id = lax.broadcasted_iota(jnp.int32, (S, S), 1)
    inside = jnp.abs(row_id - col_id) <= HALF
    wide[...] = jnp.zeros_like(wide)
    wide[0:BASIS, LEAD : LEAD + TAPS] = rows_ref[...].astype(jnp.float32)
    wide[8 : 8 + BASIS, LEAD : LEAD + TAPS] = cols_ref[...].astype(jnp.float32)
    for which in range(2):
        for k in range(BASIS):
            taps = jnp.broadcast_to(wide[which * 8 + k : which * 8 + k + 1, :], (8, S))
            band = jnp.concatenate(
                [pltpu.roll(taps, (S - HALF - LEAD + row) % S, 1, stride=1, stride_axis=0) for row in range(0, S, 8)]
            )
            band = jnp.where(inside, band, 0.0).astype(jnp.bfloat16)
            if which:
                cols_tab[:, k * S : (k + 1) * S] = band
            else:
                rows_tab[k * S : (k + 1) * S, :] = band
    y = (lax.broadcasted_iota(jnp.int32, (S, 1), 0).astype(jnp.float32) - (S - 1) / 2.0) / S
    x = (lax.broadcasted_iota(jnp.int32, (1, S), 1).astype(jnp.float32) - (S - 1) / 2.0) / S

    def clear(patch, carry):
        taken[patch] = 0
        out_ref[patch, 2 * S : 2 * S + META, :] = jnp.zeros((META, S), jnp.bfloat16)
        return carry

    lax.fori_loop(0, out_ref.shape[0], clear, 0)

    def some(step, carry):
        for part in range(GROUP):
            i = step * GROUP + part
            across = lax.dot_general(
                blocks_ref[i], rows_tab[...], (((1,), (1,)), ((), ())), preferred_element_type=jnp.float32
            )
            for k in range(BASIS):
                image = across[:, k * S : (k + 1) * S]
                plain = coef_ref[3 * k, 0, i] + coef_ref[3 * k + 2, 0, i] * x
                stack[part, k * S : (k + 1) * S, 0:S] = (image * plain).astype(jnp.bfloat16)
                stack[part, k * S : (k + 1) * S, S : 2 * S] = (image * coef_ref[3 * k + 1, 0, i]).astype(jnp.bfloat16)
        for part in range(GROUP):
            i = step * GROUP + part
            sums = jnp.dot(cols_tab[...], stack[part], preferred_element_type=jnp.float32)
            weight = weight_ref[i].astype(jnp.float32)
            term = ((sums[:, 0:S] + y * sums[:, S : 2 * S]) * weight).astype(jnp.bfloat16)
            for n in range(2):
                patch, *numbers = places(dest_ref, off_ref, i, n)
                slot = taken[patch]
                taken[patch] = slot + 1
                out_ref[patch, pl.ds(pl.multiple_of(slot * S, S), S), :] = term
                notes = out_ref[patch, 2 * S : 2 * S + META, :].astype(jnp.float32).astype(jnp.int32)
                for at, number in enumerate([1] + numbers):
                    notes = jnp.where((line == slot) & (lane == at), number, notes)
                out_ref[patch, 2 * S : 2 * S + META, :] = notes.astype(jnp.float32).astype(jnp.bfloat16)
        return carry

    lax.fori_loop(0, count // GROUP, some, 0)


def match(blocks, weight, destinations, offsets, coefficients, basis_rows, basis_cols, owners):
    vmem = pl.BlockSpec(memory_space=pltpu.VMEM)
    smem = pl.BlockSpec(memory_space=pltpu.SMEM)
    return pl.pallas_call(
        match_kernel,
        out_shape=jax.ShapeDtypeStruct((owners, 2 * S + META, S), jnp.bfloat16),
        in_specs=[smem, smem, smem, vmem, vmem, vmem, vmem],
        out_specs=vmem,
        scratch_shapes=[
            pltpu.VMEM((16, S), jnp.float32),
            pltpu.VMEM((BASIS * S, S), jnp.bfloat16),
            pltpu.VMEM((S, BASIS * S), jnp.bfloat16),
            pltpu.VMEM((GROUP, BASIS * S, 2 * S), jnp.bfloat16),
            pltpu.SMEM((owners,), jnp.int32),
        ],
        compiler_params=pltpu.CompilerParams(vmem_limit_bytes=60 * 2**20),
        cost_estimate=pl.CostEstimate(flops=2**30, bytes_accessed=16 * 2**20, transcendentals=0),
        name="match",
    )(
        jnp.transpose(coefficients, (2, 0, 1)),
        destinations.T,
        jnp.transpose(offsets, (1, 2, 0)),
        basis_rows,
        basis_cols,
        blocks,
        weight,
    )


def lines_kernel(dest_ref, off_ref, weight_ref, near_ref, told, sems):
    rows = weight_ref.shape[0]
    main = pltpu.make_async_copy(weight_ref, near_ref.at[pl.ds(0, rows)], sems.at[0])
    main.start()
    line = lax.broadcasted_iota(jnp.int32, (META, S), 0)
    lane = lax.broadcasted_iota(jnp.int32, (META, S), 1)
    words = jnp.zeros((META, S), jnp.int32)
    for block in range(rows // S):
        for n in range(2):
            for at, number in enumerate(places(dest_ref, off_ref, block, n)):
                words = jnp.where((line == n) & (lane == 8 * block + at), number, words)
    told[...] = words.astype(jnp.float32).astype(jnp.bfloat16)
    tail = pltpu.make_async_copy(told, near_ref.at[pl.ds(rows, META)], sems.at[1])
    tail.start()
    main.wait()
    tail.wait()


def with_lines(weight, destinations, offsets):
    smem = pl.BlockSpec(memory_space=pltpu.SMEM)
    hbm = pl.BlockSpec(memory_space=pltpu.HBM)
    rows = weight.shape[0] * S
    return pl.pallas_call(
        lines_kernel,
        out_shape=jax.ShapeDtypeStruct((rows + META, S), jnp.bfloat16),
        in_specs=[smem, smem, hbm],
        out_specs=hbm,
        scratch_shapes=[pltpu.VMEM((META, S), jnp.bfloat16), pltpu.SemaphoreType.DMA((2,))],
        compiler_params=pltpu.CompilerParams(vmem_limit_bytes=60 * 2**20),
        cost_estimate=pl.CostEstimate(flops=2**16, bytes_accessed=2**22, transcendentals=0),
        name="lines",
    )(destinations.T, jnp.transpose(offsets, (1, 2, 0)), weight.reshape(rows, S))


def listed(codes, total, queue, idle):
    def one(i, found):
        code = codes(i)
        queue[0, found] = code
        queue[1, found] = i
        return found + jnp.where(code >= 0, 1, 0)

    found = lax.fori_loop(0, total, one, jnp.int32(0), unroll=8)
    for after in range(4):
        queue[0, found + after] = idle
        queue[1, found + after] = 0
    return found


def add_pieces(queue, found, rows, piece, canvas):
    lane = lax.broadcasted_iota(jnp.int32, (rows, LANES), 1)

    def some(step, carry):
        values = []
        for part in range(4):
            code = queue[0, 4 * step + part]
            shift = code & 127
            value = piece(queue[1, 4 * step + part], ((code >> 7) & 7) * 16)
            value = pltpu.roll(value.astype(jnp.float32), shift, 1)
            values.append((code >> 13, (code >> 10) & 7, value, lane >= shift))
        for row, tile, value, here in values:
            canvas[tile, pl.ds(row, rows), :] += jnp.where(here, value, 0.0)
            canvas[tile + 1, pl.ds(row, rows), :] += jnp.where(here, 0.0, value)
        return carry

    lax.fori_loop(0, (found + 3) // 4, some, 0)


def whole_kernel(slots_ref, out_ref, canvas, told, codes, queue, sem):
    sources = slots_ref.shape[0]
    notes = slots_ref[:, 2 * S : 2 * S + META, :].astype(jnp.float32).astype(jnp.int32)[:, 0:8, :]
    notes = notes.reshape(sources * 8, S)
    at = [notes] + [pltpu.roll(notes, S - i, 1) for i in range(1, 5)]
    code = ((at[1] * LANES + at[2]) << 13) + (at[3] << 10) + at[4]
    code = jnp.where(at[0] > 0, code, -1)[:, 0:1].reshape(sources, 8, 1)
    lane = lax.broadcasted_iota(jnp.int32, (sources, 8, S), 2)
    source = lax.broadcasted_iota(jnp.int32, (sources, 8, S), 0)
    told[...] = jnp.sum(jnp.where(lane == source, code, 0), axis=0)
    tell = pltpu.make_async_copy(told, codes, sem)
    tell.start()
    for tile in range(P_SIZE // LANES):
        canvas[tile] = jnp.zeros((P_SIZE, LANES), jnp.float32)
    tell.wait()
    found = listed(lambda i: codes[i & 1, i >> 1], 2 * sources, queue, (P_SIZE // LANES) << 10)

    def piece(i, start):
        return slots_ref[i >> 1, pl.ds(pl.multiple_of((i & 1) * S, S), S), :]

    add_pieces(queue, found, S, piece, canvas)
    for tile in range(P_SIZE // LANES):
        out_ref[:, tile * LANES : (tile + 1) * LANES] = canvas[tile].astype(jnp.bfloat16)


def place_whole(slots):
    sources = slots.shape[0]
    return pl.pallas_call(
        whole_kernel,
        out_shape=jax.ShapeDtypeStruct((P_SIZE, P_SIZE), jnp.bfloat16),
        in_specs=[pl.BlockSpec(memory_space=pltpu.VMEM)],
        out_specs=pl.BlockSpec(memory_space=pltpu.VMEM),
        scratch_shapes=[
            pltpu.VMEM((P_SIZE // LANES + 2, P_SIZE, LANES), jnp.float32),
            pltpu.VMEM((8, S), jnp.int32),
            pltpu.SMEM((8, S), jnp.int32),
            pltpu.SMEM((2, 2 * sources + 4), jnp.int32),
            pltpu.SemaphoreType.DMA,
        ],
        compiler_params=pltpu.CompilerParams(vmem_limit_bytes=8 * 2**20),
        cost_estimate=pl.CostEstimate(flops=2**23, bytes_accessed=16 * 2**20, transcendentals=0),
        name="place_whole",
    )(slots)


def band_kernel(where_ref, parts_ref, out_ref, held, lines, canvas, told, codes, queue, sems):
    sources, rows = held.shape[0], held.shape[1]
    count, patches = rows // S, out_ref.shape[0]
    ask = pltpu.make_async_copy(parts_ref.at[:, pl.ds(rows, META)], lines, sems.at[2])
    ask.start()
    fetch = pltpu.make_async_copy(parts_ref.at[:, pl.ds(0, rows)], held, sems.at[0])
    fetch.start()
    band = where_ref[0] * BAND
    for patch in range(patches):
        for tile in range(P_SIZE // LANES):
            canvas[tile, patch * S + MARGIN : patch * S + MARGIN + BAND, :] = jnp.zeros((BAND, LANES), jnp.float32)
    ask.wait()
    notes = lines[...].astype(jnp.float32).astype(jnp.int32)[:, 0:8, :]
    notes = notes.reshape(sources * 8, S)
    at = [notes] + [pltpu.roll(notes, S - i, 1) for i in range(1, 5)]
    ahead = band - (at[1] * LANES + at[2])
    start = jnp.clip((ahead >> 4) << 4, 0, S - WINDOW)
    row = at[0] * S + MARGIN + start - ahead
    code = (row << 13) + (at[3] << 10) + ((start >> 4) << 7) + at[4]
    code = jnp.where((ahead > -BAND) & (ahead < S), code, -1)
    first = (lax.broadcasted_iota(jnp.int32, (8, S), 1) & 7) == 0
    for group in range(sources // 8):
        words = jnp.zeros((8, S), jnp.int32)
        for i in range(8):
            source = 8 * group + i
            words += pltpu.roll(jnp.where(first, code[8 * source : 8 * source + 8, :], 0), i, 1)
        told[group] = words
    tell = pltpu.make_async_copy(told, codes, sems.at[1])
    tell.start()
    tell.wait()
    idle = ((patches - 1) * S + MARGIN + BAND) << 13
    found = listed(lambda i: codes[i >> 8, (i >> 7) & 1, i & 127], 2 * sources * count, queue, idle)
    fetch.wait()

    def piece(i, start):
        begin = ((i & 127) >> 3) * S + start
        return held[(i >> 8) * 8 + (i & 7), pl.ds(pl.multiple_of(begin, 16), WINDOW), :]

    add_pieces(queue, found, WINDOW, piece, canvas)
    for patch in range(patches):
        for tile in range(P_SIZE // LANES):
            rows = canvas[tile, patch * S + MARGIN : patch * S + MARGIN + BAND, :]
            out_ref[patch, :, tile * LANES : (tile + 1) * LANES] = rows.astype(jnp.bfloat16)


def place_band(where, parts, patches):
    sources, rows = parts.shape[0], parts.shape[1] - META
    return pl.pallas_call(
        band_kernel,
        out_shape=jax.ShapeDtypeStruct((patches, BAND, P_SIZE), jnp.bfloat16),
        in_specs=[pl.BlockSpec(memory_space=pltpu.SMEM), pl.BlockSpec(memory_space=pltpu.HBM)],
        out_specs=pl.BlockSpec(memory_space=pltpu.VMEM),
        scratch_shapes=[
            pltpu.VMEM((sources, rows, S), jnp.bfloat16),
            pltpu.VMEM((sources, META, S), jnp.bfloat16),
            pltpu.VMEM((P_SIZE // LANES + 1, patches * S, LANES), jnp.float32),
            pltpu.VMEM((sources // 8, 8, S), jnp.int32),
            pltpu.SMEM((sources // 8, 8, S), jnp.int32),
            pltpu.SMEM((2, 2 * sources * (rows // S) + 4), jnp.int32),
            pltpu.SemaphoreType.DMA((3,)),
        ],
        compiler_params=pltpu.CompilerParams(vmem_limit_bytes=60 * 2**20),
        cost_estimate=pl.CostEstimate(flops=2**24, bytes_accessed=24 * 2**20, transcendentals=0),
        name="place_band",
    )(where, parts)


def body(blocks, inv_variance, destinations, offsets, coefficients, basis_rows, basis_cols):
    along = lax.axis_size("x")
    owners = along * lax.axis_size("z")
    where = lax.axis_index(("y", "core")).astype(jnp.int32).reshape(1)
    weight = inv_variance[0]

    near = lax.all_gather(with_lines(weight, destinations[0], offsets[0]), ("y", "core"))
    den = place_band(where, near, owners).reshape(along, owners // along, BAND, P_SIZE)
    den = lax.psum_scatter(den, "x", scatter_dimension=0, tiled=True)[0]
    den = lax.all_to_all(den, "z", 0, 0, tiled=True)

    slots = match(blocks[0], weight, destinations[0], offsets[0], coefficients, basis_rows, basis_cols, owners)
    slots = lax.all_to_all(slots, ("x", "z"), 0, 0, tiled=True)
    num = place_whole(slots).reshape(16, BAND, P_SIZE)
    num = lax.all_to_all(num, ("y", "core"), 0, 0, tiled=True)

    num = jnp.sum(num.astype(jnp.float32), axis=0)
    den = jnp.sum(den.astype(jnp.float32), axis=0)
    return (num / jnp.maximum(den, 1.0))[None]


def solution(mesh):
    visits = mesh.shape["visit"]
    grid = Mesh(mesh.devices.reshape(visits // 2, 2, 4, mesh.shape["patch"] // 4), ("y", "core", "x", "z"))
    visit, patch = ("y", "core"), ("x", "z")
    return jax.shard_map(
        body,
        mesh=grid,
        in_specs=(
            P(visit, patch, None, None),
            P(visit, patch, None, None),
            P(visit, patch, None),
            P(visit, patch, None, None),
            P(visit, patch, None),
            P(),
            P(),
        ),
        out_specs=P(patch, visit, None),
        check_vma=False,
    )
```

```python
import functools

import jax
import jax.numpy as jnp
from jax import lax
from jax.experimental import pallas as pl
from jax.experimental.pallas import tpu as pltpu
from jax.sharding import Mesh
from jax.sharding import PartitionSpec as P

S = 128
P_SIZE = 512
TAPS = 41
HALF = (TAPS - 1) // 2
BASIS = 5
BAND = 32
LANES = 128
META = 16
LEAD = 4
GROUP = 4
MARGIN = 48
WINDOW = 48


def places(dest_ref, off_ref, block, n):
    row, col = off_ref[n, 0, block], off_ref[n, 1, block]
    return dest_ref[n, block], row // LANES, lax.rem(row, LANES), col // LANES, lax.rem(col, LANES)


def match_kernel(
    coef_ref, dest_ref, off_ref, rows_ref, cols_ref, blocks_ref, weight_ref, out_ref, wide, rows_tab, cols_tab, stack, taken
):
    count = blocks_ref.shape[0]
    line = lax.broadcasted_iota(jnp.int32, (META, S), 0)
    lane = lax.broadcasted_iota(jnp.int32, (META, S), 1)
    row_id = lax.broadcasted_iota(jnp.int32, (S, S), 0)
    col_id = lax.broadcasted_iota(jnp.int32, (S, S), 1)
    inside = jnp.abs(row_id - col_id) <= HALF
    wide[...] = jnp.zeros_like(wide)
    wide[0:BASIS, LEAD : LEAD + TAPS] = rows_ref[...].astype(jnp.float32)
    wide[8 : 8 + BASIS, LEAD : LEAD + TAPS] = cols_ref[...].astype(jnp.float32)
    for which in range(2):
        for k in range(BASIS):
            taps = jnp.broadcast_to(wide[which * 8 + k : which * 8 + k + 1, :], (8, S))
            band = jnp.concatenate(
                [pltpu.roll(taps, (S - HALF - LEAD + row) % S, 1, stride=1, stride_axis=0) for row in range(0, S, 8)]
            )
            band = jnp.where(inside, band, 0.0).astype(jnp.bfloat16)
            if which:
                cols_tab[:, k * S : (k + 1) * S] = band
            else:
                rows_tab[k * S : (k + 1) * S, :] = band
    y = (lax.broadcasted_iota(jnp.int32, (S, 1), 0).astype(jnp.float32) - (S - 1) / 2.0) / S
    x = (lax.broadcasted_iota(jnp.int32, (1, S), 1).astype(jnp.float32) - (S - 1) / 2.0) / S

    def clear(patch, carry):
        taken[patch] = 0
        out_ref[patch, 2 * S : 2 * S + META, :] = jnp.zeros((META, S), jnp.bfloat16)
        return carry

    lax.fori_loop(0, out_ref.shape[0], clear, 0)

    def some(step, carry):
        for part in range(GROUP):
            i = step * GROUP + part
            across = lax.dot_general(
                blocks_ref[i], rows_tab[...], (((1,), (1,)), ((), ())), preferred_element_type=jnp.float32
            )
            for k in range(BASIS):
                image = across[:, k * S : (k + 1) * S]
                plain = coef_ref[3 * k, 0, i] + coef_ref[3 * k + 2, 0, i] * x
                stack[part, k * S : (k + 1) * S, 0:S] = (image * plain).astype(jnp.bfloat16)
                stack[part, k * S : (k + 1) * S, S : 2 * S] = (image * coef_ref[3 * k + 1, 0, i]).astype(jnp.bfloat16)
        for part in range(GROUP):
            i = step * GROUP + part
            sums = jnp.dot(cols_tab[...], stack[part], preferred_element_type=jnp.float32)
            weight = weight_ref[i].astype(jnp.float32)
            term = ((sums[:, 0:S] + y * sums[:, S : 2 * S]) * weight).astype(jnp.bfloat16)
            for n in range(2):
                patch, *numbers = places(dest_ref, off_ref, i, n)
                slot = taken[patch]
                taken[patch] = slot + 1
                out_ref[patch, pl.ds(pl.multiple_of(slot * S, S), S), :] = term
                notes = out_ref[patch, 2 * S : 2 * S + META, :].astype(jnp.float32).astype(jnp.int32)
                for at, number in enumerate([1] + numbers):
                    notes = jnp.where((line == slot) & (lane == at), number, notes)
                out_ref[patch, 2 * S : 2 * S + META, :] = notes.astype(jnp.float32).astype(jnp.bfloat16)
        return carry

    lax.fori_loop(0, count // GROUP, some, 0)


def match(blocks, weight, destinations, offsets, coefficients, basis_rows, basis_cols, owners):
    vmem = pl.BlockSpec(memory_space=pltpu.VMEM)
    smem = pl.BlockSpec(memory_space=pltpu.SMEM)
    return pl.pallas_call(
        match_kernel,
        out_shape=jax.ShapeDtypeStruct((owners, 2 * S + META, S), jnp.bfloat16),
        in_specs=[smem, smem, smem, vmem, vmem, vmem, vmem],
        out_specs=vmem,
        scratch_shapes=[
            pltpu.VMEM((16, S), jnp.float32),
            pltpu.VMEM((BASIS * S, S), jnp.bfloat16),
            pltpu.VMEM((S, BASIS * S), jnp.bfloat16),
            pltpu.VMEM((GROUP, BASIS * S, 2 * S), jnp.bfloat16),
            pltpu.SMEM((owners,), jnp.int32),
        ],
        compiler_params=pltpu.CompilerParams(vmem_limit_bytes=60 * 2**20),
        cost_estimate=pl.CostEstimate(flops=2**30, bytes_accessed=16 * 2**20, transcendentals=0),
        name="match",
    )(
        jnp.transpose(coefficients, (2, 0, 1)),
        destinations.T,
        jnp.transpose(offsets, (1, 2, 0)),
        basis_rows,
        basis_cols,
        blocks,
        weight,
    )


def lines_kernel(dest_ref, off_ref, weight_ref, near_ref, held, sems):
    rows = weight_ref.shape[0]
    fetch = pltpu.make_async_copy(weight_ref, held.at[pl.ds(0, rows)], sems.at[0])
    fetch.start()
    line = lax.broadcasted_iota(jnp.int32, (META, S), 0)
    lane = lax.broadcasted_iota(jnp.int32, (META, S), 1)
    words = jnp.zeros((META, S), jnp.int32)
    for block in range(rows // S):
        for n in range(2):
            for at, number in enumerate(places(dest_ref, off_ref, block, n)):
                words = jnp.where((line == n) & (lane == 8 * block + at), number, words)
    held[rows : rows + META, :] = words.astype(jnp.float32).astype(jnp.bfloat16)
    fetch.wait()
    put = pltpu.make_async_copy(held, near_ref, sems.at[1])
    put.start()
    put.wait()


def with_lines(weight, destinations, offsets):
    smem = pl.BlockSpec(memory_space=pltpu.SMEM)
    hbm = pl.BlockSpec(memory_space=pltpu.HBM)
    rows = weight.shape[0] * S
    return pl.pallas_call(
        lines_kernel,
        out_shape=jax.ShapeDtypeStruct((rows + META, S), jnp.bfloat16),
        in_specs=[smem, smem, hbm],
        out_specs=hbm,
        scratch_shapes=[pltpu.VMEM((rows + META, S), jnp.bfloat16), pltpu.SemaphoreType.DMA((2,))],
        compiler_params=pltpu.CompilerParams(vmem_limit_bytes=60 * 2**20),
        cost_estimate=pl.CostEstimate(flops=2**16, bytes_accessed=2**22, transcendentals=0),
        name="lines",
    )(destinations.T, jnp.transpose(offsets, (1, 2, 0)), weight.reshape(rows, S))


def listed(codes, total, queue, idle):
    def one(i, found):
        code = codes(i)
        queue[0, found] = code
        queue[1, found] = i
        return found + jnp.where(code >= 0, 1, 0)

    found = lax.fori_loop(0, total, one, jnp.int32(0), unroll=8)
    for after in range(8):
        queue[0, found + after] = idle
        queue[1, found + after] = 0
    return found


def add_pieces(queue, found, many, rows, piece, canvas):
    lane = lax.broadcasted_iota(jnp.int32, (rows, LANES), 1)

    def some(step, carry):
        values = []
        for part in range(many):
            code = queue[0, many * step + part]
            shift = code & 127
            value = piece(queue[1, many * step + part], ((code >> 7) & 7) * 16)
            value = pltpu.roll(value.astype(jnp.float32), shift, 1)
            values.append((code >> 13, (code >> 10) & 7, value, lane >= shift))
        for row, tile, value, here in values:
            canvas[tile, pl.ds(row, rows), :] += jnp.where(here, value, 0.0)
            canvas[tile + 1, pl.ds(row, rows), :] += jnp.where(here, 0.0, value)
        return carry

    lax.fori_loop(0, (found + many - 1) // many, some, 0)


def whole_kernel(slots_ref, out_ref, canvas, told, codes, queue, sem):
    sources = slots_ref.shape[0]
    notes = slots_ref[:, 2 * S : 2 * S + META, :].astype(jnp.float32).astype(jnp.int32)[:, 0:8, :]
    notes = notes.reshape(sources * 8, S)
    at = [notes] + [pltpu.roll(notes, S - i, 1) for i in range(1, 5)]
    code = ((at[1] * LANES + at[2]) << 13) + (at[3] << 10) + at[4]
    code = jnp.where(at[0] > 0, code, -1)[:, 0:1].reshape(sources, 8, 1)
    lane = lax.broadcasted_iota(jnp.int32, (sources, 8, S), 2)
    source = lax.broadcasted_iota(jnp.int32, (sources, 8, S), 0)
    told[...] = jnp.sum(jnp.where(lane == source, code, 0), axis=0)
    tell = pltpu.make_async_copy(told, codes, sem)
    tell.start()
    for tile in range(P_SIZE // LANES):
        canvas[tile] = jnp.zeros((P_SIZE, LANES), jnp.float32)
    tell.wait()
    found = listed(lambda i: codes[i & 1, i >> 1], 2 * sources, queue, (P_SIZE // LANES) << 10)

    def piece(i, start):
        return slots_ref[i >> 1, pl.ds(pl.multiple_of((i & 1) * S, S), S), :]

    add_pieces(queue, found, 4, S, piece, canvas)
    for tile in range(P_SIZE // LANES):
        out_ref[:, tile * LANES : (tile + 1) * LANES] = canvas[tile].astype(jnp.bfloat16)


def place_whole(slots):
    sources = slots.shape[0]
    return pl.pallas_call(
        whole_kernel,
        out_shape=jax.ShapeDtypeStruct((P_SIZE, P_SIZE), jnp.bfloat16),
        in_specs=[pl.BlockSpec(memory_space=pltpu.VMEM)],
        out_specs=pl.BlockSpec(memory_space=pltpu.VMEM),
        scratch_shapes=[
            pltpu.VMEM((P_SIZE // LANES + 2, P_SIZE, LANES), jnp.float32),
            pltpu.VMEM((8, S), jnp.int32),
            pltpu.SMEM((8, S), jnp.int32),
            pltpu.SMEM((2, 2 * sources + 8), jnp.int32),
            pltpu.SemaphoreType.DMA,
        ],
        compiler_params=pltpu.CompilerParams(vmem_limit_bytes=8 * 2**20),
        cost_estimate=pl.CostEstimate(flops=2**23, bytes_accessed=16 * 2**20, transcendentals=0),
        name="place_whole",
    )(slots)


def band_kernel(where_ref, parts_ref, out_ref, held, lines, canvas, told, codes, queue, sems):
    sources, rows = held.shape[0], held.shape[1]
    count, patches = rows // S, out_ref.shape[0]
    ask = pltpu.make_async_copy(parts_ref.at[:, pl.ds(rows, META)], lines, sems.at[2])
    ask.start()
    fetch = pltpu.make_async_copy(parts_ref.at[:, pl.ds(0, rows)], held, sems.at[0])
    fetch.start()
    band = where_ref[0] * BAND
    for patch in range(patches):
        for tile in range(P_SIZE // LANES):
            canvas[tile, patch * S + MARGIN : patch * S + MARGIN + BAND, :] = jnp.zeros((BAND, LANES), jnp.float32)
    ask.wait()
    notes = lines[...].astype(jnp.float32).astype(jnp.int32)[:, 0:8, :]
    notes = notes.reshape(sources * 8, S)
    at = [notes] + [pltpu.roll(notes, S - i, 1) for i in range(1, 5)]
    ahead = band - (at[1] * LANES + at[2])
    start = jnp.clip((ahead >> 4) << 4, 0, S - WINDOW)
    row = at[0] * S + MARGIN + start - ahead
    code = (row << 13) + (at[3] << 10) + ((start >> 4) << 7) + at[4]
    code = jnp.where((ahead > -BAND) & (ahead < S), code, -1)
    first = (lax.broadcasted_iota(jnp.int32, (8, S), 1) & 7) == 0
    for group in range(sources // 8):
        words = jnp.zeros((8, S), jnp.int32)
        for i in range(8):
            source = 8 * group + i
            words += pltpu.roll(jnp.where(first, code[8 * source : 8 * source + 8, :], 0), i, 1)
        told[group] = words
    tell = pltpu.make_async_copy(told, codes, sems.at[1])
    tell.start()
    tell.wait()
    idle = ((patches - 1) * S + MARGIN + BAND) << 13
    found = listed(lambda i: codes[i >> 8, (i >> 7) & 1, i & 127], 2 * sources * count, queue, idle)
    fetch.wait()

    def piece(i, start):
        begin = ((i & 127) >> 3) * S + start
        return held[(i >> 8) * 8 + (i & 7), pl.ds(pl.multiple_of(begin, 16), WINDOW), :]

    add_pieces(queue, found, 8, WINDOW, piece, canvas)
    for patch in range(patches):
        for tile in range(P_SIZE // LANES):
            rows = canvas[tile, patch * S + MARGIN : patch * S + MARGIN + BAND, :]
            out_ref[patch, :, tile * LANES : (tile + 1) * LANES] = rows.astype(jnp.bfloat16)


def place_band(where, parts, patches):
    sources, rows = parts.shape[0], parts.shape[1] - META
    return pl.pallas_call(
        band_kernel,
        out_shape=jax.ShapeDtypeStruct((patches, BAND, P_SIZE), jnp.bfloat16),
        in_specs=[pl.BlockSpec(memory_space=pltpu.SMEM), pl.BlockSpec(memory_space=pltpu.HBM)],
        out_specs=pl.BlockSpec(memory_space=pltpu.VMEM),
        scratch_shapes=[
            pltpu.VMEM((sources, rows, S), jnp.bfloat16),
            pltpu.VMEM((sources, META, S), jnp.bfloat16),
            pltpu.VMEM((P_SIZE // LANES + 1, patches * S, LANES), jnp.float32),
            pltpu.VMEM((sources // 8, 8, S), jnp.int32),
            pltpu.SMEM((sources // 8, 8, S), jnp.int32),
            pltpu.SMEM((2, 2 * sources * (rows // S) + 8), jnp.int32),
            pltpu.SemaphoreType.DMA((3,)),
        ],
        compiler_params=pltpu.CompilerParams(vmem_limit_bytes=60 * 2**20),
        cost_estimate=pl.CostEstimate(flops=2**24, bytes_accessed=24 * 2**20, transcendentals=0),
        name="place_band",
    )(where, parts)


def body(blocks, inv_variance, destinations, offsets, coefficients, basis_rows, basis_cols):
    along = lax.axis_size("x")
    owners = along * lax.axis_size("z")
    where = lax.axis_index(("y", "core")).astype(jnp.int32).reshape(1)
    weight = inv_variance[0]

    near = lax.all_gather(with_lines(weight, destinations[0], offsets[0]), ("y", "core"))
    den = place_band(where, near, owners).reshape(along, owners // along, BAND, P_SIZE)
    den = lax.psum_scatter(den, "x", scatter_dimension=0, tiled=True)[0]
    den = lax.all_to_all(den, "z", 0, 0, tiled=True)

    slots = match(blocks[0], weight, destinations[0], offsets[0], coefficients, basis_rows, basis_cols, owners)
    slots = lax.all_to_all(slots, ("x", "z"), 0, 0, tiled=True)
    num = place_whole(slots).reshape(16, BAND, P_SIZE)
    num = lax.all_to_all(num, ("y", "core"), 0, 0, tiled=True)

    num = jnp.sum(num.astype(jnp.float32), axis=0)
    den = jnp.sum(den.astype(jnp.float32), axis=0)
    return (num / jnp.maximum(den, 1.0))[None]


def solution(mesh):
    visits = mesh.shape["visit"]
    grid = Mesh(mesh.devices.reshape(visits // 2, 2, 4, mesh.shape["patch"] // 4), ("y", "core", "x", "z"))
    visit, patch = ("y", "core"), ("x", "z")
    return jax.shard_map(
        body,
        mesh=grid,
        in_specs=(
            P(visit, patch, None, None),
            P(visit, patch, None, None),
            P(visit, patch, None),
            P(visit, patch, None, None),
            P(visit, patch, None),
            P(),
            P(),
        ),
        out_specs=P(patch, visit, None),
        check_vma=False,
    )
```

```python
import functools

import jax
import jax.numpy as jnp
from jax import lax
from jax.experimental import pallas as pl
from jax.experimental.pallas import tpu as pltpu
from jax.sharding import Mesh
from jax.sharding import PartitionSpec as P

S = 128
P_SIZE = 512
TAPS = 41
HALF = (TAPS - 1) // 2
BASIS = 5
BAND = 32
LANES = 128
META = 16
LEAD = 4
GROUP = 4
MARGIN = 48
WINDOW = 48


def places(dest_ref, off_ref, block, n):
    row, col = off_ref[n, 0, block], off_ref[n, 1, block]
    return dest_ref[n, block], row // LANES, lax.rem(row, LANES), col // LANES, lax.rem(col, LANES)


def match_kernel(
    coef_ref, dest_ref, off_ref, rows_ref, cols_ref, blocks_ref, weight_ref, out_ref, wide, rows_tab, cols_tab, stack, taken
):
    count = blocks_ref.shape[0]
    line = lax.broadcasted_iota(jnp.int32, (META, S), 0)
    lane = lax.broadcasted_iota(jnp.int32, (META, S), 1)
    row_id = lax.broadcasted_iota(jnp.int32, (S, S), 0)
    col_id = lax.broadcasted_iota(jnp.int32, (S, S), 1)
    inside = jnp.abs(row_id - col_id) <= HALF
    wide[...] = jnp.zeros_like(wide)
    wide[0:BASIS, LEAD : LEAD + TAPS] = rows_ref[...].astype(jnp.float32)
    wide[8 : 8 + BASIS, LEAD : LEAD + TAPS] = cols_ref[...].astype(jnp.float32)
    for which in range(2):
        for k in range(BASIS):
            taps = jnp.broadcast_to(wide[which * 8 + k : which * 8 + k + 1, :], (8, S))
            band = jnp.concatenate(
                [pltpu.roll(taps, (S - HALF - LEAD + row) % S, 1, stride=1, stride_axis=0) for row in range(0, S, 8)]
            )
            band = jnp.where(inside, band, 0.0).astype(jnp.bfloat16)
            if which:
                cols_tab[:, k * S : (k + 1) * S] = band
            else:
                rows_tab[k * S : (k + 1) * S, :] = band
    y = (lax.broadcasted_iota(jnp.int32, (S, 1), 0).astype(jnp.float32) - (S - 1) / 2.0) / S
    x = (lax.broadcasted_iota(jnp.int32, (1, S), 1).astype(jnp.float32) - (S - 1) / 2.0) / S

    def clear(patch, carry):
        taken[patch] = 0
        out_ref[patch, 2 * S : 2 * S + META, :] = jnp.zeros((META, S), jnp.bfloat16)
        return carry

    lax.fori_loop(0, out_ref.shape[0], clear, 0)

    def some(step, carry):
        for part in range(GROUP):
            i = step * GROUP + part
            across = lax.dot_general(
                blocks_ref[i], rows_tab[...], (((1,), (1,)), ((), ())), preferred_element_type=jnp.float32
            )
            for k in range(BASIS):
                image = across[:, k * S : (k + 1) * S]
                plain = coef_ref[3 * k, 0, i] + coef_ref[3 * k + 2, 0, i] * x
                stack[part, k * S : (k + 1) * S, 0:S] = (image * plain).astype(jnp.bfloat16)
                stack[part, k * S : (k + 1) * S, S : 2 * S] = (image * coef_ref[3 * k + 1, 0, i]).astype(jnp.bfloat16)
        for part in range(GROUP):
            i = step * GROUP + part
            sums = jnp.dot(cols_tab[...], stack[part], preferred_element_type=jnp.float32)
            weight = weight_ref[i].astype(jnp.float32)
            term = ((sums[:, 0:S] + y * sums[:, S : 2 * S]) * weight).astype(jnp.bfloat16)
            for n in range(2):
                patch, *numbers = places(dest_ref, off_ref, i, n)
                slot = taken[patch]
                taken[patch] = slot + 1
                out_ref[patch, pl.ds(pl.multiple_of(slot * S, S), S), :] = term
                notes = out_ref[patch, 2 * S : 2 * S + META, :].astype(jnp.float32).astype(jnp.int32)
                for at, number in enumerate([1] + numbers):
                    notes = jnp.where((line == slot) & (lane == at), number, notes)
                out_ref[patch, 2 * S : 2 * S + META, :] = notes.astype(jnp.float32).astype(jnp.bfloat16)
        return carry

    lax.fori_loop(0, count // GROUP, some, 0)


def match(blocks, weight, destinations, offsets, coefficients, basis_rows, basis_cols, owners):
    vmem = pl.BlockSpec(memory_space=pltpu.VMEM)
    smem = pl.BlockSpec(memory_space=pltpu.SMEM)
    return pl.pallas_call(
        match_kernel,
        out_shape=jax.ShapeDtypeStruct((owners, 2 * S + META, S), jnp.bfloat16),
        in_specs=[smem, smem, smem, vmem, vmem, vmem, vmem],
        out_specs=vmem,
        scratch_shapes=[
            pltpu.VMEM((16, S), jnp.float32),
            pltpu.VMEM((BASIS * S, S), jnp.bfloat16),
            pltpu.VMEM((S, BASIS * S), jnp.bfloat16),
            pltpu.VMEM((GROUP, BASIS * S, 2 * S), jnp.bfloat16),
            pltpu.SMEM((owners,), jnp.int32),
        ],
        compiler_params=pltpu.CompilerParams(vmem_limit_bytes=60 * 2**20),
        cost_estimate=pl.CostEstimate(flops=2**30, bytes_accessed=16 * 2**20, transcendentals=0),
        name="match",
    )(
        jnp.transpose(coefficients, (2, 0, 1)),
        destinations.T,
        jnp.transpose(offsets, (1, 2, 0)),
        basis_rows,
        basis_cols,
        blocks,
        weight,
    )


def lines_kernel(dest_ref, off_ref, weight_ref, near_ref, held, sems):
    rows = weight_ref.shape[0]
    fetch = pltpu.make_async_copy(weight_ref, held.at[pl.ds(0, rows)], sems.at[0])
    fetch.start()
    line = lax.broadcasted_iota(jnp.int32, (META, S), 0)
    lane = lax.broadcasted_iota(jnp.int32, (META, S), 1)
    words = jnp.zeros((META, S), jnp.int32)
    for block in range(rows // S):
        for n in range(2):
            for at, number in enumerate(places(dest_ref, off_ref, block, n)):
                words = jnp.where((line == n) & (lane == 8 * block + at), number, words)
    held[rows : rows + META, :] = words.astype(jnp.float32).astype(jnp.bfloat16)
    fetch.wait()
    put = pltpu.make_async_copy(held, near_ref, sems.at[1])
    put.start()
    put.wait()


def with_lines(weight, destinations, offsets):
    smem = pl.BlockSpec(memory_space=pltpu.SMEM)
    hbm = pl.BlockSpec(memory_space=pltpu.HBM)
    rows = weight.shape[0] * S
    return pl.pallas_call(
        lines_kernel,
        out_shape=jax.ShapeDtypeStruct((rows + META, S), jnp.bfloat16),
        in_specs=[smem, smem, hbm],
        out_specs=hbm,
        scratch_shapes=[pltpu.VMEM((rows + META, S), jnp.bfloat16), pltpu.SemaphoreType.DMA((2,))],
        compiler_params=pltpu.CompilerParams(vmem_limit_bytes=60 * 2**20),
        cost_estimate=pl.CostEstimate(flops=2**16, bytes_accessed=2**22, transcendentals=0),
        name="lines",
    )(destinations.T, jnp.transpose(offsets, (1, 2, 0)), weight.reshape(rows, S))


def listed(code_of, first, total, queue, idle):
    def one(i, found):
        queue[found] = i
        return found + jnp.where(code_of(i) >= 0, 1, 0)

    found = lax.fori_loop(first, first + total, one, jnp.int32(0), unroll=16)
    for after in range(8):
        queue[found + after] = idle
    return found


def add_pieces(queue, found, code_of, many, rows, piece, canvas):
    lane = lax.broadcasted_iota(jnp.int32, (rows, LANES), 1)

    def some(step, carry):
        values = []
        for part in range(many):
            number = queue[many * step + part]
            code = code_of(number)
            shift = code & 127
            value = piece(number, ((code >> 7) & 7) * 16)
            value = pltpu.roll(value.astype(jnp.float32), shift, 1)
            values.append((code >> 13, (code >> 10) & 7, value, lane >= shift))
        for row, tile, value, here in values:
            canvas[tile, pl.ds(row, rows), :] += jnp.where(here, value, 0.0)
            canvas[tile + 1, pl.ds(row, rows), :] += jnp.where(here, 0.0, value)
        return carry

    lax.fori_loop(0, (found + many - 1) // many, some, 0)


def whole_kernel(slots_ref, out_ref, canvas, told, codes, queue, sem):
    sources = slots_ref.shape[0]
    notes = slots_ref[:, 2 * S : 2 * S + META, :].astype(jnp.float32).astype(jnp.int32)[:, 0:8, :]
    notes = notes.reshape(sources * 8, S)
    at = [notes] + [pltpu.roll(notes, S - i, 1) for i in range(1, 5)]
    code = ((at[1] * LANES + at[2]) << 13) + (at[3] << 10) + at[4]
    code = jnp.where(at[0] > 0, code, -1)[:, 0:1].reshape(sources, 8, 1)
    lane = lax.broadcasted_iota(jnp.int32, (sources, 8, S), 2)
    source = lax.broadcasted_iota(jnp.int32, (sources, 8, S), 0)
    told[...] = jnp.sum(jnp.where(lane == source, code, 0), axis=0)
    tell = pltpu.make_async_copy(told, codes, sem)
    tell.start()
    for tile in range(P_SIZE // LANES):
        canvas[tile] = jnp.zeros((P_SIZE, LANES), jnp.float32)
    tell.wait()
    codes[0, sources] = (P_SIZE // LANES) << 10

    def code_of(i):
        return codes[i & 1, i >> 1]

    found = listed(code_of, 0, 2 * sources, queue, 2 * sources)

    def piece(i, start):
        source = lax.rem(i >> 1, sources)
        return slots_ref[source, pl.ds(pl.multiple_of((i & 1) * S, S), S), :]

    add_pieces(queue, found, code_of, 4, S, piece, canvas)
    for tile in range(P_SIZE // LANES):
        out_ref[:, tile * LANES : (tile + 1) * LANES] = canvas[tile].astype(jnp.bfloat16)


def place_whole(slots):
    sources = slots.shape[0]
    return pl.pallas_call(
        whole_kernel,
        out_shape=jax.ShapeDtypeStruct((P_SIZE, P_SIZE), jnp.bfloat16),
        in_specs=[pl.BlockSpec(memory_space=pltpu.VMEM)],
        out_specs=pl.BlockSpec(memory_space=pltpu.VMEM),
        scratch_shapes=[
            pltpu.VMEM((P_SIZE // LANES + 2, P_SIZE, LANES), jnp.float32),
            pltpu.VMEM((8, S), jnp.int32),
            pltpu.SMEM((8, S), jnp.int32),
            pltpu.SMEM((2 * sources + 8,), jnp.int32),
            pltpu.SemaphoreType.DMA,
        ],
        compiler_params=pltpu.CompilerParams(vmem_limit_bytes=8 * 2**20),
        cost_estimate=pl.CostEstimate(flops=2**23, bytes_accessed=16 * 2**20, transcendentals=0),
        name="place_whole",
    )(slots)


def band_kernel(where_ref, parts_ref, out_ref, held, lines, canvas, told, codes, queue, sems):
    sources, rows = held.shape[0], held.shape[1]
    count, patches = rows // S, out_ref.shape[0]
    ask = pltpu.make_async_copy(parts_ref.at[:, pl.ds(rows, META)], lines, sems.at[2])
    ask.start()
    half = sources // 2
    fetches = []
    for part in range(2):
        taken = pl.ds(part * half, half)
        fetches.append(pltpu.make_async_copy(parts_ref.at[taken, pl.ds(0, rows)], held.at[taken], sems.at[part]))
        fetches[-1].start()
    band = where_ref[0] * BAND
    ask.wait()
    notes = lines[...].astype(jnp.float32).astype(jnp.int32)[:, 0:8, :]
    notes = notes.reshape(sources * 8, S)
    at = [notes] + [pltpu.roll(notes, S - i, 1) for i in range(1, 5)]
    ahead = band - (at[1] * LANES + at[2])
    start = jnp.clip((ahead >> 4) << 4, 0, S - WINDOW)
    row = at[0] * S + MARGIN + start - ahead
    code = (row << 13) + (at[3] << 10) + ((start >> 4) << 7) + at[4]
    code = jnp.where((ahead > -BAND) & (ahead < S), code, -1)
    first = (lax.broadcasted_iota(jnp.int32, (8, S), 1) & 7) == 0
    for group in range(sources // 8):
        words = jnp.zeros((8, S), jnp.int32)
        for i in range(8):
            source = 8 * group + i
            words += pltpu.roll(jnp.where(first, code[8 * source : 8 * source + 8, :], 0), i, 1)
        told[group] = words
    tell = pltpu.make_async_copy(told, codes.at[pl.ds(0, sources // 8)], sems.at[3])
    tell.start()
    for patch in range(patches):
        for tile in range(P_SIZE // LANES):
            canvas[tile, patch * S + MARGIN : patch * S + MARGIN + BAND, :] = jnp.zeros((BAND, LANES), jnp.float32)
    tell.wait()
    codes[sources // 8, 0, 0] = ((patches - 1) * S + MARGIN + BAND) << 13

    def code_of(i):
        return codes[i >> 8, (i >> 7) & 1, i & 127]

    def piece(i, start):
        begin = ((i & 127) >> 3) * S + start
        return held[lax.rem(i >> 8, sources // 8) * 8 + (i & 7), pl.ds(pl.multiple_of(begin, 16), WINDOW), :]

    for part in range(2):
        number = half * count * 2
        first = part * number
        found = listed(code_of, first, number, queue, 2 * number)
        fetches[part].wait()
        add_pieces(queue, found, code_of, 8, WINDOW, piece, canvas)
    for patch in range(patches):
        for tile in range(P_SIZE // LANES):
            rows = canvas[tile, patch * S + MARGIN : patch * S + MARGIN + BAND, :]
            out_ref[patch, :, tile * LANES : (tile + 1) * LANES] = rows.astype(jnp.bfloat16)


def place_band(where, parts, patches):
    sources, rows = parts.shape[0], parts.shape[1] - META
    return pl.pallas_call(
        band_kernel,
        out_shape=jax.ShapeDtypeStruct((patches, BAND, P_SIZE), jnp.bfloat16),
        in_specs=[pl.BlockSpec(memory_space=pltpu.SMEM), pl.BlockSpec(memory_space=pltpu.HBM)],
        out_specs=pl.BlockSpec(memory_space=pltpu.VMEM),
        scratch_shapes=[
            pltpu.VMEM((sources, rows, S), jnp.bfloat16),
            pltpu.VMEM((sources, META, S), jnp.bfloat16),
            pltpu.VMEM((P_SIZE // LANES + 1, patches * S, LANES), jnp.float32),
            pltpu.VMEM((sources // 8, 8, S), jnp.int32),
            pltpu.SMEM((sources // 8 + 1, 8, S), jnp.int32),
            pltpu.SMEM((2 * sources * (rows // S) + 8,), jnp.int32),
            pltpu.SemaphoreType.DMA((4,)),
        ],
        compiler_params=pltpu.CompilerParams(vmem_limit_bytes=60 * 2**20),
        cost_estimate=pl.CostEstimate(flops=2**24, bytes_accessed=24 * 2**20, transcendentals=0),
        name="place_band",
    )(where, parts)


def body(blocks, inv_variance, destinations, offsets, coefficients, basis_rows, basis_cols):
    along = lax.axis_size("x")
    owners = along * lax.axis_size("z")
    where = lax.axis_index(("y", "core")).astype(jnp.int32).reshape(1)
    weight = inv_variance[0]

    near = lax.all_gather(with_lines(weight, destinations[0], offsets[0]), ("y", "core"))
    den = place_band(where, near, owners).reshape(along, owners // along, BAND, P_SIZE)
    den = lax.psum_scatter(den, "x", scatter_dimension=0, tiled=True)[0]
    den = lax.all_to_all(den, "z", 0, 0, tiled=True)

    slots = match(blocks[0], weight, destinations[0], offsets[0], coefficients, basis_rows, basis_cols, owners)
    slots = lax.all_to_all(slots, ("x", "z"), 0, 0, tiled=True)
    num = place_whole(slots).reshape(16, BAND, P_SIZE)
    num = lax.all_to_all(num, ("y", "core"), 0, 0, tiled=True)

    num = jnp.sum(num.astype(jnp.float32), axis=0)
    den = jnp.sum(den.astype(jnp.float32), axis=0)
    return (num / jnp.maximum(den, 1.0))[None]


def solution(mesh):
    visits = mesh.shape["visit"]
    grid = Mesh(mesh.devices.reshape(visits // 2, 2, 4, mesh.shape["patch"] // 4), ("y", "core", "x", "z"))
    visit, patch = ("y", "core"), ("x", "z")
    return jax.shard_map(
        body,
        mesh=grid,
        in_specs=(
            P(visit, patch, None, None),
            P(visit, patch, None, None),
            P(visit, patch, None),
            P(visit, patch, None, None),
            P(visit, patch, None),
            P(),
            P(),
        ),
        out_specs=P(patch, visit, None),
        check_vma=False,
    )
```
